32 devices in a mesh: batch: 8 (over z, y), expert: 4 (over x, core).
Axes of the slice: x: 2, y: 2, z: 4, core: 2. Of those that a mesh axis runs over, the one named last changes fastest.
Arguments:
- tokens: bfloat16 [2, 16384, 512], P(None, ('batch', 'expert')), may hold values from -6 to 6
- routes: int32 [2, 16384, 3], P(None, ('batch', 'expert')), may hold values from 0 to 11, all different within a row; in each aligned block of 512 rows (0 to 511, 512 to 1023, ..., all dimensions but the last counted through in order) at most 256 rows name the same one
- lengths: int32 [2, 8, 8], P(None, 'batch'), may hold values from 1 to 1537, 2048 in all within a row
- gain_one: bfloat16 [512], replicated, may hold values from 0.5 to 1.5
- shift_one: bfloat16 [512], replicated, may hold values from -1 to 1
- router: bfloat16 [512, 12], replicated, may hold values from -0.1875 to 0.1875
- key_value: bfloat16 [512, 128], replicated, may hold values from -0.25 to 0.25
- w_query: bfloat16 [12, 512, 64], P('expert'), may hold values from -0.25 to 0.25
- w_out: bfloat16 [12, 64, 512], P('expert'), may hold values from -4 to 4
- gain_two: bfloat16 [512], replicated, may hold values from 0.5 to 1.5
- shift_two: bfloat16 [512], replicated, may hold values from -1 to 1
- w_up: bfloat16 [512, 2048], replicated, may hold values from -0.25 to 0.25
- up_bias: bfloat16 [2048], replicated, may hold values from -1 to 1
- w_down: bfloat16 [2048, 512], replicated, may hold values from -0.125 to 0.125
- down_bias: bfloat16 [512], replicated, may hold values from -1 to 1
- cotangent: bfloat16 [2, 16384, 512], P(None, ('batch', 'expert')), may hold values from -6 to 6
Outputs:
- block_out: bfloat16 [2, 16384, 512], P(None, ('batch', 'expert'))
- input_grad: float32 [2, 16384, 512], P(None, ('batch', 'expert'))
- grad_gain_one: float32 [512], replicated
- grad_shift_one: float32 [512], replicated
- grad_router: float32 [512, 12], replicated
- grad_key_value: float32 [512, 128], replicated
- grad_w_query: float32 [12, 512, 64], P('expert')
- grad_w_out: float32 [12, 64, 512], P('expert')
- grad_gain_two: float32 [512], replicated
- grad_shift_two: float32 [512], replicated
- grad_up: float32 [512, 2048], replicated
- grad_up_bias: float32 [2048], replicated
- grad_down: float32 [2048, 512], replicated
- grad_down_bias: float32 [512], replicated
The draws below stay inside these ranges and needn't reach their ends.
Inputs may be any that keep to these rules, and one draw needn't show every extreme that they name: `routes`: each token names 3 different experts. In each aligned block of 512 rows (the tokens of one device in one micro-batch) no expert is named by more than 256 rows, a bound that some block reaches. Each row gives the lengths of the sequences of one group in order; they sum to 2048, and the longest is exactly 1537.
All inputs are finite; a program needn't handle non-finite values.
Results may differ from the reference program's by a relative error of at most 0.011.
Values may be sent and summed in bfloat16 or wider, within the bound.
No kernel may reach another device: no remote copies, remote signals or barrier semaphores. Data moves between devices by JAX's collectives and lax.ppermute only.
A program may use at most 192 MiB of HBM per device.

```python
import math
import jax
import jax.numpy as jnp
import numpy as np
from jax import lax

D = 512
HEAD = 64
FF = 2048
TOP = 3
MICRO = 2
NSEG = 8
TOK_DEV = 512
EXPERTS = 12
CAP = 256
GROUP = 2048
TOKENS = 16384
LONGEST = 1537
N_BATCH = 8


def block_levels(stream_key, dims, split, least, largest):
    level, own = 1.0, jax.random.fold_in(stream_key, 6)
    for dim, parts in split:
        steps = jnp.exp(jax.random.uniform(jax.random.fold_in(own, dim), (parts,), jnp.float32, least / len(split), largest / len(split)))
        level = level * jnp.repeat(steps, dims[dim] // parts).reshape([-1 if axis == dim else 1 for axis in range(len(dims))])
    return level


def length_profile(number_of, total, bound, slope):
    loads = [(1 << 20) // math.isqrt(rank ** slope) + 1 for rank in range(2, number_of + 1)]
    rest, given = total - bound - (number_of - 1), [1] * (number_of - 1)
    while rest > 0:
        movable = [i for i in range(number_of - 1) if given[i] < bound]
        mass, left = sum([loads[i] for i in movable]), rest
        for i in movable:
            addition = min(bound - given[i], max(1, left * loads[i] // mass), rest)
            given[i] = given[i] + addition
            rest = rest - addition
    return np.array([bound] + given)


def uneven_parts(own_key, amount, total, limit, lean):
    if amount == 2:
        one = jax.random.randint(own_key, (), max(1, total - limit), min(limit, total - 1) + 1)
        return jnp.stack([one, total - one])
    sizes = jnp.asarray(length_profile(amount, total, limit, lean), jnp.int32)
    pairs = (amount - 1) // 2
    source_of, taker = sizes[1:1 + 2 * pairs:2], sizes[2:2 + 2 * pairs:2]
    slack = jnp.minimum(source_of - 1, limit - taker)
    passed = jax.random.randint(jax.random.fold_in(own_key, 1), (pairs,), 0, 1 << 20) % (slack + 1)
    sizes = sizes.at[1:1 + 2 * pairs:2].set(source_of - passed).at[2:2 + 2 * pairs:2].set(taker + passed)
    return sizes[jax.random.permutation(jax.random.fold_in(own_key, 2), amount)]


def assign_block(stream_key, own, number, rows, count, top, bound, lean):
    ranking = jax.random.permutation(stream_key, count)
    packed, usual = portions_of(count, rows * top, bound, lean, True), portions_of(count, rows * top, bound, lean, False)
    places = jnp.arange(count)

    def named(sizes, rotation):
        used = int((sizes > 0).sum())
        fixed = max(1, used // 4)
        moved = fixed + (places - fixed + rotation * (used - fixed)) % max(1, count - fixed)
        return jnp.zeros((count,), jnp.int32).at[ranking[jnp.where(places < fixed, places, moved)]].set(jnp.asarray(sizes, jnp.int32))

    sizes = jnp.where(number % 4 == 0, named(packed, number // 4), named(usual, number - number // 4 - 1))
    mixed = jax.random.permutation(jax.random.fold_in(own, 3), count)
    donor, receiver = mixed[0:count // 2 * 2:2], mixed[1:count // 2 * 2:2]
    room = jnp.minimum(sizes[donor] - 1, bound - sizes[receiver]) // 2
    room = jnp.where((donor == ranking[0]) | (receiver == ranking[0]) | (sizes[receiver] == 0), 0, jnp.maximum(room, 0))
    moved = jax.random.randint(jax.random.fold_in(own, 4), (count // 2,), 0, 1 << 20) % (room + 1)
    sizes = sizes.at[donor].add(-moved).at[receiver].add(moved)
    labels = jnp.searchsorted(jnp.cumsum(sizes), jnp.arange(rows * top), side="right").astype(jnp.int32)
    grid = labels.reshape(top, rows).T
    grid = grid[jax.random.permutation(jax.random.fold_in(own, 1), rows)]
    rotation = jax.random.randint(jax.random.fold_in(own, 2), (rows, 1), 0, top)
    return jnp.take_along_axis(grid, (jnp.arange(top)[None, :] + rotation) % top, axis=1)


def portions_of(amount, total, limit, skew, full):
    loads = [(1 << 20) // math.isqrt(rank ** skew) + 1 for rank in range(1, amount + 1)]
    largest = limit if full else min(limit, max(-(-total // amount), total * loads[0] // sum(loads)))
    least = 1 if total - largest >= amount - 1 else 0
    holding, rest = [largest] + [least] * (amount - 1), total - largest - least * (amount - 1)
    while rest > 0:
        candidates = [i for i in range(1, amount) if holding[i] < largest] or [i for i in range(1, amount) if holding[i] < limit]
        mass, left = sum([loads[i] for i in candidates]), rest
        for i in candidates:
            more = min(limit - holding[i], max(1, left * loads[i] // mass), rest)
            holding[i] = holding[i] + more
            rest = rest - more
    return np.array(holding)


def normal_values(key, extent, scale, bound, shards=(), kind=jnp.bfloat16):
    level = block_levels(key, extent, shards, -0.22, 0.18) if shards else 1.0
    values = jax.random.normal(key, extent, jnp.float32) * scale * level
    return jnp.minimum(jnp.maximum(values, -bound), bound).astype(kind)


def setup_inputs(seed: int = 0) -> dict:
    key_list = jax.random.split(jax.random.key(seed), 17)
    tokens = normal_values(key_list[0], (MICRO, TOKENS, D), 1.0, 6.0, ((1, 32),))
    routes_keys = jax.random.split(jax.random.fold_in(key_list[1], 1), MICRO * TOKENS // TOK_DEV)
    routes_turns = jax.random.permutation(jax.random.fold_in(key_list[1], 3), MICRO * TOKENS // TOK_DEV)
    routes = jax.vmap(lambda own, number: assign_block(jax.random.fold_in(key_list[1], 2), own, number, TOK_DEV, EXPERTS, TOP, CAP, 2))(routes_keys, routes_turns).reshape((MICRO, TOKENS, TOP))
    lengths = jax.vmap(lambda own: uneven_parts(own, NSEG, GROUP, LONGEST, 2))(jax.random.split(key_list[2], MICRO * N_BATCH)).reshape((MICRO, N_BATCH, NSEG)).astype(jnp.int32)
    gain_one = jnp.clip(1.0 + 0.1 * jax.random.normal(key_list[3], (D,), jnp.float32), 0.5, 1.5).astype(jnp.bfloat16)
    shift_one = normal_values(key_list[4], (D,), 0.2, 1.0)
    router = normal_values(key_list[5], (D, EXPERTS), (2 * D) ** -0.5, 0.1875)
    key_value = normal_values(key_list[6], (D, 2 * HEAD), D ** -0.5, 0.25)
    w_query = normal_values(key_list[7], (EXPERTS, D, HEAD), D ** -0.5, 0.25, ((0, 4),))
    w_out = normal_values(key_list[8], (EXPERTS, HEAD, D), 2 ** -0.5, 4.0, ((0, 4),))
    gain_two = jnp.clip(1.0 + 0.1 * jax.random.normal(key_list[9], (D,), jnp.float32), 0.5, 1.5).astype(jnp.bfloat16)
    shift_two = normal_values(key_list[10], (D,), 0.2, 1.0)
    w_up = normal_values(key_list[11], (D, FF), D ** -0.5, 0.25)
    up_bias = normal_values(key_list[12], (FF,), 0.2, 1.0)
    w_down = normal_values(key_list[13], (FF, D), FF ** -0.5, 0.125)
    down_bias = normal_values(key_list[14], (D,), 0.2, 1.0)
    cotangent = normal_values(key_list[15], (MICRO, TOKENS, D), 1.0, 6.0, ((1, 32),))
    return {"tokens": tokens, "routes": routes, "lengths": lengths, "gain_one": gain_one, "shift_one": shift_one, "router": router, "key_value": key_value, "w_query": w_query, "w_out": w_out, "gain_two": gain_two, "shift_two": shift_two, "w_up": w_up, "up_bias": up_bias, "w_down": w_down, "down_bias": down_bias, "cotangent": cotangent}


epsilon = 1e-05
highest = lax.Precision.HIGHEST

@jax.custom_vjp
def low(v):
    return lax.optimization_barrier(v.astype(jnp.bfloat16)).astype(jnp.float32)

@jax.custom_vjp
def low_back(v):
    return v

def low_keep(v):
    return (low(v), None)

def low_pass(kept, grad):
    return (grad,)

def back_keep(v):
    return (v, None)

def back_low(kept, grad):
    return (low(grad),)
low.defvjp(low_keep, low_pass)
low_back.defvjp(back_keep, back_low)

def layer_norm(values, gain_vector, shift_vector):
    centred = values - lax.optimization_barrier(jnp.mean(values, axis=-1, keepdims=True))
    spread = lax.optimization_barrier(jnp.mean(centred * centred, axis=-1, keepdims=True))
    return centred * lax.rsqrt(spread + epsilon) * gain_vector + shift_vector

def soft_gates(chosen):
    row_peak = lax.optimization_barrier(jnp.max(chosen, axis=-1, keepdims=True))
    powers = jnp.exp(chosen - row_peak)
    return powers / lax.optimization_barrier(jnp.sum(powers, axis=-1, keepdims=True))

def matmul(left_side, right_side):
    return jnp.dot(left_side, right_side, precision=highest)

def route_project(row_data, weights, experts):
    width_in = row_data.shape[-1]

    def one_block(block_pair):
        block_rows, block_ids = block_pair
        picked = jnp.take(weights, block_ids, axis=0)
        return jnp.einsum('tk,tkn->tn', block_rows, picked, precision=highest)
    shaped = row_data.reshape(-1, TOK_DEV, width_in)
    ids_shaped = experts.reshape(-1, TOK_DEV)
    result = lax.map(jax.checkpoint(one_block), (shaped, ids_shaped))
    return result.reshape(row_data.shape[0], weights.shape[-1])

def attend(queries, places, key_value_rows, segment):
    key_rows = key_value_rows[:, :HEAD]
    value_rows = key_value_rows[:, HEAD:]
    key_places = jnp.arange(GROUP, dtype=jnp.int32)

    def one_block(block_pair):
        block_rows, block_places = block_pair
        scores = low_back(matmul(block_rows, key_rows.T) * 0.125)
        query_seg = jnp.take(segment, block_places)
        allowed = (query_seg[:, None] == segment[None, :]) & (key_places[None, :] <= block_places[:, None])
        masked = jnp.where(allowed, scores, -1e+30)
        row_peak = lax.optimization_barrier(jnp.max(masked, axis=1, keepdims=True))
        powers = jnp.exp(masked - row_peak)
        weights_soft = powers / lax.optimization_barrier(jnp.sum(powers, axis=1, keepdims=True))
        return matmul(low(weights_soft), value_rows)
    shaped = queries.reshape(-1, TOK_DEV, HEAD)
    places_shaped = places.reshape(-1, TOK_DEV)
    return lax.map(jax.checkpoint(one_block), (shaped, places_shaped)).reshape(-1, HEAD)

def group_forward(params, group_tokens, group_routes, group_lengths):
    gain_one, shift_one, router, key_value, w_query, w_out, gain_two, shift_two, w_up, up_bias, w_down, down_bias = params
    normed = low(layer_norm(group_tokens, gain_one, shift_one))
    logits = matmul(normed, router)
    chosen = jnp.take_along_axis(logits, group_routes, axis=1)
    gate_weights = soft_gates(chosen)
    seq_ends = jnp.cumsum(group_lengths).astype(jnp.int32)
    token_places = jnp.arange(GROUP, dtype=jnp.int32)
    segment = lax.optimization_barrier(jnp.sum((token_places[:, None] >= seq_ends[None, :]).astype(jnp.int32), axis=1)).astype(jnp.int32)
    key_value_rows = low_back(low(matmul(normed, key_value)))
    query_list = []
    for route_index in range(TOP):
        projected = route_project(low_back(normed), w_query, group_routes[:, route_index])
        query_list.append(low_back(low(projected)))
    queries = jnp.concatenate(query_list, axis=0)
    places = jnp.concatenate([token_places] * TOP, axis=0)
    head_out = low_back(low(attend(queries, places, key_value_rows, segment)))
    mixed_sum = jnp.zeros_like(group_tokens)
    for route_index in range(TOP):
        route_part = head_out[route_index * GROUP:(route_index + 1) * GROUP]
        route_rows = low_back(low(route_project(route_part, w_out, group_routes[:, route_index])))
        mixed_sum = mixed_sum + gate_weights[:, route_index:route_index + 1] * route_rows
    hidden = group_tokens + mixed_sum
    normed_two = low(layer_norm(hidden, gain_two, shift_two))
    upward = low_back(matmul(normed_two, w_up) + up_bias)
    active = low(jax.nn.gelu(upward, approximate=True))
    return hidden + matmul(active, w_down) + down_bias

def reference(tokens, routes, lengths, gain_one, shift_one, router, key_value, w_query, w_out, gain_two, shift_two, w_up, up_bias, w_down, down_bias, cotangent):
    params = tuple((weight.astype(jnp.float32) for weight in (gain_one, shift_one, router, key_value, w_query, w_out, gain_two, shift_two, w_up, up_bias, w_down, down_bias)))
    group_count = MICRO * N_BATCH
    token_groups = tokens.astype(jnp.float32).reshape(group_count, GROUP, D)
    route_groups = routes.reshape(group_count, GROUP, TOP)
    length_groups = lengths.reshape(group_count, NSEG)
    cotan_groups = cotangent.astype(jnp.float32).reshape(group_count, GROUP, D)

    def step(totals, inputs):
        token_now, route_now, length_now, cotan_now = inputs

        def forward(param_set, token_set):
            return group_forward(param_set, token_set, route_now, length_now)
        result, pullback = jax.vjp(forward, params, token_now)
        grad_params, grad_tokens = pullback(cotan_now)
        totals = jax.tree.map(jnp.add, totals, grad_params)
        return (totals, (result.astype(jnp.bfloat16), grad_tokens))
    zero_grads = jax.tree.map(jnp.zeros_like, params)
    totals, outputs = lax.scan(step, zero_grads, (token_groups, route_groups, length_groups, cotan_groups))
    block_out = outputs[0].reshape(MICRO, TOKENS, D)
    input_grad = outputs[1].reshape(MICRO, TOKENS, D)
    grad_gain_one, grad_shift_one, grad_router, grad_key_value, grad_w_query, grad_w_out, grad_gain_two, grad_shift_two, grad_up, grad_up_bias, grad_down, grad_down_bias = totals
    return (block_out, input_grad, grad_gain_one, grad_shift_one, grad_router, grad_key_value, grad_w_query, grad_w_out, grad_gain_two, grad_shift_two, grad_up, grad_up_bias, grad_down, grad_down_bias)
```

```python
import functools

import jax
import jax.numpy as jnp
from jax import lax
from jax.experimental import pallas as pl
from jax.experimental.pallas import tpu as pltpu
from jax.sharding import PartitionSpec as P

epsilon = 1e-05
b16 = jnp.bfloat16
f32 = jnp.float32
LOW = -1e30
LIMIT = 56 * 1024 * 1024


def dot(left, right, over=((1,), (0,))):
    return lax.dot_general(left, right, (over, ((), ())), preferred_element_type=f32)


def log2(size):
    return size.bit_length() - 1


def flip(values, axis, bit):
    size = lax.axis_size(axis)
    return lax.ppermute(values, axis, [(i, i ^ (1 << bit)) for i in range(size)])


def add(left, right):
    return (left.astype(f32) + right.astype(f32)).astype(b16)


def normalize(values):
    centred = values - jnp.mean(values, axis=-1, keepdims=True)
    spread = lax.rsqrt(jnp.mean(centred * centred, axis=-1, keepdims=True) + epsilon)
    return centred * spread, spread


def norm_back(grad, unit, spread):
    inner = jnp.mean(grad * unit, axis=-1, keepdims=True)
    return spread * (grad - jnp.mean(grad, axis=-1, keepdims=True) - unit * inner)


def first_kernel(tokens, routes, gain, shift, router, key_value, normed, kv, gates):
    unit, _ = normalize(tokens[0].astype(f32))
    rows = (unit * gain[...].astype(f32) + shift[...].astype(f32)).astype(b16)
    normed[0] = rows
    kv[0] = dot(rows, key_value[...]).astype(b16)
    logits = dot(router[...], rows, ((1,), (1,)))
    ids = lax.broadcasted_iota(jnp.int32, logits.shape, 0)
    top = routes.shape[1]
    chosen = [
        jnp.sum(jnp.where(ids == routes[0, k : k + 1, :], logits, 0.0), axis=0, keepdims=True)
        for k in range(top)
    ]
    peak = functools.reduce(jnp.maximum, chosen)
    powers = [jnp.exp(c - peak) for c in chosen]
    total = sum(powers)
    for k in range(top):
        gates[0, k : k + 1, :] = powers[k] / total


def bounds(lens, micro, first, count):
    place = first + lax.broadcasted_iota(jnp.int32, (1, count), 1)
    run = jnp.int32(0)
    low = jnp.int32(0)
    start = jnp.zeros((1, count), jnp.int32)
    for j in range(lens.shape[1]):
        run = run + lens[micro, j]
        start = jnp.where(place >= run, run, start)
        low = jnp.where(first >= run, run, low)
    return place, start, low


def spread_rows(pieces, ids, expert):
    out = jnp.zeros_like(pieces[0])
    for piece, row in zip(pieces, ids):
        out = jnp.where(row == expert, piece, out)
    return out


def gather_rows(table, ids, experts, head):
    out = jnp.zeros((head, table.shape[1]), f32)
    for i, expert in enumerate(experts):
        out = jnp.where(ids == expert, table[i * head : (i + 1) * head], out)
    return out


def expert_ids(meta, groups, local):
    base = 4 + groups
    return [meta[base + s] * local + l for s in range(groups) for l in range(local)]


def transpose_kv(kv, kvt, groups, tok):
    for s in range(groups):
        kvt[:, s * tok : (s + 1) * tok] = kv[s, 0].T


def masked(scores, key_base, place, start):
    keys = key_base + lax.broadcasted_iota(jnp.int32, scores.shape, 0)
    return jnp.where((keys <= place) & (keys >= start), scores, LOW)


def forward_kernel(
    dims, meta, lens, normed, tokens, routes, gates, kv, wq, wo, gain, shift,
    hidden, second, qt, ot, lse, mixt, kvt, acc,
):
    groups, tok, head, tile, block, top, local = dims
    micro = pl.program_id(0)
    me = meta[0]
    experts = expert_ids(meta, groups, local)
    transpose_kv(kv, kvt, groups, tok)
    table = dot(wq[...], normed[0], ((1,), (1,)))
    for i in range(tok // tile):
        cols = slice(i * tile, (i + 1) * tile)
        ids = [routes[0, k : k + 1, cols] for k in range(top)]
        heads = [gather_rows(table[:, cols], row, experts, head) for row in ids]
        query = jnp.concatenate(heads, axis=1).astype(b16) * jnp.asarray(0.125, b16)
        qt[0, i] = query
        padded = jnp.concatenate([query, jnp.zeros_like(query)], axis=0)
        first = me * tok + i * tile
        place, start, low = bounds(lens, micro, first, tile)
        place = jnp.concatenate([place] * top, axis=1)
        start = jnp.concatenate([start] * top, axis=1)
        acc[...] = jnp.zeros_like(acc)

        def one_block(index, carry):
            peak, total = carry
            chunk = (index * block) // tok
            row = pl.multiple_of(index * block - chunk * tok, block)
            slot = meta[4 + chunk]
            column = pl.multiple_of(slot * tok + row, block)
            scores = dot(kv[slot, 0, pl.ds(row, block), :], padded)
            scores = masked(scores, index * block, place, start)
            new_peak = jnp.maximum(peak, jnp.max(scores, axis=0, keepdims=True))
            scale = jnp.exp(peak - new_peak)
            powers = jnp.exp(scores - new_peak)
            total = total * scale + jnp.sum(powers, axis=0, keepdims=True)
            acc[...] = acc[...] * scale + dot(
                kvt[head:, pl.ds(column, block)], powers.astype(b16)
            )
            return new_peak, total

        width = top * tile
        peak, total = lax.fori_loop(
            low // block,
            (first + tile - 1) // block + 1,
            one_block,
            (jnp.full((1, width), LOW, f32), jnp.zeros((1, width), f32)),
        )
        out = acc[...] / total
        ot[0, i] = out
        lse[0, i] = peak + jnp.log(total)
        rounded = out.astype(b16).astype(f32)
        pieces = [
            rounded[:, k * tile : (k + 1) * tile] * gates[0, k : k + 1, cols] for k in range(top)
        ]
        for e, expert in enumerate(experts):
            mixt[0, e * head : (e + 1) * head, cols] = spread_rows(pieces, ids, expert).astype(b16)
        mixed = dot(mixt[0, :, cols], wo[...], ((0,), (0,)))
        rows = tokens[0, cols, :].astype(f32) + mixed
        hidden[0, cols, :] = rows
        unit, _ = normalize(rows)
        second[0, cols, :] = (unit * gain[...].astype(f32) + shift[...].astype(f32)).astype(b16)


def backward_kernel(
    dims, meta, lens, normed, gh, routes, gates, kv, qt, ot, lse, mixt, wqr, wo,
    part, dkv, wbuf, router_rows, kvt, dkv_acc, dq, gq, wq_acc, wo_acc,
):
    groups, tok, head, tile, block, top, local = dims
    micro = pl.program_id(0)
    me = meta[0]
    experts = expert_ids(meta, groups, local)
    every = len(experts) * head
    pad = gq.shape[0] - every
    transpose_kv(kv, kvt, groups, tok)
    dkv_acc[...] = jnp.zeros_like(dkv_acc)

    @pl.when(micro == 0)
    def _():
        wq_acc[...] = jnp.zeros_like(wq_acc)
        wo_acc[...] = jnp.zeros_like(wo_acc)

    grad_rows = gh[0].astype(b16)
    table = dot(wo[...], grad_rows, ((1,), (1,)))
    wo_acc[...] += dot(mixt[0], grad_rows)
    for i in range(tok // tile):
        cols = slice(i * tile, (i + 1) * tile)
        ids = [routes[0, k : k + 1, cols] for k in range(top)]
        back = [gather_rows(table[:, cols], row, experts, head) for row in ids]
        weights = [gates[0, k : k + 1, cols] for k in range(top)]
        out = ot[0, i]
        outs = [out[:, k * tile : (k + 1) * tile] for k in range(top)]
        grad_gates = [
            jnp.sum(b * o.astype(b16).astype(f32), axis=0, keepdims=True)
            for b, o in zip(back, outs)
        ]
        inner = sum(w * g for w, g in zip(weights, grad_gates))
        chosen = [w * (g - inner) for w, g in zip(weights, grad_gates)]
        names = lax.broadcasted_iota(jnp.int32, (pad, tile), 0)
        gq[every:, cols] = spread_rows(
            [jnp.broadcast_to(c, (pad, tile)) for c in chosen], ids, names
        ).astype(b16)
        grad = jnp.concatenate([w * b for w, b in zip(weights, back)], axis=1).astype(b16)
        delta = jnp.sum(grad.astype(f32) * out, axis=0, keepdims=True)
        query = qt[0, i]
        padded = jnp.concatenate([query, jnp.zeros_like(query)], axis=0)
        grad_pad = jnp.concatenate([jnp.zeros_like(grad), grad], axis=0)
        level = lse[0, i]
        first = me * tok + i * tile
        place, start, low = bounds(lens, micro, first, tile)
        place = jnp.concatenate([place] * top, axis=1)
        start = jnp.concatenate([start] * top, axis=1)
        dq[...] = jnp.zeros_like(dq)

        def one_block(index, carry):
            chunk = (index * block) // tok
            row = pl.multiple_of(index * block - chunk * tok, block)
            slot = meta[4 + chunk]
            column = pl.multiple_of(slot * tok + row, block)
            keys = kv[slot, 0, pl.ds(row, block), :]
            scores = masked(dot(keys, padded), index * block, place, start)
            soft = jnp.exp(scores - level)
            grad_scores = (soft * (dot(keys, grad_pad) - delta)).astype(b16)
            dkv_acc[pl.ds(column, block), :] += dot(grad_scores, padded, ((1,), (1,))) + dot(
                soft.astype(b16), grad_pad, ((1,), (1,))
            )
            dq[...] += dot(kvt[:head, pl.ds(column, block)], grad_scores)
            return carry

        lax.fori_loop(low // block, (first + tile - 1) // block + 1, one_block, 0)
        grad_query = dq[...] * 0.125
        pieces = [grad_query[:, k * tile : (k + 1) * tile] for k in range(top)]
        for e, expert in enumerate(experts):
            gq[e * head : (e + 1) * head, cols] = spread_rows(pieces, ids, expert).astype(b16)
    part[0] = dot(gq[...], wqr[...], ((0,), (0,)))
    wq_acc[...] += dot(gq[...], normed[0])
    for s in range(groups):
        dkv[s, 0] = dkv_acc[s * tok : (s + 1) * tok, :].astype(b16)

    @pl.when(micro == pl.num_programs(0) - 1)
    def _():
        size = local * head
        for s in range(groups):
            wbuf[s, :size] = wq_acc[s * size : (s + 1) * size, :].astype(b16)
            wbuf[s, size:] = wo_acc[s * size : (s + 1) * size, :].astype(b16)
        router_rows[...] = wq_acc[every:, :]


def ffn_kernel(
    dims, meta, hidden, second, cotan, w_up, up_bias, w_down, down_bias, gain,
    block_out, gh, own_a, own_b, snd_a, snd_b, up_row, rows,
    acc, grad_acc, act_s, gu_s,
):
    chunk, sub = dims
    step = pl.program_id(0)
    total, width = hidden.shape
    tile = w_up.shape[1]
    half = width // 2

    @pl.when(step == 0)
    def _():
        acc[...] = jnp.zeros_like(acc)
        grad_acc[...] = jnp.zeros_like(grad_acc)

    bias = up_bias[...].astype(f32)
    up_sum = jnp.zeros((1, tile), f32)
    c0 = 0.7978845608028654
    c1 = c0 * 0.044715
    for i in range(total // sub):
        at = slice(i * sub, (i + 1) * sub)
        upward = dot(second[at, :], w_up[...]) + bias
        grad = dot(cotan[at, :], w_down[...], ((1,), (1,)))
        square = upward * upward
        curve = jnp.tanh(upward * (c0 + c1 * square))
        lift = 0.5 + 0.5 * curve
        value = upward * lift
        slope = lift + value * (1.0 - curve) * (c0 + (3.0 * c1) * square)
        active = value.astype(b16)
        grad_up = (grad * slope).astype(b16)
        act_s[at, :] = active
        gu_s[at, :] = grad_up
        up_sum = up_sum + jnp.sum(grad_up.astype(f32), axis=0, keepdims=True)
        acc[at, :] += dot(active, w_down[...])
        grad_acc[at, :] += dot(grad_up, w_up[...], ((1,), (1,)))
    up_row[...] = up_sum
    grad_down = dot(act_s[...], cotan[...], ((0,), (0,))).astype(b16)
    grad_up_t = dot(gu_s[...], second[...], ((0,), (0,))).astype(b16)
    per = tile // chunk

    def place(values, left, right):
        for target, low, lanes in ((left, meta[2], slice(0, half)), (right, meta[3], slice(half, width))):
            for i in range(per):
                at = pl.multiple_of((i ^ (low & (per - 1))) * chunk, chunk)
                target[pl.ds(at, chunk), :] = values[i * chunk : (i + 1) * chunk, lanes]

    @pl.when(meta[1] == 0)
    def _():
        place(grad_down, own_a, own_b)
        place(grad_up_t, snd_a, snd_b)

    @pl.when(meta[1] != 0)
    def _():
        place(grad_up_t, own_a, own_b)
        place(grad_down, snd_a, snd_b)

    @pl.when(step == pl.num_programs(0) - 1)
    def _():
        gain_row = gain[...].astype(f32)
        sums = [jnp.zeros((1, width), f32) for _ in range(3)]
        for i in range(total // sub):
            at = slice(i * sub, (i + 1) * sub)
            rows_now = hidden[at, :]
            cot = cotan[at, :].astype(f32)
            block_out[at, :] = (rows_now + acc[at, :] + down_bias[...].astype(f32)).astype(b16)
            unit, spread = normalize(rows_now)
            grad = grad_acc[at, :]
            gh[at, :] = cot + norm_back(grad * gain_row, unit, spread)
            for j, piece in enumerate((cot, grad * unit, grad)):
                sums[j] = sums[j] + jnp.sum(piece, axis=0, keepdims=True)
        rows[...] = jnp.zeros_like(rows)
        for j in range(3):
            rows[j : j + 1, :] = sums[j]


def last_kernel(
    tokens, normed, part, kv_own, kv_got, gh, gain, key_value, up_row, rows, router_rows,
    input_grad, bundle, acc, sums,
):
    micro = pl.program_id(0)
    width = tokens.shape[2]

    @pl.when(micro == 0)
    def _():
        acc[...] = jnp.zeros_like(acc)
        sums[...] = jnp.zeros_like(sums)

    grad_kv = (kv_own[0, 0].astype(f32) + kv_got[0, 0].astype(f32)).astype(b16)
    acc[...] += dot(grad_kv, normed[0], ((0,), (0,)))
    grad = part[0] + dot(grad_kv, key_value[...], ((1,), (1,)))
    unit, spread = normalize(tokens[0].astype(f32))
    input_grad[0] = gh[0] + norm_back(grad * gain[...].astype(f32), unit, spread)
    sums[0:1, :] += jnp.sum(grad * unit, axis=0, keepdims=True)
    sums[1:2, :] += jnp.sum(grad, axis=0, keepdims=True)

    @pl.when(micro == pl.num_programs(0) - 1)
    def _():
        at = acc.shape[0]
        pad = router_rows.shape[0]
        bundle[:at, :] = acc[...].astype(b16)
        bundle[at : at + pad, :] = router_rows[...].astype(b16)
        count = up_row.shape[1] // width
        pieces = [up_row[:, i * width : (i + 1) * width] for i in range(count)]
        pieces += [rows[0:3, :], sums[0:2, :]]
        left = bundle.shape[0] - at - pad - count - 5
        pieces.append(jnp.zeros((left, width), f32))
        bundle[at + pad :, :] = jnp.concatenate(pieces, axis=0).astype(b16)


def order_kernel(chunk, meta, own_a, own_b, got_a, got_b, down, up):
    tile, half = own_a.shape
    per = tile // chunk

    def sorted_rows(left, right):
        parts = []
        for ref, low in ((left, meta[2]), (right, meta[3])):
            blocks = []
            for i in range(per):
                at = pl.multiple_of((i ^ (low & (per - 1))) * chunk, chunk)
                blocks.append(ref[pl.ds(at, chunk), :])
            parts.append(blocks[0] if per == 1 else jnp.concatenate(blocks, axis=0))
        return jnp.concatenate(parts, axis=1).astype(f32)

    own = sorted_rows(own_a, own_b)
    got = sorted_rows(got_a, got_b)

    @pl.when(meta[1] == 0)
    def _():
        down[...] = own
        up[...] = got.T

    @pl.when(meta[1] != 0)
    def _():
        down[...] = got
        up[...] = own.T


def shards(
    tokens, routes, lengths, gain_one, shift_one, router, key_value, w_query, w_out,
    gain_two, shift_two, w_up, up_bias, w_down, down_bias, cotangent,
):
    groups = lax.axis_size("expert")
    batch = lax.axis_size("batch")
    me = lax.axis_index("expert")
    mine = lax.axis_index("batch")
    micros, tok, width = tokens.shape
    top = routes.shape[2]
    local, _, head = w_query.shape
    experts = local * groups
    every = experts * head
    hidden_units = w_up.shape[1]
    group_bits, batch_bits = log2(groups), log2(batch)
    chips = groups * batch // 2
    chip_bits = log2(chips)
    chunk = hidden_units // chips
    tile, block = min(256, tok), min(256, tok)
    tiles = tok // tile
    span = top * tile
    pad = -(-experts // 16) * 16
    both = 2 * head

    x_bits = [("expert", bit) for bit in range(1, group_bits)]
    b_bits = [("batch", bit) for bit in range(batch_bits)]
    order_a = x_bits + b_bits
    order_b = b_bits[:1] + x_bits + b_bits[1:]
    shared = len(b_bits) - 1

    def place_of(order):
        total = jnp.int32(0)
        for i, (axis, bit) in enumerate(order):
            index = me if axis == "expert" else mine
            total = total | (((index >> bit) & 1) << (len(order) - 1 - i))
        return total

    high = group_bits - 1
    offsets = jnp.arange(groups, dtype=jnp.int32)
    away = offsets ^ me
    slots = (away >> 1) | ((away & 1) << high)
    devices = (((offsets << 1) & (groups - 1)) | (offsets >> high)) ^ me
    meta = jnp.concatenate(
        [jnp.stack([me, me & 1, place_of(order_a), place_of(order_b)]).astype(jnp.int32), slots, devices]
    )
    lens = lengths.reshape(micros, lengths.shape[2])

    def row(vector):
        return vector.reshape(1, -1)

    def gather(values):
        for axis, bit in x_bits + [("expert", 0)]:
            values = jnp.concatenate([values, flip(values, axis, bit)], axis=0)
        return values

    own_weights = jnp.concatenate(
        [w_query.transpose(0, 2, 1).reshape(local * head, width), w_out.reshape(local * head, width)]
    )
    all_weights = gather(own_weights[None])
    size = local * head
    wq = all_weights[:, :size].reshape(every, width)
    wo = all_weights[:, size:].reshape(every, width)
    router_t = jnp.zeros((pad, width), b16).at[:experts].set(router.T)
    routes_t = routes.transpose(0, 2, 1)

    def full(shape):
        return pl.BlockSpec(shape, lambda *a: (0,) * len(shape))

    def micro_block(*shape):
        return pl.BlockSpec((1, *shape), lambda m, *a: (m,) + (0,) * len(shape))

    def params():
        return pltpu.CompilerParams(vmem_limit_bytes=LIMIT)

    normed, kv, gates = pl.pallas_call(
        first_kernel,
        grid=(micros,),
        in_specs=[
            micro_block(tok, width), micro_block(top, tok), full((1, width)), full((1, width)),
            full((pad, width)), full((width, both)),
        ],
        out_specs=[micro_block(tok, width), micro_block(tok, both), micro_block(8, tok)],
        out_shape=[
            jax.ShapeDtypeStruct((micros, tok, width), b16),
            jax.ShapeDtypeStruct((micros, tok, both), b16),
            jax.ShapeDtypeStruct((micros, 8, tok), f32),
        ],
        compiler_params=params(),
    )(tokens, routes_t, row(gain_one), row(shift_one), router_t, key_value)

    kv_all = gather(kv[None])
    dims = (groups, tok, head, tile, block, top, local)
    kv_spec = pl.BlockSpec((groups, 1, tok, both), lambda m, *a: (0, m, 0, 0))
    state_specs = [
        micro_block(tiles, head, span), micro_block(tiles, head, span), micro_block(tiles, 1, span),
        micro_block(every, tok),
    ]
    hidden, second, qt, ot, lse, mixt = pl.pallas_call(
        functools.partial(forward_kernel, dims),
        grid_spec=pltpu.PrefetchScalarGridSpec(
            num_scalar_prefetch=2,
            grid=(micros,),
            in_specs=[
                micro_block(tok, width), micro_block(tok, width), micro_block(top, tok),
                micro_block(8, tok), kv_spec, full((every, width)), full((every, width)),
                full((1, width)), full((1, width)),
            ],
            out_specs=[micro_block(tok, width), micro_block(tok, width)] + state_specs,
            scratch_shapes=[
                pltpu.VMEM((both, groups * tok), b16),
                pltpu.VMEM((head, span), f32),
            ],
        ),
        out_shape=[
            jax.ShapeDtypeStruct((micros, tok, width), f32),
            jax.ShapeDtypeStruct((micros, tok, width), b16),
            jax.ShapeDtypeStruct((micros, tiles, head, span), b16),
            jax.ShapeDtypeStruct((micros, tiles, head, span), f32),
            jax.ShapeDtypeStruct((micros, tiles, 1, span), f32),
            jax.ShapeDtypeStruct((micros, every, tok), b16),
        ],
        compiler_params=params(),
    )(meta, lens, normed, tokens, routes_t, gates, kv_all, wq, wo, row(gain_two), row(shift_two))

    total = micros * tok
    f_tile = 256
    low_bits = log2(f_tile // chunk)
    grad_a = pl.BlockSpec((f_tile, width // 2), lambda j, meta: (j ^ (meta[2] >> low_bits), 0))
    grad_b = pl.BlockSpec((f_tile, width // 2), lambda j, meta: (j ^ (meta[3] >> low_bits), 0))
    grad_shape = jax.ShapeDtypeStruct((hidden_units, width // 2), b16)
    block_out, gh, own_a, own_b, snd_a, snd_b, up_row, ffn_rows = pl.pallas_call(
        functools.partial(ffn_kernel, (chunk, 256)),
        grid_spec=pltpu.PrefetchScalarGridSpec(
            num_scalar_prefetch=1,
            grid=(hidden_units // f_tile,),
            in_specs=[
                full((total, width)), full((total, width)), full((total, width)),
                pl.BlockSpec((width, f_tile), lambda j, meta: (0, j)),
                pl.BlockSpec((1, f_tile), lambda j, meta: (0, j)),
                pl.BlockSpec((f_tile, width), lambda j, meta: (j, 0)),
                full((1, width)), full((1, width)),
            ],
            out_specs=[
                full((total, width)), full((total, width)), grad_a, grad_b, grad_a, grad_b,
                pl.BlockSpec((1, f_tile), lambda j, meta: (0, j)), full((8, width)),
            ],
            scratch_shapes=[
                pltpu.VMEM((total, width), f32),
                pltpu.VMEM((total, width), f32),
                pltpu.VMEM((total, f_tile), b16),
                pltpu.VMEM((total, f_tile), b16),
            ],
        ),
        out_shape=[
            jax.ShapeDtypeStruct((total, width), b16),
            jax.ShapeDtypeStruct((total, width), f32),
            grad_shape, grad_shape, grad_shape, grad_shape,
            jax.ShapeDtypeStruct((1, hidden_units), f32),
            jax.ShapeDtypeStruct((8, width), f32),
        ],
        compiler_params=params(),
    )(
        meta, hidden.reshape(total, width), second.reshape(total, width),
        cotangent.reshape(total, width), w_up, row(up_bias), w_down, row(down_bias), row(gain_two),
    )
    gh = gh.reshape(micros, tok, width)

    keep_a, keep_b = own_a, own_b
    got_a, got_b = flip(snd_a, "expert", 0), flip(snd_b, "expert", 0)
    ways_a, ways_b = order_a[: len(order_a) - shared], order_b[: len(order_b) - shared]

    def halve(keep, got, way):
        count = keep.shape[0] // 2
        sent = add(keep[count:], got[count:])
        return add(keep[:count], got[:count]), flip(sent, *way)

    for way_a, way_b in zip(ways_a, ways_b):
        keep_a, got_a = halve(keep_a, got_a, way_a)
        keep_b, got_b = halve(keep_b, got_b, way_b)
    keep = jnp.concatenate([keep_a, keep_b], axis=1)
    got = jnp.concatenate([got_a, got_b], axis=1)
    for way in order_a[len(order_a) - shared :]:
        keep, got = halve(keep, got, way)
    whole = add(keep, got)
    for way in order_a[len(order_a) - shared :][::-1]:
        whole = jnp.concatenate([whole, flip(whole, *way)], axis=0)
    whole_a, whole_b = whole[:, : width // 2], whole[:, width // 2 :]
    for way_a, way_b in list(zip(ways_a, ways_b))[::-1]:
        whole_a = jnp.concatenate([whole_a, flip(whole_a, *way_a)], axis=0)
        whole_b = jnp.concatenate([whole_b, flip(whole_b, *way_b)], axis=0)
    other_a, other_b = flip(whole_a, "expert", 0), flip(whole_b, "expert", 0)

    wqr = jnp.concatenate([wq, router_t], axis=0)
    part, dkv, wbuf, router_rows = pl.pallas_call(
        functools.partial(backward_kernel, dims),
        grid_spec=pltpu.PrefetchScalarGridSpec(
            num_scalar_prefetch=2,
            grid=(micros,),
            in_specs=[
                micro_block(tok, width), micro_block(tok, width), micro_block(top, tok),
                micro_block(8, tok), kv_spec,
            ] + state_specs + [full((every + pad, width)), full((every, width))],
            out_specs=[
                micro_block(tok, width), kv_spec, full((groups, 2 * size, width)), full((pad, width)),
            ],
            scratch_shapes=[
                pltpu.VMEM((both, groups * tok), b16),
                pltpu.VMEM((groups * tok, both), f32),
                pltpu.VMEM((head, span), f32),
                pltpu.VMEM((every + pad, tok), b16),
                pltpu.VMEM((every + pad, width), f32),
                pltpu.VMEM((every, width), f32),
            ],
        ),
        out_shape=[
            jax.ShapeDtypeStruct((micros, tok, width), f32),
            jax.ShapeDtypeStruct((groups, micros, tok, both), b16),
            jax.ShapeDtypeStruct((groups, 2 * size, width), b16),
            jax.ShapeDtypeStruct((pad, width), f32),
        ],
        compiler_params=params(),
    )(meta, lens, normed, gh, routes_t, gates, kv_all, qt, ot, lse, mixt, wqr, wo)

    def scatter(values):
        count = groups // 2
        keep, sent = values[:count], values[count:]
        for i, way in enumerate([("expert", 0)] + x_bits[::-1]):
            got = flip(sent, *way)
            if count > 1:
                sent = add(keep[count // 2 :], got[count // 2 :])
                keep, got = keep[: count // 2], got[: count // 2]
                if i < len(x_bits):
                    keep = add(keep, got)
            count //= 2
        return keep, got

    kv_own, kv_got = scatter(dkv)
    rows_all = both + pad + 16
    input_grad, bundle = pl.pallas_call(
        last_kernel,
        grid=(micros,),
        in_specs=[
            micro_block(tok, width), micro_block(tok, width), micro_block(tok, width),
            pl.BlockSpec((1, 1, tok, both), lambda m: (0, m, 0, 0)),
            pl.BlockSpec((1, 1, tok, both), lambda m: (0, m, 0, 0)),
            micro_block(tok, width), full((1, width)), full((width, both)),
            full((1, hidden_units)), full((8, width)), full((pad, width)),
        ],
        out_specs=[micro_block(tok, width), full((rows_all, width))],
        out_shape=[
            jax.ShapeDtypeStruct((micros, tok, width), f32),
            jax.ShapeDtypeStruct((rows_all, width), b16),
        ],
        scratch_shapes=[pltpu.VMEM((both, width), f32), pltpu.VMEM((8, width), f32)],
        compiler_params=params(),
    )(tokens, normed, part, kv_own, kv_got, gh, row(gain_one), key_value, up_row, ffn_rows, router_rows)

    w_own, w_got = scatter(wbuf)
    w_sum = add(w_own, w_got)[0]
    for way in [("expert", 0)] + x_bits:
        bundle = add(bundle, flip(bundle, *way))
    tail = jnp.concatenate([w_sum, bundle], axis=0)
    for way in b_bits:
        tail = add(tail, flip(tail, *way))

    grad_down, grad_up = pl.pallas_call(
        functools.partial(order_kernel, chunk),
        grid_spec=pltpu.PrefetchScalarGridSpec(
            num_scalar_prefetch=1,
            grid=(hidden_units // f_tile,),
            in_specs=[grad_a, grad_b, grad_a, grad_b],
            out_specs=[
                pl.BlockSpec((f_tile, width), lambda j, meta: (j, 0)),
                pl.BlockSpec((width, f_tile), lambda j, meta: (0, j)),
            ],
        ),
        out_shape=[
            jax.ShapeDtypeStruct((hidden_units, width), f32),
            jax.ShapeDtypeStruct((width, hidden_units), f32),
        ],
        compiler_params=params(),
    )(meta, whole_a, whole_b, other_a, other_b)

    tail = tail.astype(f32)
    grad_wq = tail[:size].reshape(local, head, width).transpose(0, 2, 1)
    grad_wo = tail[size : 2 * size].reshape(local, head, width)
    at = 2 * size
    grad_key_value = tail[at : at + both].T
    grad_router = tail[at + both : at + both + experts].T
    at = at + both + pad
    count = hidden_units // width
    grad_up_bias = tail[at : at + count].reshape(hidden_units)
    at = at + count
    return (
        block_out.reshape(micros, tok, width),
        input_grad,
        tail[at + 3],
        tail[at + 4],
        grad_router,
        grad_key_value,
        grad_wq,
        grad_wo,
        tail[at + 1],
        tail[at + 2],
        grad_up,
        grad_up_bias,
        grad_down,
        tail[at],
    )


def solution(mesh):
    split = P(None, ("batch", "expert"), None)
    own = P("expert", None, None)
    in_specs = (
        split, split, P(None, "batch", None), P(), P(), P(), P(), own, own, P(), P(), P(), P(), P(),
        P(), split,
    )
    out_specs = (split, split, P(), P(), P(), P(), own, own, P(), P(), P(), P(), P(), P())
    return jax.shard_map(shards, mesh=mesh, in_specs=in_specs, out_specs=out_specs, check_vma=False)
```

```python
import functools

import jax
import jax.numpy as jnp
from jax import lax
from jax.experimental import pallas as pl
from jax.experimental.pallas import tpu as pltpu
from jax.sharding import PartitionSpec as P

epsilon = 1e-05
b16 = jnp.bfloat16
f32 = jnp.float32
LOW = -1e30
MIB = 1024 * 1024


def dot(left, right, over=((1,), (0,))):
    return lax.dot_general(left, right, (over, ((), ())), preferred_element_type=f32)


def log2(size):
    return size.bit_length() - 1


def flip(values, axis, bit):
    size = lax.axis_size(axis)
    return lax.ppermute(values, axis, [(i, i ^ (1 << bit)) for i in range(size)])


def hop(values, ways, groups, batch):
    pairs = []
    for b in range(batch):
        for e in range(groups):
            axis, bit = ways[e & 1]
            to_b, to_e = (b, e ^ (1 << bit)) if axis == "expert" else (b ^ (1 << bit), e)
            pairs.append((b * groups + e, to_b * groups + to_e))
    return lax.ppermute(values, ("batch", "expert"), pairs)


def add(left, right):
    return (left.astype(f32) + right.astype(f32)).astype(b16)


def normalize(values):
    centred = values - jnp.mean(values, axis=-1, keepdims=True)
    spread = lax.rsqrt(jnp.mean(centred * centred, axis=-1, keepdims=True) + epsilon)
    return centred * spread, spread


def norm_back(grad, unit, spread):
    inner = jnp.mean(grad * unit, axis=-1, keepdims=True)
    return spread * (grad - jnp.mean(grad, axis=-1, keepdims=True) - unit * inner)


def first_kernel(micro, tokens, routes, vectors, router, key_value, normed, kv, gates):
    unit, _ = normalize(tokens[micro].astype(f32))
    rows = (unit * vectors[0:1, :] + vectors[1:2, :]).astype(b16)
    normed[...] = rows
    kv[...] = dot(rows, key_value[...]).astype(b16)
    logits = dot(router[...], rows, ((1,), (1,)))
    ids = lax.broadcasted_iota(jnp.int32, logits.shape, 0)
    top = routes.shape[1]
    chosen = [
        jnp.sum(jnp.where(ids == routes[micro, k : k + 1, :], logits, 0.0), axis=0, keepdims=True)
        for k in range(top)
    ]
    peak = functools.reduce(jnp.maximum, chosen)
    powers = [jnp.exp(c - peak) for c in chosen]
    total = sum(powers)
    for k in range(top):
        gates[k : k + 1, :] = powers[k] / total


def bounds(lens, micro, first, count):
    place = first + lax.broadcasted_iota(jnp.int32, (1, count), 1)
    run = jnp.int32(0)
    low = jnp.int32(0)
    high = jnp.int32(0)
    start = jnp.zeros((1, count), jnp.int32)
    for j in range(lens.shape[1]):
        run = run + lens[micro, j]
        start = jnp.where(place >= run, run, start)
        low = jnp.where(first >= run, run, low)
        high = jnp.where(first + count - 1 >= run, run, high)
    return place, start, low, high


def key_loops(body, carry, first, tile, low, high, block):
    begin = low // block
    full_end = first // block
    full_begin = jnp.minimum((high + block - 1) // block, full_end)
    end = (first + tile - 1) // block + 1
    carry = lax.fori_loop(begin, full_begin, functools.partial(body, True), carry)
    carry = lax.fori_loop(full_begin, full_end, functools.partial(body, False), carry)
    return lax.fori_loop(full_end, end, functools.partial(body, True), carry)


def spread_rows(pieces, ids, expert):
    out = jnp.zeros_like(pieces[0])
    for piece, row in zip(pieces, ids):
        out = jnp.where(row == expert, piece, out)
    return out


def gather_rows(table, ids, experts, head):
    out = jnp.zeros((head, table[0].shape[1]), f32)
    for piece, expert in zip(table, experts):
        out = jnp.where(ids == expert, piece, out)
    return out


def expert_ids(meta, groups, local):
    base = 4 + groups
    return [meta[base + s] * local + l for s in range(groups) for l in range(local)]


def head_table(weights, rows, local, head):
    out = []
    for piece in weights:
        whole = dot(piece[...], rows, ((1,), (1,)))
        out += [whole[l * head : (l + 1) * head] for l in range(local)]
    return out


def masked(scores, key_base, place, start):
    keys = key_base + lax.broadcasted_iota(jnp.int32, scores.shape, 0)
    return jnp.where((keys <= place) & (keys >= start), scores, LOW)


def forward_kernel(dims, micro, *refs):
    groups, tok, head, tile, block, top, local = dims
    meta, lens, normed, routes, gates = refs[:5]
    pieces_kv = refs[5 : 5 + groups]
    weights = refs[5 + groups : 5 + 2 * groups]
    kv, kvt, qt, ot, lse, mixt, acc = refs[5 + 2 * groups :]
    me = meta[0]
    experts = expert_ids(meta, groups, local)
    for s, piece in enumerate(pieces_kv):
        kv[s * tok : (s + 1) * tok, :] = piece[...]
        kvt[:, s * tok : (s + 1) * tok] = piece[...].T
    table = head_table(weights, normed[...], local, head)
    for i in range(tok // tile):
        cols = slice(i * tile, (i + 1) * tile)
        ids = [routes[micro, k : k + 1, cols] for k in range(top)]
        part = [t[:, cols] for t in table]
        heads = [gather_rows(part, row, experts, head) for row in ids]
        query = jnp.concatenate(heads, axis=1).astype(b16) * jnp.asarray(0.125, b16)
        qt[i] = query
        padded = jnp.concatenate([query, jnp.zeros_like(query)], axis=0)
        first = me * tok + i * tile
        place, start, low, high = bounds(lens, micro, first, tile)
        place = jnp.concatenate([place] * top, axis=1)
        start = jnp.concatenate([start] * top, axis=1)
        acc[...] = jnp.zeros_like(acc)

        def one_block(edge, index, carry):
            peak, total = carry
            chunk = (index * block) // tok
            row = index * block - chunk * tok
            at = pl.multiple_of(meta[4 + chunk] * tok + row, block)
            scores = dot(kv[pl.ds(at, block), :], padded)
            if edge:
                scores = masked(scores, index * block, place, start)
            new_peak = jnp.maximum(peak, jnp.max(scores, axis=0, keepdims=True))
            scale = jnp.exp(peak - new_peak)
            powers = jnp.exp(scores - new_peak)
            total = total * scale + jnp.sum(powers, axis=0, keepdims=True)
            acc[...] = acc[...] * scale + dot(kvt[head:, pl.ds(at, block)], powers.astype(b16))
            return new_peak, total

        width = top * tile
        none = (jnp.full((1, width), LOW, f32), jnp.zeros((1, width), f32))
        peak, total = key_loops(one_block, none, first, tile, low, high, block)
        out = acc[...] / total
        ot[i] = out
        lse[i] = peak + jnp.log(total)
        rounded = out.astype(b16).astype(f32)
        pieces = [
            rounded[:, k * tile : (k + 1) * tile] * gates[k : k + 1, cols] for k in range(top)
        ]
        for e, expert in enumerate(experts):
            mixt[e * head : (e + 1) * head, cols] = spread_rows(pieces, ids, expert).astype(b16)


def backward_kernel(dims, micro, *refs):
    groups, tok, head, tile, block, top, local = dims
    meta, lens, gh, routes, gates, kv, kvt, qt, ot, lse, router = refs[:11]
    wq = refs[11 : 11 + groups]
    wo = refs[11 + groups : 11 + 2 * groups]
    part, keep, sent, gq, dkv, dq = refs[11 + 2 * groups :]
    me = meta[0]
    experts = expert_ids(meta, groups, local)
    every = len(experts) * head
    pad = gq.shape[0] - every
    dkv[...] = jnp.zeros_like(dkv)
    table = head_table(wo, gh[micro * tok : (micro + 1) * tok, :].astype(b16), local, head)
    for i in range(tok // tile):
        cols = slice(i * tile, (i + 1) * tile)
        ids = [routes[micro, k : k + 1, cols] for k in range(top)]
        cut = [t[:, cols] for t in table]
        back = [gather_rows(cut, row, experts, head) for row in ids]
        weights = [gates[k : k + 1, cols] for k in range(top)]
        out = ot[i]
        outs = [out[:, k * tile : (k + 1) * tile] for k in range(top)]
        grad_gates = [
            jnp.sum(b * o.astype(b16).astype(f32), axis=0, keepdims=True)
            for b, o in zip(back, outs)
        ]
        inner = sum(w * g for w, g in zip(weights, grad_gates))
        chosen = [w * (g - inner) for w, g in zip(weights, grad_gates)]
        names = lax.broadcasted_iota(jnp.int32, (pad, tile), 0)
        gq[every:, cols] = spread_rows(
            [jnp.broadcast_to(c, (pad, tile)) for c in chosen], ids, names
        ).astype(b16)
        grad = jnp.concatenate([w * b for w, b in zip(weights, back)], axis=1).astype(b16)
        delta = jnp.sum(grad.astype(f32) * out, axis=0, keepdims=True)
        query = qt[i]
        padded = jnp.concatenate([query, jnp.zeros_like(query)], axis=0)
        grad_pad = jnp.concatenate([jnp.zeros_like(grad), grad], axis=0)
        level = lse[i]
        first = me * tok + i * tile
        place, start, low, high = bounds(lens, micro, first, tile)
        place = jnp.concatenate([place] * top, axis=1)
        start = jnp.concatenate([start] * top, axis=1)
        dq[...] = jnp.zeros_like(dq)

        def one_block(edge, index, carry):
            chunk = (index * block) // tok
            row = index * block - chunk * tok
            at = pl.multiple_of(meta[4 + chunk] * tok + row, block)
            keys = kv[pl.ds(at, block), :]
            scores = dot(keys, padded)
            if edge:
                scores = masked(scores, index * block, place, start)
            soft = jnp.exp(scores - level)
            grad_scores = (soft * (dot(keys, grad_pad) - delta)).astype(b16)
            dkv[pl.ds(at, block), :] += dot(grad_scores, padded, ((1,), (1,))) + dot(
                soft.astype(b16), grad_pad, ((1,), (1,))
            )
            dq[...] += dot(kvt[:head, pl.ds(at, block)], grad_scores)
            return carry

        key_loops(one_block, 0, first, tile, low, high, block)
        grad_query = dq[...] * 0.125
        pieces = [grad_query[:, k * tile : (k + 1) * tile] for k in range(top)]
        for e, expert in enumerate(experts):
            gq[e * head : (e + 1) * head, cols] = spread_rows(pieces, ids, expert).astype(b16)
    half = groups // 2
    for s in range(half):
        keep[s] = dkv[s * tok : (s + 1) * tok, :].astype(b16)
        sent[s] = dkv[(half + s) * tok : (half + s + 1) * tok, :].astype(b16)
    size = local * head
    total = dot(gq[every : every + router.shape[0], :], router[...], ((0,), (0,)))
    for s in range(groups):
        total = total + dot(gq[s * size : (s + 1) * size, :], wq[s][...], ((0,), (0,)))
    part[...] = total


def weights_kernel(dims, rows, *refs):
    groups, size, tok, micros = dims
    table, gh = refs[:2]
    gq = refs[2 : 2 + micros]
    normed = refs[2 + micros : 2 + 2 * micros]
    mixt = refs[2 + 2 * micros : 2 + 3 * micros]
    own, sent, router_rows = refs[2 + 3 * micros :]
    every = groups * size
    router_rows[...] = sum(dot(g[every:, :], n[...]) for g, n in zip(gq, normed))
    grads = [gh[m * tok : (m + 1) * tok, :].astype(b16) for m in range(micros)]
    for s in range(groups):
        at = slice(s * size, (s + 1) * size)
        wq = sum(dot(g[at, :], n[...]) for g, n in zip(gq, normed)).astype(b16)
        wo = sum(dot(m[at, :], g) for m, g in zip(mixt, grads)).astype(b16)
        target = own if s < groups // 2 else sent
        for k in range(2 * size // rows):
            to = pl.multiple_of(table[s, k] * rows, 16)
            source = wq if k * rows < size else wo
            begin = k * rows % size
            target[pl.ds(to, rows), :] = source[begin : begin + rows, :]


def ffn_kernel(dims, *refs):
    chunk, tile, sub, micros, groups = dims
    meta, tokens, cotan, vectors, w_up, up_bias, w_down = refs[:7]
    mixt = refs[7 : 7 + micros]
    wo = refs[7 + micros : 7 + micros + groups]
    block_out, gh, own, sent, up_row, rows = refs[7 + micros + groups : 13 + micros + groups]
    hidden, second, acc, grad_acc, act_s, gu_s = refs[13 + micros + groups :]
    total, width = hidden.shape
    tok = tokens.shape[1]
    size = wo[0].shape[0]
    for m in range(micros):
        at = slice(m * tok, (m + 1) * tok)
        mixed = dot(mixt[m][:size, :], wo[0][...], ((0,), (0,)))
        for s in range(1, groups):
            mixed = mixed + dot(mixt[m][s * size : (s + 1) * size, :], wo[s][...], ((0,), (0,)))
        values = tokens[m].astype(f32) + mixed
        hidden[at, :] = values
        unit, _ = normalize(values)
        second[at, :] = (unit * vectors[2:3, :] + vectors[3:4, :]).astype(b16)
    acc[...] = jnp.zeros_like(acc)
    grad_acc[...] = jnp.zeros_like(grad_acc)
    c0 = 0.7978845608028654
    c1 = c0 * 0.044715
    per = tile // chunk

    def one_tile(step, carry):
        base = pl.multiple_of(step * tile, tile)
        span = pl.ds(base, tile)
        bias = up_bias[:, span]
        up_sum = jnp.zeros((1, tile), f32)
        for i in range(total // sub):
            at = slice(i * sub, (i + 1) * sub)
            upward = dot(second[at, :], w_up[:, span]) + bias
            grad = dot(cotan[at, :], w_down[span, :], ((1,), (1,)))
            square = upward * upward
            curve = jnp.tanh(upward * (c0 + c1 * square))
            lift = 0.5 + 0.5 * curve
            value = upward * lift
            slope = lift + value * (1.0 - curve) * (c0 + (3.0 * c1) * square)
            active = value.astype(b16)
            grad_up = (grad * slope).astype(b16)
            act_s[at, :] = active
            gu_s[at, :] = grad_up
            up_sum = up_sum + jnp.sum(grad_up.astype(f32), axis=0, keepdims=True)
            acc[at, :] += dot(active, w_down[span, :])
            grad_acc[at, :] += dot(grad_up, w_up[:, span], ((1,), (1,)))
        up_row[:, span] = up_sum
        grad_down = dot(act_s[...], cotan[...], ((0,), (0,))).astype(b16)
        grad_up_t = dot(gu_s[...], second[...], ((0,), (0,))).astype(b16)

        def place(values, target, low):
            for i in range(per):
                at = pl.multiple_of(((step * per + i) ^ low) * chunk, chunk)
                target[pl.ds(at, chunk), :] = values[i * chunk : (i + 1) * chunk, :]

        @pl.when(meta[1] == 0)
        def _():
            place(grad_down, own, meta[2])
            place(grad_up_t, sent, meta[3])

        @pl.when(meta[1] != 0)
        def _():
            place(grad_up_t, own, meta[2])
            place(grad_down, sent, meta[3])

        return carry

    lax.fori_loop(0, w_up.shape[1] // tile, one_tile, 0)
    sums = [jnp.zeros((1, width), f32) for _ in range(3)]
    for i in range(total // sub):
        at = slice(i * sub, (i + 1) * sub)
        rows_now = hidden[at, :]
        cot = cotan[at, :].astype(f32)
        block_out[at, :] = (rows_now + acc[at, :] + vectors[4:5, :]).astype(b16)
        unit, spread = normalize(rows_now)
        grad = grad_acc[at, :]
        gh[at, :] = cot + norm_back(grad * vectors[2:3, :], unit, spread)
        for j, piece in enumerate((cot, grad * unit, grad)):
            sums[j] = sums[j] + jnp.sum(piece, axis=0, keepdims=True)
    rows[...] = jnp.zeros_like(rows)
    for j in range(3):
        rows[j : j + 1, :] = sums[j]


def last_kernel(micros, *refs):
    meta, tokens, gh, vectors, key_value, up_row, rows, router_rows = refs[:8]
    normed = refs[8 : 8 + micros]
    part = refs[8 + micros : 8 + 2 * micros]
    kept = refs[8 + 2 * micros : 8 + 3 * micros]
    got = refs[8 + 3 * micros : 8 + 4 * micros]
    input_grad, own, sent, bundle = refs[8 + 4 * micros :]
    _, tok, width = tokens.shape
    key_rows = 0.0
    gain_sum = jnp.zeros((1, width), f32)
    shift_sum = jnp.zeros((1, width), f32)
    for m in range(micros):
        at = slice(m * tok, (m + 1) * tok)
        grad_kv = (kept[m][0].astype(f32) + got[m][0].astype(f32)).astype(b16)
        key_rows = key_rows + dot(grad_kv, normed[m][...], ((0,), (0,)))
        grad = part[m][...] + dot(grad_kv, key_value[...], ((1,), (1,)))
        unit, spread = normalize(tokens[m].astype(f32))
        input_grad[m] = gh[at, :] + norm_back(grad * vectors[0:1, :], unit, spread)
        gain_sum = gain_sum + jnp.sum(grad * unit, axis=0, keepdims=True)
        shift_sum = shift_sum + jnp.sum(grad, axis=0, keepdims=True)
    at = key_rows.shape[0]
    pad = router_rows.shape[0]
    bundle[:at, :] = key_rows.astype(b16)
    bundle[at : at + pad, :] = router_rows[...].astype(b16)
    count = up_row.shape[1] // width
    pieces = [up_row[:, i * width : (i + 1) * width] for i in range(count)]
    pieces += [rows[0:3, :], gain_sum, shift_sum]
    left = bundle.shape[0] - at - pad - count - 5
    pieces.append(jnp.zeros((left, width), f32))
    bundle[at + pad :, :] = jnp.concatenate(pieces, axis=0).astype(b16)
    half = own.shape[0]
    own[...] = bundle[pl.ds(pl.multiple_of(meta[1] * half, 16), half), :]
    sent[...] = bundle[pl.ds(pl.multiple_of((1 - meta[1]) * half, 16), half), :]


def order_kernel(chunk, meta, own_low, own_high, got_low, got_high, down, up):
    tile = down.shape[0]
    per = tile // chunk
    step = pl.program_id(0)
    half = own_low.shape[0] // chunk

    def sorted_rows(low, high, place):
        blocks = []
        for i in range(per):
            slot = (step * per + i) ^ place
            at = pl.multiple_of((slot & (half - 1)) * chunk, chunk)
            rows = jnp.where(slot < half, low[pl.ds(at, chunk), :].astype(f32), high[pl.ds(at, chunk), :].astype(f32))
            blocks.append(rows)
        return blocks[0] if per == 1 else jnp.concatenate(blocks, axis=0)

    own = sorted_rows(own_low, own_high, meta[2])
    got = sorted_rows(got_low, got_high, meta[3])

    @pl.when(meta[1] == 0)
    def _():
        down[...] = own
        up[...] = got.T

    @pl.when(meta[1] != 0)
    def _():
        down[...] = got
        up[...] = own.T


def small_kernel(dims, meta, table, weights, own, got, wq, wo, keys, router, up_row, *outs):
    both, pad, rows = dims
    bundle = outs[-1]
    half, width = own.shape
    bundle[pl.ds(pl.multiple_of(meta[1] * half, 16), half), :] = own[...]
    bundle[pl.ds(pl.multiple_of((1 - meta[1]) * half, 16), half), :] = got[...]
    keys[...] = bundle[:both, :].astype(f32).T
    values = bundle[both:, :].astype(f32)
    router[...] = values[: router.shape[0], :]
    count = up_row.shape[0] // width
    for i in range(count):
        up_row[i * width : (i + 1) * width] = values[pad + i]
    for i, out in enumerate(outs[:-1]):
        out[...] = values[pad + count + i]
    size = wq.shape[0]
    for k in range(2 * size // rows):
        at = pl.multiple_of(table[k] * rows, 16)
        target = wq if k * rows < size else wo
        begin = k * rows % size
        target[begin : begin + rows, :] = weights[pl.ds(at, rows), :].astype(f32)


def shards(
    tokens, routes, lengths, gain_one, shift_one, router, key_value, w_query, w_out,
    gain_two, shift_two, w_up, up_bias, w_down, down_bias, cotangent,
):
    groups = lax.axis_size("expert")
    batch = lax.axis_size("batch")
    me = lax.axis_index("expert").astype(jnp.int32)
    mine = lax.axis_index("batch").astype(jnp.int32)
    micros, tok, width = tokens.shape
    top = routes.shape[2]
    local, _, head = w_query.shape
    experts = local * groups
    every = experts * head
    size = local * head
    hidden_units = w_up.shape[1]
    group_bits, batch_bits = log2(groups), log2(batch)
    chips = groups * batch // 2
    chunk = hidden_units // chips
    tile, block = min(256, tok), min(256, tok)
    tiles = tok // tile
    span = top * tile
    pad = -(-experts // 16) * 16
    both = 2 * head
    total = micros * tok
    core = me & 1

    x_bits = [("expert", bit) for bit in range(1, group_bits)]
    b_bits = [("batch", bit) for bit in range(batch_bits)]
    orders = (x_bits + b_bits, b_bits[:2] + x_bits + b_bits[2:])
    hops = list(zip(*orders))

    def place_of(order, expert, row):
        out = jnp.int32(0)
        for i, (axis, bit) in enumerate(order):
            index = expert if axis == "expert" else row
            out = out | (((index >> bit) & 1) << (len(order) - 1 - i))
        return out

    def by_core(first, second):
        return jnp.where(core == 0, first, second)

    high = group_bits - 1
    offsets = jnp.arange(groups, dtype=jnp.int32)
    away = offsets ^ me
    slots = (away >> 1) | ((away & 1) << high)
    devices = (((offsets << 1) & (groups - 1)) | (offsets >> high)) ^ me
    places = [place_of(order, me, mine) for order in orders]
    place_own, place_other = by_core(places[0], places[1]), by_core(places[1], places[0])
    meta = jnp.concatenate([jnp.stack([me, core, place_own, place_other]), slots, devices])
    rows_w = -(-2 * size // (16 * batch)) * 16
    subs = jnp.arange(2 * size // rows_w, dtype=jnp.int32)
    tables = [place_of(order, devices[:, None], subs[None, :]) for order in orders]
    table = jnp.where(
        (offsets < groups // 2)[:, None],
        by_core(tables[0], tables[1]) ^ place_own,
        by_core(tables[1], tables[0]) ^ place_other,
    )
    final_table = place_of(b_bits, me, subs) ^ place_of(b_bits, me, mine)
    lens = lengths.reshape(micros, lengths.shape[2])

    def gather(values):
        pieces = [values]
        for axis, bit in x_bits + [("expert", 0)]:
            pieces = pieces + [flip(p, axis, bit) for p in pieces]
        return pieces

    vmem = pl.BlockSpec(memory_space=pltpu.VMEM)
    smem = pl.BlockSpec(memory_space=pltpu.SMEM)

    def call(kernel, scalars, arrays, outs, scratch=(), limit=16, flops=0, exps=0):
        return pl.pallas_call(
            kernel,
            in_specs=[smem] * len(scalars) + [vmem] * len(arrays),
            out_specs=[vmem] * len(outs),
            out_shape=[jax.ShapeDtypeStruct(*o) for o in outs],
            scratch_shapes=[pltpu.VMEM(*s) for s in scratch],
            compiler_params=pltpu.CompilerParams(vmem_limit_bytes=limit * MIB),
            cost_estimate=pl.CostEstimate(flops=flops, bytes_accessed=0, transcendentals=exps),
        )(*scalars, *arrays)

    wq = gather(w_query.transpose(0, 2, 1).reshape(size, width))
    vectors = jnp.stack([gain_one, shift_one, gain_two, shift_two, down_bias]).astype(f32)
    router_t = router.T
    routes_t = routes.transpose(0, 2, 1)

    normed, kv_pieces, gates = [], [], []
    for m in range(micros):
        n, kv, g = call(
            functools.partial(first_kernel, m),
            [],
            [tokens, routes_t, vectors, router_t, key_value],
            [((tok, width), b16), ((tok, both), b16), ((8, tok), f32)],
            flops=2 * tok * width * both,
        )
        normed.append(n)
        gates.append(g)
        kv_pieces.append(gather(kv))
    wo = gather(w_out.reshape(size, width))

    dims = (groups, tok, head, tile, block, top, local)
    keys, keys_t, qt, ot, lse, mixt = [], [], [], [], [], []
    keys_all = groups * tok
    work = 2 * tok * top * keys_all * both
    for m in range(micros):
        results = call(
            functools.partial(forward_kernel, dims, m),
            [meta, lens],
            [normed[m], routes_t, gates[m]] + kv_pieces[m] + wq,
            [
                ((keys_all, both), b16), ((both, keys_all), b16), ((tiles, head, span), b16),
                ((tiles, head, span), f32), ((tiles, 1, span), f32), ((every, tok), b16),
            ],
            [((head, span), f32)],
            flops=2 * work,
            exps=tok * top * keys_all,
        )
        for target, value in zip((keys, keys_t, qt, ot, lse, mixt), results):
            target.append(value)

    f_tile = 512
    block_out, gh, own, sent, up_row, ffn_rows = call(
        functools.partial(ffn_kernel, (chunk, f_tile, min(512, tok), micros, groups)),
        [meta],
        [tokens, cotangent.reshape(total, width), vectors, w_up, up_bias.reshape(1, -1).astype(f32), w_down]
        + mixt + wo,
        [
            ((total, width), b16), ((total, width), f32), ((hidden_units, width), b16),
            ((hidden_units, width), b16), ((1, hidden_units), f32), ((8, width), f32),
        ],
        [
            ((total, width), f32), ((total, width), b16), ((total, width), f32),
            ((total, width), f32), ((total, f_tile), b16), ((total, f_tile), b16),
        ],
        limit=32,
        flops=12 * total * width * hidden_units,
    )

    def halve(keep, got, ways):
        count = keep.shape[0] // 2
        moving = hop(add(keep[count:], got[count:]), ways, groups, batch)
        return add(keep[:count], got[:count]), moving

    keep, got = own, flip(sent, "expert", 0)
    for ways in hops:
        keep, got = halve(keep, got, ways)
    whole = add(keep, got)
    for ways in hops[:0:-1]:
        whole = jnp.concatenate([whole, hop(whole, ways, groups, batch)], axis=0)
    own_low, got_low = whole, flip(whole, "expert", 0)
    own_high = hop(whole, hops[0], groups, batch)
    got_high = flip(own_high, "expert", 0)

    part, gq, kept, arrived = [], [], [], []
    for m in range(micros):
        p, keep, sent, g = call(
            functools.partial(backward_kernel, dims, m),
            [meta, lens],
            [gh, routes_t, gates[m], keys[m], keys_t[m], qt[m], ot[m], lse[m], router_t] + wq + wo,
            [
                ((tok, width), f32), ((groups // 2, tok, both), b16),
                ((groups // 2, tok, both), b16), ((every + pad, tok), b16),
            ],
            [((keys_all, both), f32), ((head, span), f32)],
            flops=5 * work,
            exps=tok * top * keys_all,
        )
        part.append(p)
        gq.append(g)
        count = groups // 2
        got = flip(sent, "expert", 0)
        for way in x_bits[::-1]:
            count //= 2
            moving = add(keep[count:], got[count:])
            keep = add(keep[:count], got[:count])
            got = flip(moving, *way)
        kept.append(keep)
        arrived.append(got)
    w_own, w_sent, router_rows = call(
        functools.partial(weights_kernel, (groups, size, tok, micros), rows_w),
        [table],
        [gh] + gq + normed + mixt,
        [((chips * rows_w, width), b16), ((chips * rows_w, width), b16), ((pad, width), f32)],
        flops=4 * total * every * width,
    )
    rows_all = both + pad + 16
    half = -(-rows_all // 32) * 16
    input_grad, b_own, b_sent = call(
        functools.partial(last_kernel, micros),
        [meta],
        [tokens, gh, vectors, key_value, up_row, ffn_rows, router_rows] + normed + part + kept + arrived,
        [((micros, tok, width), f32), ((half, width), b16), ((half, width), b16)],
        [((2 * half, width), b16)],
        flops=8 * total * width * both,
    )

    keep, got = w_own, flip(w_sent, "expert", 0)
    bundle = add(b_own, flip(b_sent, "expert", 0))
    for ways in hops:
        count = keep.shape[0] // 2
        moving = jnp.concatenate([add(keep[count:], got[count:]), bundle], axis=0)
        keep = add(keep[:count], got[:count])
        moving = hop(moving, ways, groups, batch)
        got = moving[:count]
        bundle = add(bundle, moving[count:])
    weights = add(keep, got)
    for way in b_bits[::-1]:
        weights = jnp.concatenate([weights, flip(weights, *way)], axis=0)

    wq_grad, wo_grad, grad_key_value, grad_router, grad_up_bias, *rows = call(
        functools.partial(small_kernel, (both, pad, rows_w)),
        [meta, final_table],
        [weights, bundle, flip(bundle, "expert", 0)],
        [
            ((size, width), f32), ((size, width), f32), ((width, both), f32),
            ((experts, width), f32), ((hidden_units,), f32),
        ] + [((width,), f32)] * 5,
        [((2 * half, width), b16)],
    )
    grad_down_bias, grad_gain_two, grad_shift_two, grad_gain_one, grad_shift_one = rows

    o_tile = 256

    def full(shape):
        return pl.BlockSpec(shape, lambda j, meta: (0,) * len(shape))

    grad_down, grad_up = pl.pallas_call(
        functools.partial(order_kernel, chunk),
        grid_spec=pltpu.PrefetchScalarGridSpec(
            num_scalar_prefetch=1,
            grid=(hidden_units // o_tile,),
            in_specs=[full(own_low.shape)] * 4,
            out_specs=[
                pl.BlockSpec((o_tile, width), lambda j, meta: (j, 0)),
                pl.BlockSpec((width, o_tile), lambda j, meta: (0, j)),
            ],
        ),
        out_shape=[
            jax.ShapeDtypeStruct((hidden_units, width), f32),
            jax.ShapeDtypeStruct((width, hidden_units), f32),
        ],
        compiler_params=pltpu.CompilerParams(vmem_limit_bytes=20 * MIB),
    )(meta, own_low, own_high, got_low, got_high)

    return (
        block_out.reshape(micros, tok, width),
        input_grad,
        grad_gain_one,
        grad_shift_one,
        grad_router.T,
        grad_key_value,
        wq_grad.reshape(local, head, width).transpose(0, 2, 1),
        wo_grad.reshape(local, head, width),
        grad_gain_two,
        grad_shift_two,
        grad_up,
        grad_up_bias,
        grad_down,
        grad_down_bias,
    )


def solution(mesh):
    split = P(None, ("batch", "expert"), None)
    own = P("expert", None, None)
    in_specs = (
        split, split, P(None, "batch", None), P(), P(), P(), P(), own, own, P(), P(), P(), P(), P(),
        P(), split,
    )
    out_specs = (split, split, P(), P(), P(), P(), own, own, P(), P(), P(), P(), P(), P())
    return jax.shard_map(shards, mesh=mesh, in_specs=in_specs, out_specs=out_specs, check_vma=False)
```

```python
import functools

import jax
import jax.numpy as jnp
from jax import lax
from jax.experimental import pallas as pl
from jax.experimental.pallas import tpu as pltpu
from jax.sharding import PartitionSpec as P

epsilon = 1e-05
b16 = jnp.bfloat16
f32 = jnp.float32
LOW = -1e30
MIB = 1024 * 1024


def dot(left, right, over=((1,), (0,))):
    return lax.dot_general(left, right, (over, ((), ())), preferred_element_type=f32)


def log2(size):
    return size.bit_length() - 1


def flip(values, axis, bit):
    size = lax.axis_size(axis)
    return lax.ppermute(values, axis, [(i, i ^ (1 << bit)) for i in range(size)])


def hop(values, ways, groups, batch):
    pairs = []
    for b in range(batch):
        for e in range(groups):
            axis, bit = ways[e & 1]
            to_b, to_e = (b, e ^ (1 << bit)) if axis == "expert" else (b ^ (1 << bit), e)
            pairs.append((b * groups + e, to_b * groups + to_e))
    return lax.ppermute(values, ("batch", "expert"), pairs)


def after(values, token):
    return lax.optimization_barrier((values, token))[0]


def add(left, right):
    return (left.astype(f32) + right.astype(f32)).astype(b16)


def normalize(values):
    centred = values - jnp.mean(values, axis=-1, keepdims=True)
    spread = lax.rsqrt(jnp.mean(centred * centred, axis=-1, keepdims=True) + epsilon)
    return centred * spread, spread


def norm_back(grad, unit, spread):
    inner = jnp.mean(grad * unit, axis=-1, keepdims=True)
    return spread * (grad - jnp.mean(grad, axis=-1, keepdims=True) - unit * inner)


def load(pairs, sems):
    copies = [pltpu.make_async_copy(a, b, sems.at[i]) for i, (a, b) in enumerate(pairs)]
    for copy in copies:
        copy.start()
    for copy in copies:
        copy.wait()


def row(vector):
    return vector[...].astype(f32).reshape(1, -1)


def first_kernel(micros, *refs):
    far = refs[:6]
    normed = refs[6 : 6 + micros]
    kv = refs[6 + micros : 6 + 2 * micros]
    gates = refs[6 + 2 * micros : 6 + 3 * micros]
    near = refs[6 + 3 * micros : -1]
    load(list(zip(far, near)), refs[-1])
    tokens, key_value, router, routes, gain, shift = near
    top = routes.shape[0]
    for m in range(micros):
        unit, _ = normalize(tokens[m].astype(f32))
        rows = (unit * row(gain) + row(shift)).astype(b16)
        normed[m][...] = rows
        kv[m][...] = dot(rows, key_value[...]).astype(b16)
        logits = dot(router[...], rows, ((1,), (1,)))
        ids = lax.broadcasted_iota(jnp.int32, logits.shape, 0)
        chosen = [
            jnp.sum(jnp.where(ids == routes[k, m : m + 1, :], logits, 0.0), axis=0, keepdims=True)
            for k in range(top)
        ]
        peak = functools.reduce(jnp.maximum, chosen)
        powers = [jnp.exp(c - peak) for c in chosen]
        total = sum(powers)
        for k in range(top):
            gates[m][k : k + 1, :] = powers[k] / total


def bounds(lens, first, count):
    place = first + lax.broadcasted_iota(jnp.int32, (1, count), 1)
    run = jnp.int32(0)
    low = jnp.int32(0)
    high = jnp.int32(0)
    start = jnp.zeros((1, count), jnp.int32)
    for length in lens:
        run = run + length
        start = jnp.where(place >= run, run, start)
        low = jnp.where(first >= run, run, low)
        high = jnp.where(first + count - 1 >= run, run, high)
    return place, start, low, high


def key_loops(body, carry, first, tile, low, high, block):
    begin = low // block
    full_end = first // block
    full_begin = jnp.minimum((high + block - 1) // block, full_end)
    end = (first + tile - 1) // block + 1
    carry = lax.fori_loop(begin, full_begin, functools.partial(body, True), carry)
    carry = lax.fori_loop(full_begin, full_end, functools.partial(body, False), carry)
    return lax.fori_loop(full_end, end, functools.partial(body, True), carry)


def spread_rows(pieces, ids, expert):
    out = jnp.zeros_like(pieces[0])
    for piece, row in zip(pieces, ids):
        out = jnp.where(row == expert, piece, out)
    return out


def gather_rows(table, ids, experts, head):
    out = jnp.zeros((head, table[0].shape[1]), f32)
    for piece, expert in zip(table, experts):
        out = jnp.where(ids == expert, piece, out)
    return out


def expert_ids(meta, groups, local):
    base = 4 + groups
    return [meta[base + s] * local + l for s in range(groups) for l in range(local)]


def head_table(weights, rows, local, head):
    out = []
    for piece in weights:
        whole = dot(piece[...], rows, ((1,), (1,)))
        out += [whole[l * head : (l + 1) * head] for l in range(local)]
    return out


def masked(scores, key_base, place, start):
    keys = key_base + lax.broadcasted_iota(jnp.int32, scores.shape, 0)
    return jnp.where((keys <= place) & (keys >= start), scores, LOW)


def forward_kernel(dims, micro, *refs):
    groups, tok, head, tile, block, top, local, pieces_all = dims
    meta, normed, routes, gates = refs[:4]
    pieces_kv = refs[4 : 4 + groups]
    weights = refs[4 + groups : 4 + 2 * groups]
    kv, kvt, qt, ot, lse, mixt, acc, held, routes_near, sems = refs[4 + 2 * groups :]
    me = meta[0]
    experts = expert_ids(meta, groups, local)
    pairs = [(piece, kv.at[pl.ds(s * tok, tok), :]) for s, piece in enumerate(pieces_kv)]
    pairs += [(piece, held.at[s]) for s, piece in enumerate(weights)]
    load(pairs + [(routes, routes_near)], sems)
    routes = routes_near
    lens = [meta[4 + 2 * groups + micro * pieces_all + j] for j in range(pieces_all)]
    for s in range(groups):
        kvt[:, s * tok : (s + 1) * tok] = kv[s * tok : (s + 1) * tok, :].T
    table = head_table([held.at[s] for s in range(groups)], normed[...], local, head)
    for i in range(tok // tile):
        cols = slice(i * tile, (i + 1) * tile)
        ids = [routes[k, micro : micro + 1, cols] for k in range(top)]
        part = [t[:, cols] for t in table]
        heads = [gather_rows(part, row, experts, head) for row in ids]
        query = jnp.concatenate(heads, axis=1).astype(b16) * jnp.asarray(0.125, b16)
        qt[i] = query
        padded = jnp.concatenate([query, jnp.zeros_like(query)], axis=0)
        first = me * tok + i * tile
        place, start, low, high = bounds(lens, first, tile)
        place = jnp.concatenate([place] * top, axis=1)
        start = jnp.concatenate([start] * top, axis=1)
        acc[...] = jnp.zeros_like(acc)

        def one_block(edge, index, carry):
            peak, total = carry
            chunk = (index * block) // tok
            row = index * block - chunk * tok
            at = pl.multiple_of(meta[4 + chunk] * tok + row, block)
            scores = dot(kv[pl.ds(at, block), :], padded)
            if edge:
                scores = masked(scores, index * block, place, start)
            new_peak = jnp.maximum(peak, jnp.max(scores, axis=0, keepdims=True))
            scale = jnp.exp(peak - new_peak)
            powers = jnp.exp(scores - new_peak)
            total = total * scale + jnp.sum(powers, axis=0, keepdims=True)
            acc[...] = acc[...] * scale + dot(kvt[head:, pl.ds(at, block)], powers.astype(b16))
            return new_peak, total

        width = top * tile
        none = (jnp.full((1, width), LOW, f32), jnp.zeros((1, width), f32))
        peak, total = key_loops(one_block, none, first, tile, low, high, block)
        out = acc[...] / total
        ot[i] = out
        lse[i] = peak + jnp.log(total)
        rounded = out.astype(b16).astype(f32)
        pieces = [
            rounded[:, k * tile : (k + 1) * tile] * gates[k : k + 1, cols] for k in range(top)
        ]
        for e, expert in enumerate(experts):
            mixt[e * head : (e + 1) * head, cols] = spread_rows(pieces, ids, expert).astype(b16)


def backward_kernel(dims, micro, *refs):
    groups, tok, head, tile, block, top, local, pieces_all = dims
    meta, gh, routes, gates, kv, kvt, qt, ot, lse, router = refs[:10]
    wq = refs[10 : 10 + groups]
    wo = refs[10 + groups : 10 + 2 * groups]
    part, keep, sent, gq, chosen_rows, token, dkv, dq = refs[10 + 2 * groups :]
    token[...] = jnp.zeros_like(token)
    lens = [meta[4 + 2 * groups + micro * pieces_all + j] for j in range(pieces_all)]
    me = meta[0]
    experts = expert_ids(meta, groups, local)
    every = len(experts) * head
    pad = chosen_rows.shape[0]
    dkv[...] = jnp.zeros_like(dkv)
    table = head_table(wo, gh[micro * tok : (micro + 1) * tok, :].astype(b16), local, head)
    for i in range(tok // tile):
        cols = slice(i * tile, (i + 1) * tile)
        ids = [routes[k, micro : micro + 1, cols] for k in range(top)]
        cut = [t[:, cols] for t in table]
        back = [gather_rows(cut, row, experts, head) for row in ids]
        weights = [gates[k : k + 1, cols] for k in range(top)]
        out = ot[i]
        outs = [out[:, k * tile : (k + 1) * tile] for k in range(top)]
        grad_gates = [
            jnp.sum(b * o.astype(b16).astype(f32), axis=0, keepdims=True)
            for b, o in zip(back, outs)
        ]
        inner = sum(w * g for w, g in zip(weights, grad_gates))
        chosen = [w * (g - inner) for w, g in zip(weights, grad_gates)]
        names = lax.broadcasted_iota(jnp.int32, (pad, tile), 0)
        chosen_rows[:, cols] = spread_rows(
            [jnp.broadcast_to(c, (pad, tile)) for c in chosen], ids, names
        ).astype(b16)
        grad = jnp.concatenate([w * b for w, b in zip(weights, back)], axis=1).astype(b16)
        delta = jnp.sum(grad.astype(f32) * out, axis=0, keepdims=True)
        query = qt[i]
        padded = jnp.concatenate([query, jnp.zeros_like(query)], axis=0)
        grad_pad = jnp.concatenate([jnp.zeros_like(grad), grad], axis=0)
        level = lse[i]
        first = me * tok + i * tile
        place, start, low, high = bounds(lens, first, tile)
        place = jnp.concatenate([place] * top, axis=1)
        start = jnp.concatenate([start] * top, axis=1)
        dq[...] = jnp.zeros_like(dq)

        def one_block(edge, index, carry):
            chunk = (index * block) // tok
            row = index * block - chunk * tok
            at = pl.multiple_of(meta[4 + chunk] * tok + row, block)
            keys = kv[pl.ds(at, block), :]
            scores = dot(keys, padded)
            if edge:
                scores = masked(scores, index * block, place, start)
            soft = jnp.exp(scores - level)
            grad_scores = (soft * (dot(keys, grad_pad) - delta)).astype(b16)
            dkv[pl.ds(at, block), :] += dot(grad_scores, padded, ((1,), (1,))) + dot(
                soft.astype(b16), grad_pad, ((1,), (1,))
            )
            dq[...] += dot(kvt[:head, pl.ds(at, block)], grad_scores)
            return carry

        key_loops(one_block, 0, first, tile, low, high, block)
        grad_query = dq[...] * 0.125
        pieces = [grad_query[:, k * tile : (k + 1) * tile] for k in range(top)]
        for e, expert in enumerate(experts):
            gq[e * head : (e + 1) * head, cols] = spread_rows(pieces, ids, expert).astype(b16)
    half = groups // 2
    for s in range(half):
        keep[s] = dkv[s * tok : (s + 1) * tok, :].astype(b16)
        sent[s] = dkv[(half + s) * tok : (half + s + 1) * tok, :].astype(b16)
    size = local * head
    total = dot(chosen_rows[: router.shape[0], :], router[...], ((0,), (0,)))
    for s in range(groups):
        total = total + dot(gq[s * size : (s + 1) * size, :], wq[s][...], ((0,), (0,)))
    part[...] = total


def weights_kernel(dims, rows, *refs):
    groups, size, tok, micros = dims
    table, _, gh = refs[:3]
    gq = refs[3 : 3 + micros]
    normed = refs[3 + micros : 3 + 2 * micros]
    mixt = refs[3 + 2 * micros : 3 + 3 * micros]
    own, sent = refs[3 + 3 * micros :]
    grads = [gh[m * tok : (m + 1) * tok, :].astype(b16) for m in range(micros)]
    for s in range(groups):
        at = slice(s * size, (s + 1) * size)
        wq = sum(dot(g[at, :], n[...]) for g, n in zip(gq, normed)).astype(b16)
        wo = sum(dot(m[at, :], g) for m, g in zip(mixt, grads)).astype(b16)
        target = own if s < groups // 2 else sent
        for k in range(2 * size // rows):
            to = pl.multiple_of(table[s, k] * rows, 16)
            source = wq if k * rows < size else wo
            begin = k * rows % size
            target[pl.ds(to, rows), :] = source[begin : begin + rows, :]


def ffn_kernel(dims, *refs):
    chunk, tile, sub, micros, groups = dims
    meta, tokens, cotan, gain, shift, down_bias, w_up, up_bias, w_down = refs[:9]
    mixt = refs[9 : 9 + micros]
    wo = refs[9 + micros : 9 + micros + groups]
    block_out, gh, own, sent, up_row, rows = refs[9 + micros + groups : 15 + micros + groups]
    hidden, second, acc, grad_acc, act_s, gu_s = refs[15 + micros + groups :]
    total, width = hidden.shape
    tok = tokens.shape[1]
    size = wo[0].shape[0]
    for m in range(micros):
        at = slice(m * tok, (m + 1) * tok)
        mixed = dot(mixt[m][:size, :], wo[0][...], ((0,), (0,)))
        for s in range(1, groups):
            mixed = mixed + dot(mixt[m][s * size : (s + 1) * size, :], wo[s][...], ((0,), (0,)))
        values = tokens[m].astype(f32) + mixed
        hidden[at, :] = values
        unit, _ = normalize(values)
        second[at, :] = (unit * row(gain) + row(shift)).astype(b16)
    acc[...] = jnp.zeros_like(acc)
    grad_acc[...] = jnp.zeros_like(grad_acc)
    c0 = 0.7978845608028654
    c1 = c0 * 0.044715
    per = tile // chunk

    def one_tile(step, carry):
        base = pl.multiple_of(step * tile, tile)
        span = pl.ds(base, tile)
        bias = up_bias[:, span].astype(f32)
        up_sum = jnp.zeros((1, tile), f32)
        for i in range(total // sub):
            at = slice(i * sub, (i + 1) * sub)
            upward = dot(second[at, :], w_up[:, span]) + bias
            grad = dot(cotan[at, :], w_down[span, :], ((1,), (1,)))
            square = upward * upward
            curve = jnp.tanh(upward * (c0 + c1 * square))
            lift = 0.5 + 0.5 * curve
            value = upward * lift
            slope = lift + value * (1.0 - curve) * (c0 + (3.0 * c1) * square)
            active = value.astype(b16)
            grad_up = (grad * slope).astype(b16)
            act_s[at, :] = active
            gu_s[at, :] = grad_up
            up_sum = up_sum + jnp.sum(grad_up.astype(f32), axis=0, keepdims=True)
            acc[at, :] += dot(active, w_down[span, :])
            grad_acc[at, :] += dot(grad_up, w_up[:, span], ((1,), (1,)))
        up_row[:, span] = up_sum
        grad_down = dot(act_s[...], cotan[...], ((0,), (0,))).astype(b16)
        grad_up_t = dot(gu_s[...], second[...], ((0,), (0,))).astype(b16)

        def place(values, target, low):
            for i in range(per):
                at = pl.multiple_of(((step * per + i) ^ low) * chunk, chunk)
                target[pl.ds(at, chunk), :] = values[i * chunk : (i + 1) * chunk, :]

        @pl.when(meta[1] == 0)
        def _():
            place(grad_down, own, meta[2])
            place(grad_up_t, sent, meta[3])

        @pl.when(meta[1] != 0)
        def _():
            place(grad_up_t, own, meta[2])
            place(grad_down, sent, meta[3])

        return carry

    lax.fori_loop(0, w_up.shape[1] // tile, one_tile, 0)
    sums = [jnp.zeros((1, width), f32) for _ in range(3)]
    for i in range(total // sub):
        at = slice(i * sub, (i + 1) * sub)
        rows_now = hidden[at, :]
        cot = cotan[at, :].astype(f32)
        block_out[at, :] = (rows_now + acc[at, :] + row(down_bias)).astype(b16)
        unit, spread = normalize(rows_now)
        grad = grad_acc[at, :]
        gh[at, :] = cot + norm_back(grad * row(gain), unit, spread)
        for j, piece in enumerate((cot, grad * unit, grad)):
            sums[j] = sums[j] + jnp.sum(piece, axis=0, keepdims=True)
    rows[...] = jnp.zeros_like(rows)
    for j in range(3):
        rows[j : j + 1, :] = sums[j]


def last_kernel(micros, *refs):
    meta, tokens, gh, gain, key_value, up_row, rows = refs[:7]
    normed = refs[7 : 7 + micros]
    part = refs[7 + micros : 7 + 2 * micros]
    kept = refs[7 + 2 * micros : 7 + 3 * micros]
    got = refs[7 + 3 * micros : 7 + 4 * micros]
    chosen = refs[7 + 4 * micros : 7 + 5 * micros]
    input_grad, own, sent, bundle = refs[7 + 5 * micros :]
    _, tok, width = tokens.shape
    key_rows = 0.0
    gain_sum = jnp.zeros((1, width), f32)
    shift_sum = jnp.zeros((1, width), f32)
    for m in range(micros):
        at = slice(m * tok, (m + 1) * tok)
        grad_kv = (kept[m][0].astype(f32) + got[m][0].astype(f32)).astype(b16)
        key_rows = key_rows + dot(grad_kv, normed[m][...], ((0,), (0,)))
        grad = part[m][...] + dot(grad_kv, key_value[...], ((1,), (1,)))
        unit, spread = normalize(tokens[m].astype(f32))
        input_grad[m] = gh[at, :] + norm_back(grad * row(gain), unit, spread)
        gain_sum = gain_sum + jnp.sum(grad * unit, axis=0, keepdims=True)
        shift_sum = shift_sum + jnp.sum(grad, axis=0, keepdims=True)
    at = key_rows.shape[0]
    pad = chosen[0].shape[0]
    bundle[:at, :] = key_rows.astype(b16)
    router_rows = sum(dot(c[...], n[...]) for c, n in zip(chosen, normed))
    bundle[at : at + pad, :] = router_rows.astype(b16)
    count = up_row.shape[1] // width
    pieces = [up_row[:, i * width : (i + 1) * width] for i in range(count)]
    pieces += [rows[0:3, :], gain_sum, shift_sum]
    left = bundle.shape[0] - at - pad - count - 5
    pieces.append(jnp.zeros((left, width), f32))
    bundle[at + pad :, :] = jnp.concatenate(pieces, axis=0).astype(b16)
    half = own.shape[0]
    own[...] = bundle[pl.ds(pl.multiple_of(meta[1] * half, 16), half), :]
    sent[...] = bundle[pl.ds(pl.multiple_of((1 - meta[1]) * half, 16), half), :]


def order_kernel(chunk, top, side, meta, own, got, *refs):
    down, up = refs[-2:]
    tile = down.shape[0]
    per = tile // chunk
    half = own.shape[0] // chunk

    def sorted_rows(ref, place):
        first = (pl.program_id(0) * per) ^ (place & (half - 1))
        blocks = []
        for i in range(per):
            at = pl.multiple_of((first ^ i) * chunk, chunk)
            blocks.append(ref[pl.ds(at, chunk), :].astype(f32))
        return blocks[0] if per == 1 else jnp.concatenate(blocks, axis=0)

    own_rows = sorted_rows(own, meta[2])
    got_rows = sorted_rows(got, meta[3])

    @pl.when(meta[1] == 0)
    def _():
        down[...] = own_rows
        up[...] = got_rows.T

    @pl.when(meta[1] != 0)
    def _():
        down[...] = got_rows
        up[...] = own_rows.T


def small_kernel(dims, meta, table, weights, own, got, wq, wo, keys, router, up_row, *outs):
    both, pad, rows = dims
    bundle = outs[-1]
    half, width = own.shape
    bundle[pl.ds(pl.multiple_of(meta[1] * half, 16), half), :] = own[...]
    bundle[pl.ds(pl.multiple_of((1 - meta[1]) * half, 16), half), :] = got[...]
    keys[...] = bundle[:both, :].astype(f32).T
    values = bundle[both:, :].astype(f32)
    router[...] = values[: router.shape[0], :]
    count = up_row.shape[0] // width
    for i in range(count):
        up_row[i * width : (i + 1) * width] = values[pad + i]
    for i, out in enumerate(outs[:-1]):
        out[...] = values[pad + count + i]
    size = wq.shape[0]
    for k in range(2 * size // rows):
        at = pl.multiple_of(table[k] * rows, 16)
        target = wq if k * rows < size else wo
        begin = k * rows % size
        target[begin : begin + rows, :] = weights[pl.ds(at, rows), :].astype(f32)


def shards(
    tokens, routes, lengths, gain_one, shift_one, router, key_value, w_query, w_out,
    gain_two, shift_two, w_up, up_bias, w_down, down_bias, cotangent,
):
    groups = lax.axis_size("expert")
    batch = lax.axis_size("batch")
    me = lax.axis_index("expert").astype(jnp.int32)
    mine = lax.axis_index("batch").astype(jnp.int32)
    micros, tok, width = tokens.shape
    top = routes.shape[2]
    local, _, head = w_query.shape
    experts = local * groups
    every = experts * head
    size = local * head
    hidden_units = w_up.shape[1]
    group_bits, batch_bits = log2(groups), log2(batch)
    chips = groups * batch // 2
    chunk = hidden_units // chips
    tile, block = min(256, tok), min(256, tok)
    tiles = tok // tile
    span = top * tile
    pad = -(-experts // 16) * 16
    both = 2 * head
    total = micros * tok
    core = me & 1

    x_bits = [("expert", bit) for bit in range(1, group_bits)]
    b_bits = [("batch", bit) for bit in range(batch_bits)]
    orders = (x_bits + b_bits, b_bits[:2] + x_bits + b_bits[2:])
    hops = list(zip(*orders))

    def place_of(order, expert, row):
        out = jnp.int32(0)
        for i, (axis, bit) in enumerate(order):
            index = expert if axis == "expert" else row
            out = out | (((index >> bit) & 1) << (len(order) - 1 - i))
        return out

    def by_core(first, second):
        return jnp.where(core == 0, first, second)

    high = group_bits - 1
    offsets = jnp.arange(groups, dtype=jnp.int32)
    away = offsets ^ me
    slots = (away >> 1) | ((away & 1) << high)
    devices = (((offsets << 1) & (groups - 1)) | (offsets >> high)) ^ me
    places = [place_of(order, me, mine) for order in orders]
    place_own, place_other = by_core(places[0], places[1]), by_core(places[1], places[0])
    meta = jnp.concatenate(
        [jnp.stack([me, core, place_own, place_other]), slots, devices, lengths.reshape(-1)]
    )
    rows_w = -(-2 * size // (16 * batch)) * 16
    subs = jnp.arange(2 * size // rows_w, dtype=jnp.int32)
    tables = [
        place_of(order, devices[:, None], subs[None, :]) ^ place_of(order, me, mine)
        for order in orders
    ]
    table = jnp.where(
        (offsets < groups // 2)[:, None],
        by_core(tables[0], tables[1]),
        by_core(tables[1], tables[0]),
    )
    final_table = place_of(b_bits, me, subs) ^ place_of(b_bits, me, mine)

    def gather_far(values):
        pieces = [values]
        for axis, bit in x_bits:
            pieces = pieces + [flip(p, axis, bit) for p in pieces]
        return pieces

    def gather_near(pieces):
        return pieces + [flip(p, "expert", 0) for p in pieces]

    def gather(values):
        return gather_near(gather_far(values))

    vmem = pl.BlockSpec(memory_space=pltpu.VMEM)
    smem = pl.BlockSpec(memory_space=pltpu.SMEM)

    def call(kernel, scalars, arrays, outs, scratch=(), limit=16, cost=1, far=(), sems=0):
        marks = [pltpu.SemaphoreType.DMA((sems,))] if sems else []
        far_spec = pl.BlockSpec(memory_space=pltpu.HBM)
        return pl.pallas_call(
            kernel,
            in_specs=[smem] * len(scalars) + [far_spec if i in far else vmem for i in range(len(arrays))],
            out_specs=[vmem] * len(outs),
            out_shape=[jax.ShapeDtypeStruct(*o) for o in outs],
            scratch_shapes=[pltpu.VMEM(*s) for s in scratch] + marks,
            compiler_params=pltpu.CompilerParams(vmem_limit_bytes=limit * MIB),
            cost_estimate=pl.CostEstimate(flops=int(cost * 1.1e9), bytes_accessed=0, transcendentals=0),
        )(
            *scalars,
            *[pltpu.with_memory_space_constraint(x, pltpu.HBM) if i in far else x for i, x in enumerate(arrays)],
        )

    wq = gather(w_query.transpose(0, 2, 1).reshape(size, width))
    router_t = router.T
    routes_t = routes.transpose(2, 0, 1)
    results = call(
        functools.partial(first_kernel, micros),
        [],
        [tokens, key_value, router_t, routes_t, gain_one, shift_one],
        [((tok, width), b16)] * micros + [((tok, both), b16)] * micros + [((8, tok), f32)] * micros,
        [
            ((micros, tok, width), b16), ((width, both), b16), ((experts, width), b16),
            ((top, micros, tok), jnp.int32), ((width,), b16), ((width,), b16),
        ],
        cost=2.4,
        far=range(6),
        sems=6,
    )
    normed, gates = list(results[:micros]), results[2 * micros :]
    kv_pieces = [gather_far(kv) for kv in results[micros : 2 * micros]]
    wo = gather(w_out.reshape(size, width))

    dims = (groups, tok, head, tile, block, top, local, lengths.shape[2])
    keys, keys_t, qt, ot, lse, mixt = [], [], [], [], [], []
    keys_all = groups * tok
    work = 2 * tok * top * keys_all * both
    for m in range(micros):
        if m > 0:
            kv_pieces[m] = after(kv_pieces[m], lse[m - 1])
        results = call(
            functools.partial(forward_kernel, dims, m),
            [meta],
            [normed[m], routes_t, gates[m]] + gather_near(kv_pieces[m]) + wq,
            [
                ((keys_all, both), b16), ((both, keys_all), b16), ((tiles, head, span), b16),
                ((tiles, head, span), f32), ((tiles, 1, span), f32), ((every, tok), b16),
            ],
            [((head, span), f32), ((groups, size, width), b16), ((top, micros, tok), jnp.int32)],
            cost=5,
            far=(1, *range(3, 3 + 2 * groups)),
            sems=2 * groups + 1,
        )
        for target, value in zip((keys, keys_t, qt, ot, lse, mixt), results):
            target.append(value)

    f_tile = 512
    block_out, gh, ffn_own, ffn_sent, up_row, ffn_rows = call(
        functools.partial(ffn_kernel, (chunk, f_tile, min(512, tok), micros, groups)),
        [meta],
        [
            tokens, cotangent.reshape(total, width), gain_two, shift_two, down_bias, w_up,
            up_bias.reshape(1, -1), w_down,
        ]
        + mixt + wo,
        [
            ((total, width), b16), ((total, width), f32), ((hidden_units, width), b16),
            ((hidden_units, width), b16), ((1, hidden_units), f32), ((8, width), f32),
        ],
        [
            ((total, width), f32), ((total, width), b16), ((total, width), f32),
            ((total, width), f32), ((total, f_tile), b16), ((total, f_tile), b16),
        ],
        limit=32,
        cost=11,
    )

    part, gq, chosen, kept, arrived, tokens_back = [], [], [], [], [], []
    for m in range(micros):
        p, keep, sent, g, c, token = call(
            functools.partial(backward_kernel, dims, m),
            [meta],
            [gh, routes_t, gates[m], keys[m], keys_t[m], qt[m], ot[m], lse[m], router_t] + wq + wo,
            [
                ((tok, width), f32), ((groups // 2, tok, both), b16),
                ((groups // 2, tok, both), b16), ((every, tok), b16), ((pad, tok), b16), ((8, 128), f32),
            ],
            [((keys_all, both), f32), ((head, span), f32)],
            cost=9,
        )
        part.append(p)
        gq.append(g)
        chosen.append(c)
        tokens_back.append(token)
        count = groups // 2
        got = flip(sent, "expert", 0)
        for way in x_bits[::-1]:
            count //= 2
            moving = add(keep[count:], got[count:])
            keep = add(keep[:count], got[:count])
            got = flip(moving, *way)
        kept.append(keep)
        arrived.append(got)
    def halve(keep, got, ways):
        count = keep.shape[0] // 2
        moving = hop(add(keep[count:], got[count:]), ways, groups, batch)
        return add(keep[:count], got[:count]), moving

    marks = []
    keep, got = ffn_own, flip(ffn_sent, "expert", 0)
    for ways in hops:
        keep, got = halve(keep, got, ways)
        marks.append(got)
    whole = add(keep, got)

    w_own, w_sent = call(
        functools.partial(weights_kernel, (groups, size, tok, micros), rows_w),
        [table],
        [marks[2], gh] + gq + normed + mixt,
        [((chips * rows_w, width), b16), ((chips * rows_w, width), b16)],
        cost=1.5,
        far=(0,),
    )
    rows_all = both + pad + 16
    half = -(-rows_all // 32) * 16
    input_grad, b_own, b_sent = call(
        functools.partial(last_kernel, micros),
        [meta],
        [tokens, gh, gain_one, key_value, up_row, ffn_rows] + normed + part + kept + arrived + chosen,
        [((micros, tok, width), f32), ((half, width), b16), ((half, width), b16)],
        [((2 * half, width), b16)],
        cost=3.8,
    )

    o_tile = 256
    o_count = hidden_units // o_tile // 2
    top_bit = log2(chips) - 1

    def ordered(side, own, got, filled):
        def block(which):
            def index(j, meta):
                place = jnp.where(meta[1] == which, meta[2], meta[3])
                return j + ((place >> top_bit) ^ side) * o_count

            return index

        down_at, up_at = block(0), block(1)
        near = pl.BlockSpec(own.shape, lambda j, meta: (0, 0))
        return pl.pallas_call(
            functools.partial(order_kernel, chunk, top_bit, side),
            grid_spec=pltpu.PrefetchScalarGridSpec(
                num_scalar_prefetch=1,
                grid=(o_count,),
                in_specs=[near, near] + [pl.BlockSpec(memory_space=pl.ANY)] * len(filled),
                out_specs=[
                    pl.BlockSpec((o_tile, width), lambda j, meta: (down_at(j, meta), 0)),
                    pl.BlockSpec((width, o_tile), lambda j, meta: (0, up_at(j, meta))),
                ],
            ),
            out_shape=[
                jax.ShapeDtypeStruct((hidden_units, width), f32),
                jax.ShapeDtypeStruct((width, hidden_units), f32),
            ],
            input_output_aliases={3 + i: i for i in range(len(filled))},
            compiler_params=pltpu.CompilerParams(vmem_limit_bytes=16 * MIB),
            cost_estimate=pl.CostEstimate(flops=0, bytes_accessed=hidden_units * width * 6, transcendentals=0),
        )(meta, own, got, *filled)

    keep, got = w_own, flip(w_sent, "expert", 0)
    bundle = add(b_own, flip(b_sent, "expert", 0))
    for up, (ways, back) in enumerate(zip(hops, hops[::-1])):
        count = keep.shape[0] // 2
        moving = jnp.concatenate([add(keep[count:], got[count:]), bundle], axis=0)
        keep = add(keep[:count], got[:count])
        arrived_rows = hop(whole, back, groups, batch)
        moving = hop(moving, ways, groups, batch)
        if up < len(hops) - 1:
            whole = jnp.concatenate([whole, arrived_rows], axis=0)
        got = moving[:count]
        bundle = add(bundle, moving[count:])
    own_low, own_high = whole, arrived_rows
    got_low, got_high = flip(own_low, "expert", 0), flip(own_high, "expert", 0)
    weights = add(keep, got)
    filled = ordered(0, own_low, got_low, ())
    for way in b_bits[::-1]:
        weights = jnp.concatenate([weights, flip(weights, *way)], axis=0)

    wq_grad, wo_grad, grad_key_value, grad_router, grad_up_bias, *rows = call(
        functools.partial(small_kernel, (both, pad, rows_w)),
        [meta, final_table],
        [weights, bundle, flip(bundle, "expert", 0)],
        [
            ((size, width), f32), ((size, width), f32), ((width, both), f32),
            ((experts, width), f32), ((hidden_units,), f32),
        ] + [((width,), f32)] * 5,
        [((2 * half, width), b16)],
    )
    grad_down_bias, grad_gain_two, grad_shift_two, grad_gain_one, grad_shift_one = rows

    grad_down, grad_up = ordered(1, own_high, got_high, filled)

    return (
        block_out.reshape(micros, tok, width),
        input_grad,
        grad_gain_one,
        grad_shift_one,
        grad_router.T,
        grad_key_value,
        wq_grad.reshape(local, head, width).transpose(0, 2, 1),
        wo_grad.reshape(local, head, width),
        grad_gain_two,
        grad_shift_two,
        grad_up,
        grad_up_bias,
        grad_down,
        grad_down_bias,
    )


def solution(mesh):
    split = P(None, ("batch", "expert"), None)
    own = P("expert", None, None)
    in_specs = (
        split, split, P(None, "batch", None), P(), P(), P(), P(), own, own, P(), P(), P(), P(), P(),
        P(), split,
    )
    out_specs = (split, split, P(), P(), P(), P(), own, own, P(), P(), P(), P(), P(), P())
    return jax.shard_map(shards, mesh=mesh, in_specs=in_specs, out_specs=out_specs, check_vma=False)
```

```python
import functools

import jax
import jax.numpy as jnp
from jax import lax
from jax.experimental import pallas as pl
from jax.experimental.pallas import tpu as pltpu
from jax.sharding import PartitionSpec as P

epsilon = 1e-05
b16 = jnp.bfloat16
f32 = jnp.float32
LOW = -1e30
MIB = 1024 * 1024


def dot(left, right, over=((1,), (0,))):
    return lax.dot_general(left, right, (over, ((), ())), preferred_element_type=f32)


def log2(size):
    return size.bit_length() - 1


def flip(values, axis, bit):
    size = lax.axis_size(axis)
    return lax.ppermute(values, axis, [(i, i ^ (1 << bit)) for i in range(size)])


def hop(values, ways, groups, batch):
    pairs = []
    for b in range(batch):
        for e in range(groups):
            axis, bit = ways[e & 1]
            to_b, to_e = (b, e ^ (1 << bit)) if axis == "expert" else (b ^ (1 << bit), e)
            pairs.append((b * groups + e, to_b * groups + to_e))
    return lax.ppermute(values, ("batch", "expert"), pairs)


def after(values, token):
    return lax.optimization_barrier((values, token))[0]


def add(left, right):
    return (left.astype(f32) + right.astype(f32)).astype(b16)


def normalize(values):
    centred = values - jnp.mean(values, axis=-1, keepdims=True)
    spread = lax.rsqrt(jnp.mean(centred * centred, axis=-1, keepdims=True) + epsilon)
    return centred * spread, spread


def norm_back(grad, unit, spread):
    inner = jnp.mean(grad * unit, axis=-1, keepdims=True)
    return spread * (grad - jnp.mean(grad, axis=-1, keepdims=True) - unit * inner)


def load(pairs, sems):
    copies = [pltpu.make_async_copy(a, b, sems.at[i]) for i, (a, b) in enumerate(pairs)]
    for copy in copies:
        copy.start()
    for copy in copies:
        copy.wait()


def row(vector):
    return vector[...].astype(f32).reshape(1, -1)


def first_kernel(micros, *refs):
    far = refs[:6]
    normed = refs[6 : 6 + micros]
    kv = refs[6 + micros : 6 + 2 * micros]
    gates = refs[6 + 2 * micros : 6 + 3 * micros]
    near = refs[6 + 3 * micros : -1]
    load(list(zip(far, near)), refs[-1])
    tokens, key_value, router, routes, gain, shift = near
    top = routes.shape[0]
    for m in range(micros):
        unit, _ = normalize(tokens[m].astype(f32))
        rows = (unit * row(gain) + row(shift)).astype(b16)
        normed[m][...] = rows
        kv[m][...] = dot(rows, key_value[...]).astype(b16)
        logits = dot(router[...], rows, ((1,), (1,)))
        ids = lax.broadcasted_iota(jnp.int32, logits.shape, 0)
        chosen = [
            jnp.sum(jnp.where(ids == routes[k, m : m + 1, :], logits, 0.0), axis=0, keepdims=True)
            for k in range(top)
        ]
        peak = functools.reduce(jnp.maximum, chosen)
        powers = [jnp.exp(c - peak) for c in chosen]
        total = sum(powers)
        for k in range(top):
            gates[m][k : k + 1, :] = powers[k] / total


def bounds(lens, first, count):
    place = first + lax.broadcasted_iota(jnp.int32, (1, count), 1)
    run = jnp.int32(0)
    low = jnp.int32(0)
    high = jnp.int32(0)
    start = jnp.zeros((1, count), jnp.int32)
    for length in lens:
        run = run + length
        start = jnp.where(place >= run, run, start)
        low = jnp.where(first >= run, run, low)
        high = jnp.where(first + count - 1 >= run, run, high)
    return place, start, low, high


def key_loops(body, carry, first, tile, low, high, block):
    begin = low // block
    full_end = first // block
    full_begin = jnp.minimum((high + block - 1) // block, full_end)
    end = (first + tile - 1) // block + 1
    carry = lax.fori_loop(begin, full_begin, functools.partial(body, True), carry)
    carry = lax.fori_loop(full_begin, full_end, functools.partial(body, False), carry)
    return lax.fori_loop(full_end, end, functools.partial(body, True), carry)


def spread_rows(pieces, ids, expert):
    out = jnp.zeros_like(pieces[0])
    for piece, row in zip(pieces, ids):
        out = jnp.where(row == expert, piece, out)
    return out


def gather_rows(table, ids, experts, head):
    out = jnp.zeros((head, table[0].shape[1]), f32)
    for piece, expert in zip(table, experts):
        out = jnp.where(ids == expert, piece, out)
    return out


def expert_ids(meta, groups, local):
    base = 4 + groups
    return [meta[base + s] * local + l for s in range(groups) for l in range(local)]


def head_table(weights, rows, local, head):
    out = []
    for piece in weights:
        whole = dot(piece[...], rows, ((1,), (1,)))
        out += [whole[l * head : (l + 1) * head] for l in range(local)]
    return out


def masked(scores, key_base, place, start):
    keys = key_base + lax.broadcasted_iota(jnp.int32, scores.shape, 0)
    return jnp.where((keys <= place) & (keys >= start), scores, LOW)


def forward_kernel(dims, micro, *refs):
    groups, tok, head, tile, block, top, local, pieces_all = dims
    meta, normed, routes, gates = refs[:4]
    pieces_kv = refs[4 : 4 + groups]
    weights = refs[4 + groups : 4 + 2 * groups]
    kv, kvt, qt, ot, lse, mixt, acc, held, routes_near, sems = refs[4 + 2 * groups :]
    me = meta[0]
    experts = expert_ids(meta, groups, local)
    pairs = [(piece, kv.at[pl.ds(s * tok, tok), :]) for s, piece in enumerate(pieces_kv)]
    pairs += [(piece, held.at[s]) for s, piece in enumerate(weights)]
    load(pairs + [(routes, routes_near)], sems)
    routes = routes_near
    lens = [meta[4 + 2 * groups + micro * pieces_all + j] for j in range(pieces_all)]
    for s in range(groups):
        kvt[:, s * tok : (s + 1) * tok] = kv[s * tok : (s + 1) * tok, :].T
    table = head_table([held.at[s] for s in range(groups)], normed[...], local, head)
    for i in range(tok // tile):
        cols = slice(i * tile, (i + 1) * tile)
        ids = [routes[k, micro : micro + 1, cols] for k in range(top)]
        part = [t[:, cols] for t in table]
        heads = [gather_rows(part, row, experts, head) for row in ids]
        query = jnp.concatenate(heads, axis=1).astype(b16) * jnp.asarray(0.125, b16)
        qt[i] = query
        padded = jnp.concatenate([query, jnp.zeros_like(query)], axis=0)
        first = me * tok + i * tile
        place, start, low, high = bounds(lens, first, tile)
        place = jnp.concatenate([place] * top, axis=1)
        start = jnp.concatenate([start] * top, axis=1)
        acc[...] = jnp.zeros_like(acc)

        def one_block(edge, index, carry):
            peak, total = carry
            chunk = (index * block) // tok
            row = index * block - chunk * tok
            at = pl.multiple_of(meta[4 + chunk] * tok + row, block)
            scores = dot(kv[pl.ds(at, block), :], padded)
            if edge:
                scores = masked(scores, index * block, place, start)
            new_peak = jnp.maximum(peak, jnp.max(scores, axis=0, keepdims=True))
            scale = jnp.exp(peak - new_peak)
            powers = jnp.exp(scores - new_peak)
            total = total * scale + jnp.sum(powers, axis=0, keepdims=True)
            acc[...] = acc[...] * scale + dot(kvt[head:, pl.ds(at, block)], powers.astype(b16))
            return new_peak, total

        width = top * tile
        none = (jnp.full((1, width), LOW, f32), jnp.zeros((1, width), f32))
        peak, total = key_loops(one_block, none, first, tile, low, high, block)
        out = acc[...] / total
        ot[i] = out
        lse[i] = peak + jnp.log(total)
        rounded = out.astype(b16).astype(f32)
        pieces = [
            rounded[:, k * tile : (k + 1) * tile] * gates[k : k + 1, cols] for k in range(top)
        ]
        for e, expert in enumerate(experts):
            mixt[e * head : (e + 1) * head, cols] = spread_rows(pieces, ids, expert).astype(b16)


def backward_kernel(dims, micro, *refs):
    groups, tok, head, tile, block, top, local, pieces_all = dims
    meta, gh, routes, gates, kv, kvt, qt, ot, lse, router = refs[:10]
    wq = refs[10 : 10 + groups]
    wo = refs[10 + groups : 10 + 2 * groups]
    part, keep, sent, gq, chosen_rows, token, dkv, dq = refs[10 + 2 * groups :]
    token[...] = jnp.zeros_like(token)
    lens = [meta[4 + 2 * groups + micro * pieces_all + j] for j in range(pieces_all)]
    me = meta[0]
    experts = expert_ids(meta, groups, local)
    every = len(experts) * head
    pad = chosen_rows.shape[0]
    dkv[...] = jnp.zeros_like(dkv)
    table = head_table(wo, gh[micro * tok : (micro + 1) * tok, :].astype(b16), local, head)
    for i in range(tok // tile):
        cols = slice(i * tile, (i + 1) * tile)
        ids = [routes[k, micro : micro + 1, cols] for k in range(top)]
        cut = [t[:, cols] for t in table]
        back = [gather_rows(cut, row, experts, head) for row in ids]
        weights = [gates[k : k + 1, cols] for k in range(top)]
        out = ot[i]
        outs = [out[:, k * tile : (k + 1) * tile] for k in range(top)]
        grad_gates = [
            jnp.sum(b * o.astype(b16).astype(f32), axis=0, keepdims=True)
            for b, o in zip(back, outs)
        ]
        inner = sum(w * g for w, g in zip(weights, grad_gates))
        chosen = [w * (g - inner) for w, g in zip(weights, grad_gates)]
        names = lax.broadcasted_iota(jnp.int32, (pad, tile), 0)
        chosen_rows[:, cols] = spread_rows(
            [jnp.broadcast_to(c, (pad, tile)) for c in chosen], ids, names
        ).astype(b16)
        grad = jnp.concatenate([w * b for w, b in zip(weights, back)], axis=1).astype(b16)
        delta = jnp.sum(grad.astype(f32) * out, axis=0, keepdims=True)
        query = qt[i]
        padded = jnp.concatenate([query, jnp.zeros_like(query)], axis=0)
        grad_pad = jnp.concatenate([jnp.zeros_like(grad), grad], axis=0)
        level = lse[i]
        first = me * tok + i * tile
        place, start, low, high = bounds(lens, first, tile)
        place = jnp.concatenate([place] * top, axis=1)
        start = jnp.concatenate([start] * top, axis=1)
        dq[...] = jnp.zeros_like(dq)

        def one_block(edge, index, carry):
            chunk = (index * block) // tok
            row = index * block - chunk * tok
            at = pl.multiple_of(meta[4 + chunk] * tok + row, block)
            keys = kv[pl.ds(at, block), :]
            scores = dot(keys, padded)
            if edge:
                scores = masked(scores, index * block, place, start)
            soft = jnp.exp(scores - level)
            grad_scores = (soft * (dot(keys, grad_pad) - delta)).astype(b16)
            dkv[pl.ds(at, block), :] += dot(grad_scores, padded, ((1,), (1,))) + dot(
                soft.astype(b16), grad_pad, ((1,), (1,))
            )
            dq[...] += dot(kvt[:head, pl.ds(at, block)], grad_scores)
            return carry

        key_loops(one_block, 0, first, tile, low, high, block)
        grad_query = dq[...] * 0.125
        pieces = [grad_query[:, k * tile : (k + 1) * tile] for k in range(top)]
        for e, expert in enumerate(experts):
            gq[e * head : (e + 1) * head, cols] = spread_rows(pieces, ids, expert).astype(b16)
    half = groups // 2
    for s in range(half):
        keep[s] = dkv[s * tok : (s + 1) * tok, :].astype(b16)
        sent[s] = dkv[(half + s) * tok : (half + s + 1) * tok, :].astype(b16)
    size = local * head
    total = dot(chosen_rows[: router.shape[0], :], router[...], ((0,), (0,)))
    for s in range(groups):
        total = total + dot(gq[s * size : (s + 1) * size, :], wq[s][...], ((0,), (0,)))
    part[...] = total


def weights_kernel(dims, rows, *refs):
    groups, size, tok, micros = dims
    table, _, gh = refs[:3]
    gq = refs[3 : 3 + micros]
    normed = refs[3 + micros : 3 + 2 * micros]
    mixt = refs[3 + 2 * micros : 3 + 3 * micros]
    own, sent = refs[3 + 3 * micros :]
    grads = [gh[m * tok : (m + 1) * tok, :].astype(b16) for m in range(micros)]
    for s in range(groups):
        at = slice(s * size, (s + 1) * size)
        wq = sum(dot(g[at, :], n[...]) for g, n in zip(gq, normed)).astype(b16)
        wo = sum(dot(m[at, :], g) for m, g in zip(mixt, grads)).astype(b16)
        target = own if s < groups // 2 else sent
        for k in range(2 * size // rows):
            to = pl.multiple_of(table[s, k] * rows, 16)
            source = wq if k * rows < size else wo
            begin = k * rows % size
            target[pl.ds(to, rows), :] = source[begin : begin + rows, :]


def ffn_kernel(dims, *refs):
    chunk, tile, sub, micros, groups = dims
    meta, tokens, cotan, gain, shift, down_bias, w_up, up_bias, w_down = refs[:9]
    mixt = refs[9 : 9 + micros]
    wo = refs[9 + micros : 9 + micros + groups]
    block_out, gh, own, sent, up_row, rows = refs[9 + micros + groups : 15 + micros + groups]
    hidden, second, acc, grad_acc, act_s, gu_s = refs[15 + micros + groups :]
    total, width = hidden.shape
    tok = tokens.shape[1]
    size = wo[0].shape[0]
    for m in range(micros):
        at = slice(m * tok, (m + 1) * tok)
        mixed = dot(mixt[m][:size, :], wo[0][...], ((0,), (0,)))
        for s in range(1, groups):
            mixed = mixed + dot(mixt[m][s * size : (s + 1) * size, :], wo[s][...], ((0,), (0,)))
        values = tokens[m].astype(f32) + mixed
        hidden[at, :] = values
        unit, _ = normalize(values)
        second[at, :] = (unit * row(gain) + row(shift)).astype(b16)
    acc[...] = jnp.zeros_like(acc)
    grad_acc[...] = jnp.zeros_like(grad_acc)
    c0 = 0.7978845608028654
    c1 = c0 * 0.044715
    per = tile // chunk

    def one_tile(step, carry):
        base = pl.multiple_of(step * tile, tile)
        span = pl.ds(base, tile)
        bias = up_bias[:, span].astype(f32)
        up_sum = jnp.zeros((1, tile), f32)
        for i in range(total // sub):
            at = slice(i * sub, (i + 1) * sub)
            upward = dot(second[at, :], w_up[:, span]) + bias
            grad = dot(cotan[at, :], w_down[span, :], ((1,), (1,)))
            square = upward * upward
            curve = jnp.tanh(upward * (c0 + c1 * square))
            lift = 0.5 + 0.5 * curve
            value = upward * lift
            slope = lift + value * (1.0 - curve) * (c0 + (3.0 * c1) * square)
            active = value.astype(b16)
            grad_up = (grad * slope).astype(b16)
            act_s[at, :] = active
            gu_s[at, :] = grad_up
            up_sum = up_sum + jnp.sum(grad_up.astype(f32), axis=0, keepdims=True)
            acc[at, :] += dot(active, w_down[span, :])
            grad_acc[at, :] += dot(grad_up, w_up[:, span], ((1,), (1,)))
        up_row[:, span] = up_sum
        grad_down = dot(act_s[...], cotan[...], ((0,), (0,))).astype(b16)
        grad_up_t = dot(gu_s[...], second[...], ((0,), (0,))).astype(b16)

        def place(values, target, low):
            for i in range(per):
                at = pl.multiple_of(((step * per + i) ^ low) * chunk, chunk)
                target[pl.ds(at, chunk), :] = values[i * chunk : (i + 1) * chunk, :]

        @pl.when(meta[1] == 0)
        def _():
            place(grad_down, own, meta[2])
            place(grad_up_t, sent, meta[3])

        @pl.when(meta[1] != 0)
        def _():
            place(grad_up_t, own, meta[2])
            place(grad_down, sent, meta[3])

        return carry

    lax.fori_loop(0, w_up.shape[1] // tile, one_tile, 0)
    sums = [jnp.zeros((1, width), f32) for _ in range(3)]
    for i in range(total // sub):
        at = slice(i * sub, (i + 1) * sub)
        rows_now = hidden[at, :]
        cot = cotan[at, :].astype(f32)
        block_out[at, :] = (rows_now + acc[at, :] + row(down_bias)).astype(b16)
        unit, spread = normalize(rows_now)
        grad = grad_acc[at, :]
        gh[at, :] = cot + norm_back(grad * row(gain), unit, spread)
        for j, piece in enumerate((cot, grad * unit, grad)):
            sums[j] = sums[j] + jnp.sum(piece, axis=0, keepdims=True)
    rows[...] = jnp.zeros_like(rows)
    for j in range(3):
        rows[j : j + 1, :] = sums[j]


def last_kernel(micros, *refs):
    meta, _, tokens, gh, gain, key_value, up_row, rows = refs[:8]
    normed = refs[8 : 8 + micros]
    part = refs[8 + micros : 8 + 2 * micros]
    kept = refs[8 + 2 * micros : 8 + 3 * micros]
    got = refs[8 + 3 * micros : 8 + 4 * micros]
    chosen = refs[8 + 4 * micros : 8 + 5 * micros]
    input_grad, own, sent, bundle = refs[8 + 5 * micros :]
    _, tok, width = tokens.shape
    key_rows = 0.0
    gain_sum = jnp.zeros((1, width), f32)
    shift_sum = jnp.zeros((1, width), f32)
    for m in range(micros):
        at = slice(m * tok, (m + 1) * tok)
        grad_kv = (kept[m][0].astype(f32) + got[m][0].astype(f32)).astype(b16)
        key_rows = key_rows + dot(grad_kv, normed[m][...], ((0,), (0,)))
        grad = part[m][...] + dot(grad_kv, key_value[...], ((1,), (1,)))
        unit, spread = normalize(tokens[m].astype(f32))
        input_grad[m] = gh[at, :] + norm_back(grad * row(gain), unit, spread)
        gain_sum = gain_sum + jnp.sum(grad * unit, axis=0, keepdims=True)
        shift_sum = shift_sum + jnp.sum(grad, axis=0, keepdims=True)
    at = key_rows.shape[0]
    pad = chosen[0].shape[0]
    bundle[:at, :] = key_rows.astype(b16)
    router_rows = sum(dot(c[...], n[...]) for c, n in zip(chosen, normed))
    bundle[at : at + pad, :] = router_rows.astype(b16)
    count = up_row.shape[1] // width
    pieces = [up_row[:, i * width : (i + 1) * width] for i in range(count)]
    pieces += [rows[0:3, :], gain_sum, shift_sum]
    left = bundle.shape[0] - at - pad - count - 5
    pieces.append(jnp.zeros((left, width), f32))
    bundle[at + pad :, :] = jnp.concatenate(pieces, axis=0).astype(b16)
    half = own.shape[0]
    own[...] = bundle[pl.ds(pl.multiple_of(meta[1] * half, 16), half), :]
    sent[...] = bundle[pl.ds(pl.multiple_of((1 - meta[1]) * half, 16), half), :]


def order_kernel(chunk, top, side, meta, own, got, *refs):
    down, up = refs[-2:]
    tile = down.shape[0]
    per = tile // chunk
    half = own.shape[0] // chunk

    def sorted_rows(ref, place):
        first = (pl.program_id(0) * per) ^ (place & (half - 1))
        blocks = []
        for i in range(per):
            at = pl.multiple_of((first ^ i) * chunk, chunk)
            blocks.append(ref[pl.ds(at, chunk), :].astype(f32))
        return blocks[0] if per == 1 else jnp.concatenate(blocks, axis=0)

    own_rows = sorted_rows(own, meta[2])
    got_rows = sorted_rows(got, meta[3])

    @pl.when(meta[1] == 0)
    def _():
        down[...] = own_rows
        up[...] = got_rows.T

    @pl.when(meta[1] != 0)
    def _():
        down[...] = got_rows
        up[...] = own_rows.T


def small_kernel(dims, meta, table, weights, own, got, wq, wo, keys, router, up_row, *outs):
    both, pad, rows = dims
    bundle = outs[-1]
    half, width = own.shape
    bundle[pl.ds(pl.multiple_of(meta[1] * half, 16), half), :] = own[...]
    bundle[pl.ds(pl.multiple_of((1 - meta[1]) * half, 16), half), :] = got[...]
    keys[...] = bundle[:both, :].astype(f32).T
    values = bundle[both:, :].astype(f32)
    router[...] = values[: router.shape[0], :]
    count = up_row.shape[0] // width
    for i in range(count):
        up_row[i * width : (i + 1) * width] = values[pad + i]
    for i, out in enumerate(outs[:-1]):
        out[...] = values[pad + count + i]
    size = wq.shape[0]
    for k in range(2 * size // rows):
        at = pl.multiple_of(table[k] * rows, 16)
        target = wq if k * rows < size else wo
        begin = k * rows % size
        target[begin : begin + rows, :] = weights[pl.ds(at, rows), :].astype(f32)


def shards(
    tokens, routes, lengths, gain_one, shift_one, router, key_value, w_query, w_out,
    gain_two, shift_two, w_up, up_bias, w_down, down_bias, cotangent,
):
    groups = lax.axis_size("expert")
    batch = lax.axis_size("batch")
    me = lax.axis_index("expert").astype(jnp.int32)
    mine = lax.axis_index("batch").astype(jnp.int32)
    micros, tok, width = tokens.shape
    top = routes.shape[2]
    local, _, head = w_query.shape
    experts = local * groups
    every = experts * head
    size = local * head
    hidden_units = w_up.shape[1]
    group_bits, batch_bits = log2(groups), log2(batch)
    chips = groups * batch // 2
    chunk = hidden_units // chips
    tile, block = min(256, tok), min(256, tok)
    tiles = tok // tile
    span = top * tile
    pad = -(-experts // 16) * 16
    both = 2 * head
    total = micros * tok
    core = me & 1

    x_bits = [("expert", bit) for bit in range(1, group_bits)]
    b_bits = [("batch", bit) for bit in range(batch_bits)]
    orders = (x_bits + b_bits, b_bits[:2] + x_bits + b_bits[2:])
    hops = list(zip(*orders))

    def place_of(order, expert, row):
        out = jnp.int32(0)
        for i, (axis, bit) in enumerate(order):
            index = expert if axis == "expert" else row
            out = out | (((index >> bit) & 1) << (len(order) - 1 - i))
        return out

    def by_core(first, second):
        return jnp.where(core == 0, first, second)

    high = group_bits - 1
    offsets = jnp.arange(groups, dtype=jnp.int32)
    away = offsets ^ me
    slots = (away >> 1) | ((away & 1) << high)
    devices = (((offsets << 1) & (groups - 1)) | (offsets >> high)) ^ me
    places = [place_of(order, me, mine) for order in orders]
    place_own, place_other = by_core(places[0], places[1]), by_core(places[1], places[0])
    meta = jnp.concatenate(
        [jnp.stack([me, core, place_own, place_other]), slots, devices, lengths.reshape(-1)]
    )
    rows_w = -(-2 * size // (16 * batch)) * 16
    subs = jnp.arange(2 * size // rows_w, dtype=jnp.int32)
    tables = [
        place_of(order, devices[:, None], subs[None, :]) ^ place_of(order, me, mine)
        for order in orders
    ]
    table = jnp.where(
        (offsets < groups // 2)[:, None],
        by_core(tables[0], tables[1]),
        by_core(tables[1], tables[0]),
    )
    final_table = place_of(b_bits, me, subs) ^ place_of(b_bits, me, mine)

    def gather_far(values):
        pieces = [values]
        for axis, bit in x_bits:
            pieces = pieces + [flip(p, axis, bit) for p in pieces]
        return pieces

    def gather_near(pieces):
        return pieces + [flip(p, "expert", 0) for p in pieces]

    def gather(values):
        return gather_near(gather_far(values))

    vmem = pl.BlockSpec(memory_space=pltpu.VMEM)
    smem = pl.BlockSpec(memory_space=pltpu.SMEM)

    def call(kernel, scalars, arrays, outs, scratch=(), limit=16, cost=1, far=(), sems=0):
        marks = [pltpu.SemaphoreType.DMA((sems,))] if sems else []
        far_spec = pl.BlockSpec(memory_space=pltpu.HBM)
        return pl.pallas_call(
            kernel,
            in_specs=[smem] * len(scalars) + [far_spec if i in far else vmem for i in range(len(arrays))],
            out_specs=[vmem] * len(outs),
            out_shape=[jax.ShapeDtypeStruct(*o) for o in outs],
            scratch_shapes=[pltpu.VMEM(*s) for s in scratch] + marks,
            compiler_params=pltpu.CompilerParams(vmem_limit_bytes=limit * MIB),
            cost_estimate=pl.CostEstimate(flops=int(cost * 1.1e9), bytes_accessed=0, transcendentals=0),
        )(
            *scalars,
            *[pltpu.with_memory_space_constraint(x, pltpu.HBM) if i in far else x for i, x in enumerate(arrays)],
        )

    wq = gather(w_query.transpose(0, 2, 1).reshape(size, width))
    router_t = router.T
    routes_t = routes.transpose(2, 0, 1)
    results = call(
        functools.partial(first_kernel, micros),
        [],
        [tokens, key_value, router_t, routes_t, gain_one, shift_one],
        [((tok, width), b16)] * micros + [((tok, both), b16)] * micros + [((8, tok), f32)] * micros,
        [
            ((micros, tok, width), b16), ((width, both), b16), ((experts, width), b16),
            ((top, micros, tok), jnp.int32), ((width,), b16), ((width,), b16),
        ],
        cost=2.4,
        far=range(6),
        sems=6,
    )
    normed, gates = list(results[:micros]), results[2 * micros :]
    kv_pieces = [gather_far(kv) for kv in results[micros : 2 * micros]]
    wo = gather(w_out.reshape(size, width))

    dims = (groups, tok, head, tile, block, top, local, lengths.shape[2])
    keys, keys_t, qt, ot, lse, mixt = [], [], [], [], [], []
    keys_all = groups * tok
    work = 2 * tok * top * keys_all * both
    for m in range(micros):
        if m > 0:
            kv_pieces[m] = after(kv_pieces[m], lse[m - 1])
        results = call(
            functools.partial(forward_kernel, dims, m),
            [meta],
            [normed[m], routes_t, gates[m]] + gather_near(kv_pieces[m]) + wq,
            [
                ((keys_all, both), b16), ((both, keys_all), b16), ((tiles, head, span), b16),
                ((tiles, head, span), f32), ((tiles, 1, span), f32), ((every, tok), b16),
            ],
            [((head, span), f32), ((groups, size, width), b16), ((top, micros, tok), jnp.int32)],
            cost=5,
            far=(1, *range(3, 3 + 2 * groups)),
            sems=2 * groups + 1,
        )
        for target, value in zip((keys, keys_t, qt, ot, lse, mixt), results):
            target.append(value)

    f_tile = 512
    block_out, gh, ffn_own, ffn_sent, up_row, ffn_rows = call(
        functools.partial(ffn_kernel, (chunk, f_tile, min(512, tok), micros, groups)),
        [meta],
        [
            tokens, cotangent.reshape(total, width), gain_two, shift_two, down_bias, w_up,
            up_bias.reshape(1, -1), w_down,
        ]
        + mixt + wo,
        [
            ((total, width), b16), ((total, width), f32), ((hidden_units, width), b16),
            ((hidden_units, width), b16), ((1, hidden_units), f32), ((8, width), f32),
        ],
        [
            ((total, width), f32), ((total, width), b16), ((total, width), f32),
            ((total, width), f32), ((total, f_tile), b16), ((total, f_tile), b16),
        ],
        limit=32,
        cost=11,
    )

    part, gq, chosen, kept, arrived, tokens_back = [], [], [], [], [], []
    for m in range(micros):
        p, keep, sent, g, c, token = call(
            functools.partial(backward_kernel, dims, m),
            [meta],
            [gh, routes_t, gates[m], keys[m], keys_t[m], qt[m], ot[m], lse[m], router_t] + wq + wo,
            [
                ((tok, width), f32), ((groups // 2, tok, both), b16),
                ((groups // 2, tok, both), b16), ((every, tok), b16), ((pad, tok), b16), ((8, 128), f32),
            ],
            [((keys_all, both), f32), ((head, span), f32)],
            cost=9,
        )
        part.append(p)
        gq.append(g)
        chosen.append(c)
        tokens_back.append(token)
        count = groups // 2
        got = flip(sent, "expert", 0)
        for way in x_bits[::-1]:
            count //= 2
            moving = add(keep[count:], got[count:])
            keep = add(keep[:count], got[:count])
            got = flip(moving, *way)
        kept.append(keep)
        arrived.append(got)
    def halve(keep, got, ways):
        count = keep.shape[0] // 2
        moving = hop(add(keep[count:], got[count:]), ways, groups, batch)
        return add(keep[:count], got[:count]), moving

    marks = []
    keep, got = ffn_own, flip(ffn_sent, "expert", 0)
    for i, ways in enumerate(hops):
        if 0 < i <= 2 and i <= micros:
            keep, gq[i - 1] = lax.optimization_barrier((keep, gq[i - 1]))
        keep, got = halve(keep, got, ways)
        marks.append(got)
    whole = add(keep, got)

    w_own, w_sent = call(
        functools.partial(weights_kernel, (groups, size, tok, micros), rows_w),
        [table],
        [marks[1], gh] + gq + normed + mixt,
        [((chips * rows_w, width), b16), ((chips * rows_w, width), b16)],
        cost=1.5,
        far=(0,),
    )
    rows_all = both + pad + 16
    half = -(-rows_all // 32) * 16
    input_grad, b_own, b_sent = call(
        functools.partial(last_kernel, micros),
        [meta],
        [marks[3], tokens, gh, gain_one, key_value, up_row, ffn_rows] + normed + part + kept + arrived + chosen,
        [((micros, tok, width), f32), ((half, width), b16), ((half, width), b16)],
        [((2 * half, width), b16)],
        cost=3.8,
        far=(0,),
    )

    o_tile = 256
    o_count = hidden_units // o_tile // 2
    top_bit = log2(chips) - 1

    def ordered(side, own, got, filled):
        def block(which):
            def index(j, meta):
                place = jnp.where(meta[1] == which, meta[2], meta[3])
                return j + ((place >> top_bit) ^ side) * o_count

            return index

        down_at, up_at = block(0), block(1)
        near = pl.BlockSpec(own.shape, lambda j, meta: (0, 0))
        return pl.pallas_call(
            functools.partial(order_kernel, chunk, top_bit, side),
            grid_spec=pltpu.PrefetchScalarGridSpec(
                num_scalar_prefetch=1,
                grid=(o_count,),
                in_specs=[near, near] + [pl.BlockSpec(memory_space=pl.ANY)] * len(filled),
                out_specs=[
                    pl.BlockSpec((o_tile, width), lambda j, meta: (down_at(j, meta), 0)),
                    pl.BlockSpec((width, o_tile), lambda j, meta: (0, up_at(j, meta))),
                ],
            ),
            out_shape=[
                jax.ShapeDtypeStruct((hidden_units, width), f32),
                jax.ShapeDtypeStruct((width, hidden_units), f32),
            ],
            input_output_aliases={3 + i: i for i in range(len(filled))},
            compiler_params=pltpu.CompilerParams(vmem_limit_bytes=16 * MIB),
            cost_estimate=pl.CostEstimate(flops=0, bytes_accessed=hidden_units * width * 6, transcendentals=0),
        )(meta, own, got, *filled)

    keep, got = w_own, flip(w_sent, "expert", 0)
    bundle = None
    for up, (ways, back) in enumerate(zip(hops, hops[::-1])):
        count = keep.shape[0] // 2
        moving = add(keep[count:], got[count:])
        keep = add(keep[:count], got[:count])
        if up == 1:
            bundle = add(b_own, flip(b_sent, "expert", 0))
        if up > 0:
            moving = jnp.concatenate([moving, bundle], axis=0)
        arrived_rows = hop(whole, back, groups, batch)
        moving = hop(moving, ways, groups, batch)
        if up < len(hops) - 1:
            whole = jnp.concatenate([whole, arrived_rows], axis=0)
        if up == len(hops) - 1:
            arrived_rows, moving = lax.optimization_barrier((arrived_rows, moving))
        got = moving[:count]
        if up > 0:
            bundle = add(bundle, moving[count:])
    bundle = add(bundle, hop(bundle, hops[0], groups, batch))
    own_low, own_high = whole, arrived_rows
    got_low, got_high = flip(own_low, "expert", 0), flip(own_high, "expert", 0)
    weights = add(keep, got)
    ways_up = b_bits[::-1]
    for i, way in enumerate(ways_up):
        came = flip(weights, *way)
        if i == len(ways_up) - 3:
            filled = ordered(0, own_low, got_low, ())
            came, *filled = lax.optimization_barrier((came, *filled))
        if i == len(ways_up) - 2:
            filled = ordered(1, own_high, got_high, filled)
            came, *filled = lax.optimization_barrier((came, *filled))
        weights = jnp.concatenate([weights, came], axis=0)
    grad_down, grad_up = filled

    wq_grad, wo_grad, grad_key_value, grad_router, grad_up_bias, *rows = call(
        functools.partial(small_kernel, (both, pad, rows_w)),
        [meta, final_table],
        [weights, bundle, flip(bundle, "expert", 0)],
        [
            ((size, width), f32), ((size, width), f32), ((width, both), f32),
            ((experts, width), f32), ((hidden_units,), f32),
        ] + [((width,), f32)] * 5,
        [((2 * half, width), b16)],
    )
    grad_down_bias, grad_gain_two, grad_shift_two, grad_gain_one, grad_shift_one = rows


    return (
        block_out.reshape(micros, tok, width),
        input_grad,
        grad_gain_one,
        grad_shift_one,
        grad_router.T,
        grad_key_value,
        wq_grad.reshape(local, head, width).transpose(0, 2, 1),
        wo_grad.reshape(local, head, width),
        grad_gain_two,
        grad_shift_two,
        grad_up,
        grad_up_bias,
        grad_down,
        grad_down_bias,
    )


def solution(mesh):
    split = P(None, ("batch", "expert"), None)
    own = P("expert", None, None)
    in_specs = (
        split, split, P(None, "batch", None), P(), P(), P(), P(), own, own, P(), P(), P(), P(), P(),
        P(), split,
    )
    out_specs = (split, split, P(), P(), P(), P(), own, own, P(), P(), P(), P(), P(), P())
    return jax.shard_map(shards, mesh=mesh, in_specs=in_specs, out_specs=out_specs, check_vma=False)
```

```python
import functools

import jax
import jax.numpy as jnp
from jax import lax
from jax.experimental import pallas as pl
from jax.experimental.pallas import tpu as pltpu
from jax.sharding import PartitionSpec as P

epsilon = 1e-05
b16 = jnp.bfloat16
f32 = jnp.float32
LOW = -1e30
MIB = 1024 * 1024


def dot(left, right, over=((1,), (0,))):
    return lax.dot_general(left, right, (over, ((), ())), preferred_element_type=f32)


def log2(size):
    return size.bit_length() - 1


def flip(values, axis, bit):
    size = lax.axis_size(axis)
    return lax.ppermute(values, axis, [(i, i ^ (1 << bit)) for i in range(size)])


def hop(values, ways, groups, batch):
    pairs = []
    for b in range(batch):
        for e in range(groups):
            axis, bit = ways[e & 1]
            to_b, to_e = (b, e ^ (1 << bit)) if axis == "expert" else (b ^ (1 << bit), e)
            pairs.append((b * groups + e, to_b * groups + to_e))
    return lax.ppermute(values, ("batch", "expert"), pairs)


def after(values, token):
    return lax.optimization_barrier((values, token))[0]


def add(left, right):
    return (left.astype(f32) + right.astype(f32)).astype(b16)


def normalize(values):
    centred = values - jnp.mean(values, axis=-1, keepdims=True)
    spread = lax.rsqrt(jnp.mean(centred * centred, axis=-1, keepdims=True) + epsilon)
    return centred * spread, spread


def norm_back(grad, unit, spread):
    inner = jnp.mean(grad * unit, axis=-1, keepdims=True)
    return spread * (grad - jnp.mean(grad, axis=-1, keepdims=True) - unit * inner)


def load(pairs, sems):
    copies = [pltpu.make_async_copy(a, b, sems.at[i]) for i, (a, b) in enumerate(pairs)]
    for copy in copies:
        copy.start()
    for copy in copies:
        copy.wait()


def row(vector):
    return vector[...].astype(f32).reshape(1, -1)


def first_kernel(micros, *refs):
    far = refs[:6]
    normed = refs[6 : 6 + micros]
    kv = refs[6 + micros : 6 + 2 * micros]
    gates = refs[6 + 2 * micros : 6 + 3 * micros]
    near = refs[6 + 3 * micros : -1]
    load(list(zip(far, near)), refs[-1])
    tokens, key_value, router, routes, gain, shift = near
    top = routes.shape[0]
    for m in range(micros):
        unit, _ = normalize(tokens[m].astype(f32))
        rows = (unit * row(gain) + row(shift)).astype(b16)
        normed[m][...] = rows
        kv[m][...] = dot(rows, key_value[...]).astype(b16)
        logits = dot(router[...], rows, ((1,), (1,)))
        ids = lax.broadcasted_iota(jnp.int32, logits.shape, 0)
        chosen = [
            jnp.sum(jnp.where(ids == routes[k, m : m + 1, :], logits, 0.0), axis=0, keepdims=True)
            for k in range(top)
        ]
        peak = functools.reduce(jnp.maximum, chosen)
        powers = [jnp.exp(c - peak) for c in chosen]
        total = sum(powers)
        for k in range(top):
            gates[m][k : k + 1, :] = powers[k] / total


def bounds(lens, first, count):
    place = first + lax.broadcasted_iota(jnp.int32, (1, count), 1)
    run = jnp.int32(0)
    low = jnp.int32(0)
    high = jnp.int32(0)
    start = jnp.zeros((1, count), jnp.int32)
    for length in lens:
        run = run + length
        start = jnp.where(place >= run, run, start)
        low = jnp.where(first >= run, run, low)
        high = jnp.where(first + count - 1 >= run, run, high)
    return place, start, low, high


def key_loops(body, carry, first, tile, low, high, block):
    begin = low // block
    full_end = first // block
    full_begin = jnp.minimum((high + block - 1) // block, full_end)
    end = (first + tile - 1) // block + 1
    carry = lax.fori_loop(begin, full_begin, functools.partial(body, True), carry)
    carry = lax.fori_loop(full_begin, full_end, functools.partial(body, False), carry)
    return lax.fori_loop(full_end, end, functools.partial(body, True), carry)


def spread_rows(pieces, ids, expert):
    out = jnp.zeros_like(pieces[0])
    for piece, row in zip(pieces, ids):
        out = jnp.where(row == expert, piece, out)
    return out


def gather_rows(table, ids, experts, head):
    out = jnp.zeros((head, table[0].shape[1]), f32)
    for piece, expert in zip(table, experts):
        out = jnp.where(ids == expert, piece, out)
    return out


def expert_ids(meta, groups, local):
    base = 4 + groups
    return [meta[base + s] * local + l for s in range(groups) for l in range(local)]


def head_table(weights, rows, local, head):
    out = []
    for piece in weights:
        whole = dot(piece[...], rows, ((1,), (1,)))
        out += [whole[l * head : (l + 1) * head] for l in range(local)]
    return out


def masked(scores, key_base, place, start):
    keys = key_base + lax.broadcasted_iota(jnp.int32, scores.shape, 0)
    return jnp.where((keys <= place) & (keys >= start), scores, LOW)


def forward_kernel(dims, micro, *refs):
    groups, tok, head, tile, block, top, local, pieces_all = dims
    meta, normed, routes, gates = refs[:4]
    pieces_kv = refs[4 : 4 + groups]
    weights = refs[4 + groups : 4 + 2 * groups]
    kv, kvt, qt, ot, lse, mixt, acc, held, routes_near, sems = refs[4 + 2 * groups :]
    me = meta[0]
    experts = expert_ids(meta, groups, local)
    pairs = [(piece, kv.at[pl.ds(s * tok, tok), :]) for s, piece in enumerate(pieces_kv)]
    pairs += [(piece, held.at[s]) for s, piece in enumerate(weights)]
    load(pairs + [(routes, routes_near)], sems)
    routes = routes_near
    lens = [meta[4 + 2 * groups + micro * pieces_all + j] for j in range(pieces_all)]
    for s in range(groups):
        kvt[:, s * tok : (s + 1) * tok] = kv[s * tok : (s + 1) * tok, :].T
    table = head_table([held.at[s] for s in range(groups)], normed[...], local, head)
    for i in range(tok // tile):
        cols = slice(i * tile, (i + 1) * tile)
        ids = [routes[k, micro : micro + 1, cols] for k in range(top)]
        part = [t[:, cols] for t in table]
        heads = [gather_rows(part, row, experts, head) for row in ids]
        query = jnp.concatenate(heads, axis=1).astype(b16) * jnp.asarray(0.125, b16)
        qt[i] = query
        padded = jnp.concatenate([query, jnp.zeros_like(query)], axis=0)
        first = me * tok + i * tile
        place, start, low, high = bounds(lens, first, tile)
        place = jnp.concatenate([place] * top, axis=1)
        start = jnp.concatenate([start] * top, axis=1)
        acc[...] = jnp.zeros_like(acc)

        def one_block(edge, index, carry):
            peak, total = carry
            chunk = (index * block) // tok
            row = index * block - chunk * tok
            at = pl.multiple_of(meta[4 + chunk] * tok + row, block)
            scores = dot(kv[pl.ds(at, block), :], padded)
            if edge:
                scores = masked(scores, index * block, place, start)
            new_peak = jnp.maximum(peak, jnp.max(scores, axis=0, keepdims=True))
            scale = jnp.exp(peak - new_peak)
            powers = jnp.exp(scores - new_peak)
            total = total * scale + jnp.sum(powers, axis=0, keepdims=True)
            acc[...] = acc[...] * scale + dot(kvt[head:, pl.ds(at, block)], powers.astype(b16))
            return new_peak, total

        width = top * tile
        none = (jnp.full((1, width), LOW, f32), jnp.zeros((1, width), f32))
        peak, total = key_loops(one_block, none, first, tile, low, high, block)
        out = acc[...] / total
        ot[i] = out
        lse[i] = peak + jnp.log(total)
        rounded = out.astype(b16).astype(f32)
        pieces = [
            rounded[:, k * tile : (k + 1) * tile] * gates[k : k + 1, cols] for k in range(top)
        ]
        for e, expert in enumerate(experts):
            mixt[e * head : (e + 1) * head, cols] = spread_rows(pieces, ids, expert).astype(b16)


def backward_kernel(dims, micro, *refs):
    groups, tok, head, tile, block, top, local, pieces_all = dims
    meta, gh, routes, gates, kv, kvt, qt, ot, lse, router = refs[:10]
    wq = refs[10 : 10 + groups]
    wo = refs[10 + groups : 10 + 2 * groups]
    part, keep, sent, gq, chosen_rows, token, dkv, dq = refs[10 + 2 * groups :]
    token[...] = jnp.zeros_like(token)
    lens = [meta[4 + 2 * groups + micro * pieces_all + j] for j in range(pieces_all)]
    me = meta[0]
    experts = expert_ids(meta, groups, local)
    every = len(experts) * head
    pad = chosen_rows.shape[0]
    dkv[...] = jnp.zeros_like(dkv)
    table = head_table(wo, gh[micro * tok : (micro + 1) * tok, :].astype(b16), local, head)
    for i in range(tok // tile):
        cols = slice(i * tile, (i + 1) * tile)
        ids = [routes[k, micro : micro + 1, cols] for k in range(top)]
        cut = [t[:, cols] for t in table]
        back = [gather_rows(cut, row, experts, head) for row in ids]
        weights = [gates[k : k + 1, cols] for k in range(top)]
        out = ot[i]
        outs = [out[:, k * tile : (k + 1) * tile] for k in range(top)]
        grad_gates = [
            jnp.sum(b * o.astype(b16).astype(f32), axis=0, keepdims=True)
            for b, o in zip(back, outs)
        ]
        inner = sum(w * g for w, g in zip(weights, grad_gates))
        chosen = [w * (g - inner) for w, g in zip(weights, grad_gates)]
        names = lax.broadcasted_iota(jnp.int32, (pad, tile), 0)
        chosen_rows[:, cols] = spread_rows(
            [jnp.broadcast_to(c, (pad, tile)) for c in chosen], ids, names
        ).astype(b16)
        grad = jnp.concatenate([w * b for w, b in zip(weights, back)], axis=1).astype(b16)
        delta = jnp.sum(grad.astype(f32) * out, axis=0, keepdims=True)
        query = qt[i]
        padded = jnp.concatenate([query, jnp.zeros_like(query)], axis=0)
        grad_pad = jnp.concatenate([jnp.zeros_like(grad), grad], axis=0)
        level = lse[i]
        first = me * tok + i * tile
        place, start, low, high = bounds(lens, first, tile)
        place = jnp.concatenate([place] * top, axis=1)
        start = jnp.concatenate([start] * top, axis=1)
        dq[...] = jnp.zeros_like(dq)

        def one_block(edge, index, carry):
            chunk = (index * block) // tok
            row = index * block - chunk * tok
            at = pl.multiple_of(meta[4 + chunk] * tok + row, block)
            keys = kv[pl.ds(at, block), :]
            scores = dot(keys, padded)
            if edge:
                scores = masked(scores, index * block, place, start)
            soft = jnp.exp(scores - level)
            grad_scores = (soft * (dot(keys, grad_pad) - delta)).astype(b16)
            dkv[pl.ds(at, block), :] += dot(grad_scores, padded, ((1,), (1,))) + dot(
                soft.astype(b16), grad_pad, ((1,), (1,))
            )
            dq[...] += dot(kvt[:head, pl.ds(at, block)], grad_scores)
            return carry

        key_loops(one_block, 0, first, tile, low, high, block)
        grad_query = dq[...] * 0.125
        pieces = [grad_query[:, k * tile : (k + 1) * tile] for k in range(top)]
        for e, expert in enumerate(experts):
            gq[e * head : (e + 1) * head, cols] = spread_rows(pieces, ids, expert).astype(b16)
    half = groups // 2
    for s in range(half):
        keep[s] = dkv[s * tok : (s + 1) * tok, :].astype(b16)
        sent[s] = dkv[(half + s) * tok : (half + s + 1) * tok, :].astype(b16)
    size = local * head
    total = dot(chosen_rows[: router.shape[0], :], router[...], ((0,), (0,)))
    for s in range(groups):
        total = total + dot(gq[s * size : (s + 1) * size, :], wq[s][...], ((0,), (0,)))
    part[...] = total


def weights_kernel(dims, rows, *refs):
    groups, size, tok, micros = dims
    table, _, gh = refs[:3]
    gq = refs[3 : 3 + micros]
    normed = refs[3 + micros : 3 + 2 * micros]
    mixt = refs[3 + 2 * micros : 3 + 3 * micros]
    own, sent = refs[3 + 3 * micros :]
    grads = [gh[m * tok : (m + 1) * tok, :].astype(b16) for m in range(micros)]
    for s in range(groups):
        at = slice(s * size, (s + 1) * size)
        wq = sum(dot(g[at, :], n[...]) for g, n in zip(gq, normed)).astype(b16)
        wo = sum(dot(m[at, :], g) for m, g in zip(mixt, grads)).astype(b16)
        target = own if s < groups // 2 else sent
        for k in range(2 * size // rows):
            to = pl.multiple_of(table[s, k] * rows, 16)
            source = wq if k * rows < size else wo
            begin = k * rows % size
            target[pl.ds(to, rows), :] = source[begin : begin + rows, :]


def ffn_kernel(dims, *refs):
    chunk, tile, sub, micros, groups = dims
    meta, tokens, cotan, gain, shift, down_bias, w_up, up_bias, w_down = refs[:9]
    mixt = refs[9 : 9 + micros]
    wo = refs[9 + micros : 9 + micros + groups]
    own, sent, up_row, hidden, acc, grad_acc = refs[9 + micros + groups : 15 + micros + groups]
    second, act_s, gu_s = refs[15 + micros + groups :]
    total, width = hidden.shape
    tok = tokens.shape[1]
    size = wo[0].shape[0]
    for m in range(micros):
        at = slice(m * tok, (m + 1) * tok)
        mixed = dot(mixt[m][:size, :], wo[0][...], ((0,), (0,)))
        for s in range(1, groups):
            mixed = mixed + dot(mixt[m][s * size : (s + 1) * size, :], wo[s][...], ((0,), (0,)))
        values = tokens[m].astype(f32) + mixed
        hidden[at, :] = values
        unit, _ = normalize(values)
        second[at, :] = (unit * row(gain) + row(shift)).astype(b16)
    acc[...] = jnp.zeros_like(acc)
    grad_acc[...] = jnp.zeros_like(grad_acc)
    c0 = 0.7978845608028654
    c1 = c0 * 0.044715
    per = tile // chunk

    def one_tile(step, carry):
        base = pl.multiple_of(step * tile, tile)
        span = pl.ds(base, tile)
        bias = up_bias[:, span].astype(f32)
        up_sum = jnp.zeros((1, tile), f32)
        for i in range(total // sub):
            at = slice(i * sub, (i + 1) * sub)
            upward = dot(second[at, :], w_up[:, span]) + bias
            grad = dot(cotan[at, :], w_down[span, :], ((1,), (1,)))
            square = upward * upward
            curve = jnp.tanh(upward * (c0 + c1 * square))
            lift = 0.5 + 0.5 * curve
            value = upward * lift
            slope = lift + value * (1.0 - curve) * (c0 + (3.0 * c1) * square)
            active = value.astype(b16)
            grad_up = (grad * slope).astype(b16)
            act_s[at, :] = active
            gu_s[at, :] = grad_up
            up_sum = up_sum + jnp.sum(grad_up.astype(f32), axis=0, keepdims=True)
            acc[at, :] += dot(active, w_down[span, :])
            grad_acc[at, :] += dot(grad_up, w_up[:, span], ((1,), (1,)))
        up_row[:, span] = up_sum
        grad_down = dot(act_s[...], cotan[...], ((0,), (0,))).astype(b16)
        grad_up_t = dot(gu_s[...], second[...], ((0,), (0,))).astype(b16)

        def place(values, target, low):
            for i in range(per):
                at = pl.multiple_of(((step * per + i) ^ low) * chunk, chunk)
                target[pl.ds(at, chunk), :] = values[i * chunk : (i + 1) * chunk, :]

        @pl.when(meta[1] == 0)
        def _():
            place(grad_down, own, meta[2])
            place(grad_up_t, sent, meta[3])

        @pl.when(meta[1] != 0)
        def _():
            place(grad_up_t, own, meta[2])
            place(grad_down, sent, meta[3])

        return carry

    lax.fori_loop(0, w_up.shape[1] // tile, one_tile, 0)


def second_norm_kernel(sub, cotan, gain, down_bias, hidden, acc, grad_acc, block_out, gh, rows):
    total, width = hidden.shape
    sums = [jnp.zeros((1, width), f32) for _ in range(3)]
    for i in range(total // sub):
        at = slice(i * sub, (i + 1) * sub)
        rows_now = hidden[at, :]
        cot = cotan[at, :].astype(f32)
        block_out[at, :] = (rows_now + acc[at, :] + row(down_bias)).astype(b16)
        unit, spread = normalize(rows_now)
        grad = grad_acc[at, :]
        gh[at, :] = cot + norm_back(grad * row(gain), unit, spread)
        for j, piece in enumerate((cot, grad * unit, grad)):
            sums[j] = sums[j] + jnp.sum(piece, axis=0, keepdims=True)
    rows[...] = jnp.zeros_like(rows)
    for j in range(3):
        rows[j : j + 1, :] = sums[j]


def last_kernel(micros, *refs):
    meta, _, tokens, gh, gain, key_value, up_row, rows = refs[:8]
    normed = refs[8 : 8 + micros]
    part = refs[8 + micros : 8 + 2 * micros]
    kept = refs[8 + 2 * micros : 8 + 3 * micros]
    got = refs[8 + 3 * micros : 8 + 4 * micros]
    chosen = refs[8 + 4 * micros : 8 + 5 * micros]
    input_grad, own, sent, bundle = refs[8 + 5 * micros :]
    _, tok, width = tokens.shape
    key_rows = 0.0
    gain_sum = jnp.zeros((1, width), f32)
    shift_sum = jnp.zeros((1, width), f32)
    for m in range(micros):
        at = slice(m * tok, (m + 1) * tok)
        grad_kv = (kept[m][0].astype(f32) + got[m][0].astype(f32)).astype(b16)
        key_rows = key_rows + dot(grad_kv, normed[m][...], ((0,), (0,)))
        grad = part[m][...] + dot(grad_kv, key_value[...], ((1,), (1,)))
        unit, spread = normalize(tokens[m].astype(f32))
        input_grad[m] = gh[at, :] + norm_back(grad * row(gain), unit, spread)
        gain_sum = gain_sum + jnp.sum(grad * unit, axis=0, keepdims=True)
        shift_sum = shift_sum + jnp.sum(grad, axis=0, keepdims=True)
    at = key_rows.shape[0]
    pad = chosen[0].shape[0]
    bundle[:at, :] = key_rows.astype(b16)
    router_rows = sum(dot(c[...], n[...]) for c, n in zip(chosen, normed))
    bundle[at : at + pad, :] = router_rows.astype(b16)
    count = up_row.shape[1] // width
    pieces = [up_row[:, i * width : (i + 1) * width] for i in range(count)]
    pieces += [rows[0:3, :], gain_sum, shift_sum]
    left = bundle.shape[0] - at - pad - count - 5
    pieces.append(jnp.zeros((left, width), f32))
    bundle[at + pad :, :] = jnp.concatenate(pieces, axis=0).astype(b16)
    half = own.shape[0]
    own[...] = bundle[pl.ds(pl.multiple_of(meta[1] * half, 16), half), :]
    sent[...] = bundle[pl.ds(pl.multiple_of((1 - meta[1]) * half, 16), half), :]


def order_kernel(chunk, top, side, meta, own, got, *refs):
    down, up = refs[-2:]
    tile = down.shape[0]
    per = tile // chunk
    half = own.shape[0] // chunk

    def sorted_rows(ref, place):
        first = (pl.program_id(0) * per) ^ (place & (half - 1))
        blocks = []
        for i in range(per):
            at = pl.multiple_of((first ^ i) * chunk, chunk)
            blocks.append(ref[pl.ds(at, chunk), :].astype(f32))
        return blocks[0] if per == 1 else jnp.concatenate(blocks, axis=0)

    own_rows = sorted_rows(own, meta[2])
    got_rows = sorted_rows(got, meta[3])

    @pl.when(meta[1] == 0)
    def _():
        down[...] = own_rows
        up[...] = got_rows.T

    @pl.when(meta[1] != 0)
    def _():
        down[...] = got_rows
        up[...] = own_rows.T


def small_kernel(dims, meta, table, weights, own, got, wq, wo, keys, router, up_row, *outs):
    both, pad, rows = dims
    bundle = outs[-1]
    half, width = own.shape
    bundle[pl.ds(pl.multiple_of(meta[1] * half, 16), half), :] = own[...]
    bundle[pl.ds(pl.multiple_of((1 - meta[1]) * half, 16), half), :] = got[...]
    keys[...] = bundle[:both, :].astype(f32).T
    values = bundle[both:, :].astype(f32)
    router[...] = values[: router.shape[0], :]
    count = up_row.shape[0] // width
    for i in range(count):
        up_row[i * width : (i + 1) * width] = values[pad + i]
    for i, out in enumerate(outs[:-1]):
        out[...] = values[pad + count + i]
    size = wq.shape[0]
    for k in range(2 * size // rows):
        at = pl.multiple_of(table[k] * rows, 16)
        target = wq if k * rows < size else wo
        begin = k * rows % size
        target[begin : begin + rows, :] = weights[pl.ds(at, rows), :].astype(f32)


def shards(
    tokens, routes, lengths, gain_one, shift_one, router, key_value, w_query, w_out,
    gain_two, shift_two, w_up, up_bias, w_down, down_bias, cotangent,
):
    groups = lax.axis_size("expert")
    batch = lax.axis_size("batch")
    me = lax.axis_index("expert").astype(jnp.int32)
    mine = lax.axis_index("batch").astype(jnp.int32)
    micros, tok, width = tokens.shape
    top = routes.shape[2]
    local, _, head = w_query.shape
    experts = local * groups
    every = experts * head
    size = local * head
    hidden_units = w_up.shape[1]
    group_bits, batch_bits = log2(groups), log2(batch)
    chips = groups * batch // 2
    chunk = hidden_units // chips
    tile, block = min(256, tok), min(256, tok)
    tiles = tok // tile
    span = top * tile
    pad = -(-experts // 16) * 16
    both = 2 * head
    total = micros * tok
    core = me & 1

    x_bits = [("expert", bit) for bit in range(1, group_bits)]
    b_bits = [("batch", bit) for bit in range(batch_bits)]
    orders = (x_bits + b_bits, b_bits[:2] + x_bits + b_bits[2:])
    hops = list(zip(*orders))

    def place_of(order, expert, row):
        out = jnp.int32(0)
        for i, (axis, bit) in enumerate(order):
            index = expert if axis == "expert" else row
            out = out | (((index >> bit) & 1) << (len(order) - 1 - i))
        return out

    def by_core(first, second):
        return jnp.where(core == 0, first, second)

    high = group_bits - 1
    offsets = jnp.arange(groups, dtype=jnp.int32)
    away = offsets ^ me
    slots = (away >> 1) | ((away & 1) << high)
    devices = (((offsets << 1) & (groups - 1)) | (offsets >> high)) ^ me
    places = [place_of(order, me, mine) for order in orders]
    place_own, place_other = by_core(places[0], places[1]), by_core(places[1], places[0])
    meta = jnp.concatenate(
        [jnp.stack([me, core, place_own, place_other]), slots, devices, lengths.reshape(-1)]
    )
    rows_w = -(-2 * size // (16 * batch)) * 16
    subs = jnp.arange(2 * size // rows_w, dtype=jnp.int32)
    tables = [
        place_of(order, devices[:, None], subs[None, :]) ^ place_of(order, me, mine)
        for order in orders
    ]
    table = jnp.where(
        (offsets < groups // 2)[:, None],
        by_core(tables[0], tables[1]),
        by_core(tables[1], tables[0]),
    )
    final_table = place_of(b_bits, me, subs) ^ place_of(b_bits, me, mine)

    def gather_far(values):
        pieces = [values]
        for axis, bit in x_bits:
            pieces = pieces + [flip(p, axis, bit) for p in pieces]
        return pieces

    def gather_near(pieces):
        return pieces + [flip(p, "expert", 0) for p in pieces]

    def gather(values):
        return gather_near(gather_far(values))

    vmem = pl.BlockSpec(memory_space=pltpu.VMEM)
    smem = pl.BlockSpec(memory_space=pltpu.SMEM)

    def call(kernel, scalars, arrays, outs, scratch=(), limit=16, cost=1, far=(), sems=0):
        marks = [pltpu.SemaphoreType.DMA((sems,))] if sems else []
        far_spec = pl.BlockSpec(memory_space=pltpu.HBM)
        return pl.pallas_call(
            kernel,
            in_specs=[smem] * len(scalars) + [far_spec if i in far else vmem for i in range(len(arrays))],
            out_specs=[vmem] * len(outs),
            out_shape=[jax.ShapeDtypeStruct(*o) for o in outs],
            scratch_shapes=[pltpu.VMEM(*s) for s in scratch] + marks,
            compiler_params=pltpu.CompilerParams(vmem_limit_bytes=limit * MIB),
            cost_estimate=pl.CostEstimate(flops=int(cost * 1.1e9), bytes_accessed=0, transcendentals=0),
        )(
            *scalars,
            *[pltpu.with_memory_space_constraint(x, pltpu.HBM) if i in far else x for i, x in enumerate(arrays)],
        )

    wq = gather(w_query.transpose(0, 2, 1).reshape(size, width))
    router_t = router.T
    routes_t = routes.transpose(2, 0, 1)
    results = call(
        functools.partial(first_kernel, micros),
        [],
        [tokens, key_value, router_t, routes_t, gain_one, shift_one],
        [((tok, width), b16)] * micros + [((tok, both), b16)] * micros + [((8, tok), f32)] * micros,
        [
            ((micros, tok, width), b16), ((width, both), b16), ((experts, width), b16),
            ((top, micros, tok), jnp.int32), ((width,), b16), ((width,), b16),
        ],
        cost=2.4,
        far=range(6),
        sems=6,
    )
    normed, gates = list(results[:micros]), results[2 * micros :]
    kv_pieces = [gather_far(kv) for kv in results[micros : 2 * micros]]
    wo = gather(w_out.reshape(size, width))

    dims = (groups, tok, head, tile, block, top, local, lengths.shape[2])
    keys, keys_t, qt, ot, lse, mixt = [], [], [], [], [], []
    keys_all = groups * tok
    work = 2 * tok * top * keys_all * both
    for m in range(micros):
        if m > 0:
            kv_pieces[m] = after(kv_pieces[m], lse[m - 1])
        results = call(
            functools.partial(forward_kernel, dims, m),
            [meta],
            [normed[m], routes_t, gates[m]] + gather_near(kv_pieces[m]) + wq,
            [
                ((keys_all, both), b16), ((both, keys_all), b16), ((tiles, head, span), b16),
                ((tiles, head, span), f32), ((tiles, 1, span), f32), ((every, tok), b16),
            ],
            [((head, span), f32), ((groups, size, width), b16), ((top, micros, tok), jnp.int32)],
            cost=5,
            far=(1, *range(3, 3 + 2 * groups)),
            sems=2 * groups + 1,
        )
        for target, value in zip((keys, keys_t, qt, ot, lse, mixt), results):
            target.append(value)

    f_tile = 512
    ffn_own, ffn_sent, up_row, hidden, acc, grad_acc = call(
        functools.partial(ffn_kernel, (chunk, f_tile, min(512, tok), micros, groups)),
        [meta],
        [
            tokens, cotangent.reshape(total, width), gain_two, shift_two, down_bias, w_up,
            up_bias.reshape(1, -1), w_down,
        ]
        + mixt + wo,
        [
            ((hidden_units, width), b16), ((hidden_units, width), b16), ((1, hidden_units), f32),
            ((total, width), f32), ((total, width), f32), ((total, width), f32),
        ],
        [
            ((total, width), b16), ((total, f_tile), b16), ((total, f_tile), b16),
        ],
        limit=26,
        cost=11,
    )

    block_out, gh, ffn_rows = call(
        functools.partial(second_norm_kernel, min(512, tok)),
        [],
        [cotangent.reshape(total, width), gain_two, down_bias, hidden, acc, grad_acc],
        [((total, width), b16), ((total, width), f32), ((8, width), f32)],
        cost=1.5,
    )

    part, gq, chosen, kept, arrived, tokens_back = [], [], [], [], [], []
    for m in range(micros):
        p, keep, sent, g, c, token = call(
            functools.partial(backward_kernel, dims, m),
            [meta],
            [gh, routes_t, gates[m], keys[m], keys_t[m], qt[m], ot[m], lse[m], router_t] + wq + wo,
            [
                ((tok, width), f32), ((groups // 2, tok, both), b16),
                ((groups // 2, tok, both), b16), ((every, tok), b16), ((pad, tok), b16), ((8, 128), f32),
            ],
            [((keys_all, both), f32), ((head, span), f32)],
            cost=9,
        )
        part.append(p)
        gq.append(g)
        chosen.append(c)
        tokens_back.append(token)
        count = groups // 2
        got = flip(sent, "expert", 0)
        for way in x_bits[::-1]:
            count //= 2
            moving = add(keep[count:], got[count:])
            keep = add(keep[:count], got[:count])
            got = flip(moving, *way)
        kept.append(keep)
        arrived.append(got)
    def halve(keep, got, ways):
        count = keep.shape[0] // 2
        moving = hop(add(keep[count:], got[count:]), ways, groups, batch)
        return add(keep[:count], got[:count]), moving

    marks = []
    keep, got = ffn_own, flip(ffn_sent, "expert", 0)
    for i, ways in enumerate(hops):
        if 0 < i <= 2 and i <= micros:
            keep, gq[i - 1] = lax.optimization_barrier((keep, gq[i - 1]))
        keep, got = halve(keep, got, ways)
        marks.append(got)
    whole = add(keep, got)

    w_own, w_sent = call(
        functools.partial(weights_kernel, (groups, size, tok, micros), rows_w),
        [table],
        [marks[1], gh] + gq + normed + mixt,
        [((chips * rows_w, width), b16), ((chips * rows_w, width), b16)],
        cost=1.5,
        far=(0,),
    )
    rows_all = both + pad + 16
    half = -(-rows_all // 32) * 16
    input_grad, b_own, b_sent = call(
        functools.partial(last_kernel, micros),
        [meta],
        [marks[3], tokens, gh, gain_one, key_value, up_row, ffn_rows] + normed + part + kept + arrived + chosen,
        [((micros, tok, width), f32), ((half, width), b16), ((half, width), b16)],
        [((2 * half, width), b16)],
        cost=3.8,
        far=(0,),
    )

    o_tile = 256
    o_count = hidden_units // o_tile // 2
    top_bit = log2(chips) - 1

    def ordered(side, own, got, filled):
        def block(which):
            def index(j, meta):
                place = jnp.where(meta[1] == which, meta[2], meta[3])
                return j + ((place >> top_bit) ^ side) * o_count

            return index

        down_at, up_at = block(0), block(1)
        near = pl.BlockSpec(own.shape, lambda j, meta: (0, 0))
        return pl.pallas_call(
            functools.partial(order_kernel, chunk, top_bit, side),
            grid_spec=pltpu.PrefetchScalarGridSpec(
                num_scalar_prefetch=1,
                grid=(o_count,),
                in_specs=[near, near] + [pl.BlockSpec(memory_space=pl.ANY)] * len(filled),
                out_specs=[
                    pl.BlockSpec((o_tile, width), lambda j, meta: (down_at(j, meta), 0)),
                    pl.BlockSpec((width, o_tile), lambda j, meta: (0, up_at(j, meta))),
                ],
            ),
            out_shape=[
                jax.ShapeDtypeStruct((hidden_units, width), f32),
                jax.ShapeDtypeStruct((width, hidden_units), f32),
            ],
            input_output_aliases={3 + i: i for i in range(len(filled))},
            compiler_params=pltpu.CompilerParams(vmem_limit_bytes=16 * MIB),
            cost_estimate=pl.CostEstimate(flops=0, bytes_accessed=hidden_units * width * 6, transcendentals=0),
        )(meta, own, got, *filled)

    keep, got = w_own, flip(w_sent, "expert", 0)
    bundle = None
    for up, (ways, back) in enumerate(zip(hops, hops[::-1])):
        count = keep.shape[0] // 2
        moving = add(keep[count:], got[count:])
        keep = add(keep[:count], got[:count])
        if up == 1:
            bundle = add(b_own, flip(b_sent, "expert", 0))
        if up > 0:
            moving = jnp.concatenate([moving, bundle], axis=0)
        arrived_rows = hop(whole, back, groups, batch)
        moving = hop(moving, ways, groups, batch)
        if up < len(hops) - 1:
            whole = jnp.concatenate([whole, arrived_rows], axis=0)
        if up == len(hops) - 1:
            arrived_rows, moving = lax.optimization_barrier((arrived_rows, moving))
        got = moving[:count]
        if up > 0:
            bundle = add(bundle, moving[count:])
    bundle = add(bundle, hop(bundle, hops[0], groups, batch))
    own_low, own_high = whole, arrived_rows
    got_low, got_high = flip(own_low, "expert", 0), flip(own_high, "expert", 0)
    weights = add(keep, got)
    ways_up = b_bits[::-1]
    for i, way in enumerate(ways_up):
        came = flip(weights, *way)
        if i == len(ways_up) - 3:
            filled = ordered(0, own_low, got_low, ())
            came, *filled = lax.optimization_barrier((came, *filled))
        if i == len(ways_up) - 1:
            filled = ordered(1, own_high, got_high, filled)
            came, *filled = lax.optimization_barrier((came, *filled))
        weights = jnp.concatenate([weights, came], axis=0)
    grad_down, grad_up = filled

    wq_grad, wo_grad, grad_key_value, grad_router, grad_up_bias, *rows = call(
        functools.partial(small_kernel, (both, pad, rows_w)),
        [meta, final_table],
        [weights, bundle, flip(bundle, "expert", 0)],
        [
            ((size, width), f32), ((size, width), f32), ((width, both), f32),
            ((experts, width), f32), ((hidden_units,), f32),
        ] + [((width,), f32)] * 5,
        [((2 * half, width), b16)],
    )
    grad_down_bias, grad_gain_two, grad_shift_two, grad_gain_one, grad_shift_one = rows


    return (
        block_out.reshape(micros, tok, width),
        input_grad,
        grad_gain_one,
        grad_shift_one,
        grad_router.T,
        grad_key_value,
        wq_grad.reshape(local, head, width).transpose(0, 2, 1),
        wo_grad.reshape(local, head, width),
        grad_gain_two,
        grad_shift_two,
        grad_up,
        grad_up_bias,
        grad_down,
        grad_down_bias,
    )


def solution(mesh):
    split = P(None, ("batch", "expert"), None)
    own = P("expert", None, None)
    in_specs = (
        split, split, P(None, "batch", None), P(), P(), P(), P(), own, own, P(), P(), P(), P(), P(),
        P(), split,
    )
    out_specs = (split, split, P(), P(), P(), P(), own, own, P(), P(), P(), P(), P(), P())
    return jax.shard_map(shards, mesh=mesh, in_specs=in_specs, out_specs=out_specs, check_vma=False)
```

```python
import functools

import jax
import jax.numpy as jnp
from jax import lax
from jax.experimental import pallas as pl
from jax.experimental.pallas import tpu as pltpu
from jax.sharding import PartitionSpec as P

epsilon = 1e-05
b16 = jnp.bfloat16
f32 = jnp.float32
LOW = -1e30
MIB = 1024 * 1024


def dot(left, right, over=((1,), (0,))):
    return lax.dot_general(left, right, (over, ((), ())), preferred_element_type=f32)


def log2(size):
    return size.bit_length() - 1


def flip(values, axis, bit):
    size = lax.axis_size(axis)
    return lax.ppermute(values, axis, [(i, i ^ (1 << bit)) for i in range(size)])


def hop(values, ways, groups, batch):
    pairs = []
    for b in range(batch):
        for e in range(groups):
            axis, bit = ways[e & 1]
            to_b, to_e = (b, e ^ (1 << bit)) if axis == "expert" else (b ^ (1 << bit), e)
            pairs.append((b * groups + e, to_b * groups + to_e))
    return lax.ppermute(values, ("batch", "expert"), pairs)


def after(values, token):
    return lax.optimization_barrier((values, token))[0]


def add(left, right):
    return (left.astype(f32) + right.astype(f32)).astype(b16)


def normalize(values):
    centred = values - jnp.mean(values, axis=-1, keepdims=True)
    spread = lax.rsqrt(jnp.mean(centred * centred, axis=-1, keepdims=True) + epsilon)
    return centred * spread, spread


def norm_back(grad, unit, spread):
    inner = jnp.mean(grad * unit, axis=-1, keepdims=True)
    return spread * (grad - jnp.mean(grad, axis=-1, keepdims=True) - unit * inner)


def load(pairs, sems):
    copies = [pltpu.make_async_copy(a, b, sems.at[i]) for i, (a, b) in enumerate(pairs)]
    for copy in copies:
        copy.start()
    for copy in copies:
        copy.wait()


def row(vector):
    return vector[...].astype(f32).reshape(1, -1)


def first_kernel(micros, *refs):
    far = refs[:6]
    normed = refs[6 : 6 + micros]
    kv = refs[6 + micros : 6 + 2 * micros]
    gates = refs[6 + 2 * micros : 6 + 3 * micros]
    near = refs[6 + 3 * micros : -1]
    load(list(zip(far, near)), refs[-1])
    tokens, key_value, router, routes, gain, shift = near
    top = routes.shape[0]
    for m in range(micros):
        unit, _ = normalize(tokens[m].astype(f32))
        rows = (unit * row(gain) + row(shift)).astype(b16)
        normed[m][...] = rows
        kv[m][...] = dot(rows, key_value[...]).astype(b16)
        logits = dot(router[...], rows, ((1,), (1,)))
        ids = lax.broadcasted_iota(jnp.int32, logits.shape, 0)
        chosen = [
            jnp.sum(jnp.where(ids == routes[k, m : m + 1, :], logits, 0.0), axis=0, keepdims=True)
            for k in range(top)
        ]
        peak = functools.reduce(jnp.maximum, chosen)
        powers = [jnp.exp(c - peak) for c in chosen]
        total = sum(powers)
        for k in range(top):
            gates[m][k : k + 1, :] = powers[k] / total


def bounds(lens, first, count):
    place = first + lax.broadcasted_iota(jnp.int32, (1, count), 1)
    run = jnp.int32(0)
    low = jnp.int32(0)
    high = jnp.int32(0)
    start = jnp.zeros((1, count), jnp.int32)
    for length in lens:
        run = run + length
        start = jnp.where(place >= run, run, start)
        low = jnp.where(first >= run, run, low)
        high = jnp.where(first + count - 1 >= run, run, high)
    return place, start, low, high


def key_loops(body, carry, first, tile, low, high, block):
    begin = low // block
    full_end = first // block
    full_begin = jnp.minimum((high + block - 1) // block, full_end)
    end = (first + tile - 1) // block + 1
    carry = lax.fori_loop(begin, full_begin, functools.partial(body, True), carry)
    carry = lax.fori_loop(full_begin, full_end, functools.partial(body, False), carry)
    return lax.fori_loop(full_end, end, functools.partial(body, True), carry)


def spread_rows(pieces, ids, expert):
    out = jnp.zeros_like(pieces[0])
    for piece, row in zip(pieces, ids):
        out = jnp.where(row == expert, piece, out)
    return out


def gather_rows(table, ids, experts, head):
    out = jnp.zeros((head, table[0].shape[1]), f32)
    for piece, expert in zip(table, experts):
        out = jnp.where(ids == expert, piece, out)
    return out


def expert_ids(meta, groups, local):
    base = 4 + groups
    return [meta[base + s] * local + l for s in range(groups) for l in range(local)]


def head_table(weights, rows, local, head):
    out = []
    for piece in weights:
        whole = dot(piece[...], rows, ((1,), (1,)))
        out += [whole[l * head : (l + 1) * head] for l in range(local)]
    return out


def masked(scores, key_base, place, start):
    keys = key_base + lax.broadcasted_iota(jnp.int32, scores.shape, 0)
    return jnp.where((keys <= place) & (keys >= start), scores, LOW)


def forward_kernel(dims, micro, *refs):
    groups, tok, head, tile, block, top, local, pieces_all = dims
    meta, normed, routes, gates = refs[:4]
    pieces_kv = refs[4 : 4 + groups]
    weights = refs[4 + groups : 4 + 2 * groups]
    kv, kvt, qt, ot, lse, mixt, acc, held, routes_near, sems = refs[4 + 2 * groups :]
    me = meta[0]
    experts = expert_ids(meta, groups, local)
    pairs = [(piece, kv.at[pl.ds(s * tok, tok), :]) for s, piece in enumerate(pieces_kv)]
    pairs += [(piece, held.at[s]) for s, piece in enumerate(weights)]
    load(pairs + [(routes, routes_near)], sems)
    routes = routes_near
    lens = [meta[4 + 2 * groups + micro * pieces_all + j] for j in range(pieces_all)]
    for s in range(groups):
        kvt[:, s * tok : (s + 1) * tok] = kv[s * tok : (s + 1) * tok, :].T
    table = head_table([held.at[s] for s in range(groups)], normed[...], local, head)
    for i in range(tok // tile):
        cols = slice(i * tile, (i + 1) * tile)
        ids = [routes[k, micro : micro + 1, cols] for k in range(top)]
        part = [t[:, cols] for t in table]
        heads = [gather_rows(part, row, experts, head) for row in ids]
        query = jnp.concatenate(heads, axis=1).astype(b16) * jnp.asarray(0.125, b16)
        qt[i] = query
        padded = jnp.concatenate([query, jnp.zeros_like(query)], axis=0)
        first = me * tok + i * tile
        place, start, low, high = bounds(lens, first, tile)
        place = jnp.concatenate([place] * top, axis=1)
        start = jnp.concatenate([start] * top, axis=1)
        acc[...] = jnp.zeros_like(acc)

        def one_block(edge, index, carry):
            peak, total = carry
            chunk = (index * block) // tok
            row = index * block - chunk * tok
            at = pl.multiple_of(meta[4 + chunk] * tok + row, block)
            scores = dot(kv[pl.ds(at, block), :], padded)
            if edge:
                scores = masked(scores, index * block, place, start)
            new_peak = jnp.maximum(peak, jnp.max(scores, axis=0, keepdims=True))
            scale = jnp.exp(peak - new_peak)
            powers = jnp.exp(scores - new_peak)
            total = total * scale + jnp.sum(powers, axis=0, keepdims=True)
            acc[...] = acc[...] * scale + dot(kvt[head:, pl.ds(at, block)], powers.astype(b16))
            return new_peak, total

        width = top * tile
        none = (jnp.full((1, width), LOW, f32), jnp.zeros((1, width), f32))
        peak, total = key_loops(one_block, none, first, tile, low, high, block)
        out = acc[...] / total
        ot[i] = out
        lse[i] = peak + jnp.log(total)
        rounded = out.astype(b16).astype(f32)
        pieces = [
            rounded[:, k * tile : (k + 1) * tile] * gates[k : k + 1, cols] for k in range(top)
        ]
        for e, expert in enumerate(experts):
            mixt[e * head : (e + 1) * head, cols] = spread_rows(pieces, ids, expert).astype(b16)


def backward_kernel(dims, micro, *refs):
    groups, tok, head, tile, block, top, local, pieces_all = dims
    meta, gh, routes, gates, kv, kvt, qt, ot, lse, router = refs[:10]
    wq = refs[10 : 10 + groups]
    wo = refs[10 + groups : 10 + 2 * groups]
    part, keep, sent, gq, chosen_rows, token, dkv, dq = refs[10 + 2 * groups :]
    token[...] = jnp.zeros_like(token)
    lens = [meta[4 + 2 * groups + micro * pieces_all + j] for j in range(pieces_all)]
    me = meta[0]
    experts = expert_ids(meta, groups, local)
    every = len(experts) * head
    pad = chosen_rows.shape[0]
    dkv[...] = jnp.zeros_like(dkv)
    table = head_table(wo, gh[micro * tok : (micro + 1) * tok, :].astype(b16), local, head)
    for i in range(tok // tile):
        cols = slice(i * tile, (i + 1) * tile)
        ids = [routes[k, micro : micro + 1, cols] for k in range(top)]
        cut = [t[:, cols] for t in table]
        back = [gather_rows(cut, row, experts, head) for row in ids]
        weights = [gates[k : k + 1, cols] for k in range(top)]
        out = ot[i]
        outs = [out[:, k * tile : (k + 1) * tile] for k in range(top)]
        grad_gates = [
            jnp.sum(b * o.astype(b16).astype(f32), axis=0, keepdims=True)
            for b, o in zip(back, outs)
        ]
        inner = sum(w * g for w, g in zip(weights, grad_gates))
        chosen = [w * (g - inner) for w, g in zip(weights, grad_gates)]
        names = lax.broadcasted_iota(jnp.int32, (pad, tile), 0)
        chosen_rows[:, cols] = spread_rows(
            [jnp.broadcast_to(c, (pad, tile)) for c in chosen], ids, names
        ).astype(b16)
        grad = jnp.concatenate([w * b for w, b in zip(weights, back)], axis=1).astype(b16)
        delta = jnp.sum(grad.astype(f32) * out, axis=0, keepdims=True)
        query = qt[i]
        padded = jnp.concatenate([query, jnp.zeros_like(query)], axis=0)
        grad_pad = jnp.concatenate([jnp.zeros_like(grad), grad], axis=0)
        level = lse[i]
        first = me * tok + i * tile
        place, start, low, high = bounds(lens, first, tile)
        place = jnp.concatenate([place] * top, axis=1)
        start = jnp.concatenate([start] * top, axis=1)
        dq[...] = jnp.zeros_like(dq)

        def one_block(edge, index, carry):
            chunk = (index * block) // tok
            row = index * block - chunk * tok
            at = pl.multiple_of(meta[4 + chunk] * tok + row, block)
            keys = kv[pl.ds(at, block), :]
            scores = dot(keys, padded)
            if edge:
                scores = masked(scores, index * block, place, start)
            soft = jnp.exp(scores - level)
            grad_scores = (soft * (dot(keys, grad_pad) - delta)).astype(b16)
            dkv[pl.ds(at, block), :] += dot(grad_scores, padded, ((1,), (1,))) + dot(
                soft.astype(b16), grad_pad, ((1,), (1,))
            )
            dq[...] += dot(kvt[:head, pl.ds(at, block)], grad_scores)
            return carry

        key_loops(one_block, 0, first, tile, low, high, block)
        grad_query = dq[...] * 0.125
        pieces = [grad_query[:, k * tile : (k + 1) * tile] for k in range(top)]
        for e, expert in enumerate(experts):
            gq[e * head : (e + 1) * head, cols] = spread_rows(pieces, ids, expert).astype(b16)
    half = groups // 2
    for s in range(half):
        keep[s] = dkv[s * tok : (s + 1) * tok, :].astype(b16)
        sent[s] = dkv[(half + s) * tok : (half + s + 1) * tok, :].astype(b16)
    size = local * head
    total = dot(chosen_rows[: router.shape[0], :], router[...], ((0,), (0,)))
    for s in range(groups):
        total = total + dot(gq[s * size : (s + 1) * size, :], wq[s][...], ((0,), (0,)))
    part[...] = total


def weights_kernel(dims, rows, *refs):
    groups, size, tok, micros = dims
    table, _, gh = refs[:3]
    gq = refs[3 : 3 + micros]
    normed = refs[3 + micros : 3 + 2 * micros]
    mixt = refs[3 + 2 * micros : 3 + 3 * micros]
    own, sent = refs[3 + 3 * micros :]
    grads = [gh[m * tok : (m + 1) * tok, :].astype(b16) for m in range(micros)]
    for s in range(groups):
        at = slice(s * size, (s + 1) * size)
        wq = sum(dot(g[at, :], n[...]) for g, n in zip(gq, normed)).astype(b16)
        wo = sum(dot(m[at, :], g) for m, g in zip(mixt, grads)).astype(b16)
        target = own if s < groups // 2 else sent
        for k in range(2 * size // rows):
            to = pl.multiple_of(table[s, k] * rows, 16)
            source = wq if k * rows < size else wo
            begin = k * rows % size
            target[pl.ds(to, rows), :] = source[begin : begin + rows, :]


def ffn_kernel(dims, *refs):
    chunk, tile, sub, micros, groups = dims
    meta, tokens, cotan, gain, shift, down_bias, w_up, up_bias, w_down = refs[:9]
    mixt = refs[9 : 9 + micros]
    wo = refs[9 + micros : 9 + micros + groups]
    own, sent, up_row, hidden, acc, grad_acc = refs[9 + micros + groups : 15 + micros + groups]
    second, act_s, gu_s = refs[15 + micros + groups :]
    total, width = hidden.shape
    tok = tokens.shape[1]
    size = wo[0].shape[0]
    for m in range(micros):
        at = slice(m * tok, (m + 1) * tok)
        mixed = dot(mixt[m][:size, :], wo[0][...], ((0,), (0,)))
        for s in range(1, groups):
            mixed = mixed + dot(mixt[m][s * size : (s + 1) * size, :], wo[s][...], ((0,), (0,)))
        values = tokens[m].astype(f32) + mixed
        hidden[at, :] = values
        unit, _ = normalize(values)
        second[at, :] = (unit * row(gain) + row(shift)).astype(b16)
    acc[...] = jnp.zeros_like(acc)
    grad_acc[...] = jnp.zeros_like(grad_acc)
    c0 = 0.7978845608028654
    c1 = c0 * 0.044715
    per = tile // chunk

    def one_tile(step, carry):
        base = pl.multiple_of(step * tile, tile)
        span = pl.ds(base, tile)
        bias = up_bias[:, span].astype(f32)
        up_sum = jnp.zeros((1, tile), f32)
        for i in range(total // sub):
            at = slice(i * sub, (i + 1) * sub)
            upward = dot(second[at, :], w_up[:, span]) + bias
            grad = dot(cotan[at, :], w_down[span, :], ((1,), (1,)))
            square = upward * upward
            curve = jnp.tanh(upward * (c0 + c1 * square))
            lift = 0.5 + 0.5 * curve
            value = upward * lift
            slope = lift + value * (1.0 - curve) * (c0 + (3.0 * c1) * square)
            active = value.astype(b16)
            grad_up = (grad * slope).astype(b16)
            act_s[at, :] = active
            gu_s[at, :] = grad_up
            up_sum = up_sum + jnp.sum(grad_up.astype(f32), axis=0, keepdims=True)
            acc[at, :] += dot(active, w_down[span, :])
            grad_acc[at, :] += dot(grad_up, w_up[:, span], ((1,), (1,)))
        up_row[:, span] = up_sum
        grad_down = dot(act_s[...], cotan[...], ((0,), (0,))).astype(b16)
        grad_up_t = dot(gu_s[...], second[...], ((0,), (0,))).astype(b16)

        def place(values, target, low):
            for i in range(per):
                at = pl.multiple_of(((step * per + i) ^ low) * chunk, chunk)
                target[pl.ds(at, chunk), :] = values[i * chunk : (i + 1) * chunk, :]

        @pl.when(meta[1] == 0)
        def _():
            place(grad_down, own, meta[2])
            place(grad_up_t, sent, meta[3])

        @pl.when(meta[1] != 0)
        def _():
            place(grad_up_t, own, meta[2])
            place(grad_down, sent, meta[3])

        return carry

    lax.fori_loop(0, w_up.shape[1] // tile, one_tile, 0)


def second_norm_kernel(sub, cotan, gain, down_bias, hidden, acc, grad_acc, block_out, gh, rows):
    total, width = hidden.shape
    sums = [jnp.zeros((1, width), f32) for _ in range(3)]
    for i in range(total // sub):
        at = slice(i * sub, (i + 1) * sub)
        rows_now = hidden[at, :]
        cot = cotan[at, :].astype(f32)
        block_out[at, :] = (rows_now + acc[at, :] + row(down_bias)).astype(b16)
        unit, spread = normalize(rows_now)
        grad = grad_acc[at, :]
        gh[at, :] = cot + norm_back(grad * row(gain), unit, spread)
        for j, piece in enumerate((cot, grad * unit, grad)):
            sums[j] = sums[j] + jnp.sum(piece, axis=0, keepdims=True)
    rows[...] = jnp.zeros_like(rows)
    for j in range(3):
        rows[j : j + 1, :] = sums[j]


def last_kernel(micros, *refs):
    meta, _, tokens, gh, gain, key_value, up_row, rows = refs[:8]
    normed = refs[8 : 8 + micros]
    part = refs[8 + micros : 8 + 2 * micros]
    kept = refs[8 + 2 * micros : 8 + 3 * micros]
    got = refs[8 + 3 * micros : 8 + 4 * micros]
    chosen = refs[8 + 4 * micros : 8 + 5 * micros]
    input_grad, own, sent, bundle = refs[8 + 5 * micros :]
    _, tok, width = tokens.shape
    key_rows = 0.0
    gain_sum = jnp.zeros((1, width), f32)
    shift_sum = jnp.zeros((1, width), f32)
    for m in range(micros):
        at = slice(m * tok, (m + 1) * tok)
        grad_kv = (kept[m][0].astype(f32) + got[m][0].astype(f32)).astype(b16)
        key_rows = key_rows + dot(grad_kv, normed[m][...], ((0,), (0,)))
        grad = part[m][...] + dot(grad_kv, key_value[...], ((1,), (1,)))
        unit, spread = normalize(tokens[m].astype(f32))
        input_grad[m] = gh[at, :] + norm_back(grad * row(gain), unit, spread)
        gain_sum = gain_sum + jnp.sum(grad * unit, axis=0, keepdims=True)
        shift_sum = shift_sum + jnp.sum(grad, axis=0, keepdims=True)
    at = key_rows.shape[0]
    pad = chosen[0].shape[0]
    bundle[:at, :] = key_rows.astype(b16)
    router_rows = sum(dot(c[...], n[...]) for c, n in zip(chosen, normed))
    bundle[at : at + pad, :] = router_rows.astype(b16)
    count = up_row.shape[1] // width
    pieces = [up_row[:, i * width : (i + 1) * width] for i in range(count)]
    pieces += [rows[0:3, :], gain_sum, shift_sum]
    left = bundle.shape[0] - at - pad - count - 5
    pieces.append(jnp.zeros((left, width), f32))
    bundle[at + pad :, :] = jnp.concatenate(pieces, axis=0).astype(b16)
    half = own.shape[0]
    own[...] = bundle[pl.ds(pl.multiple_of(meta[1] * half, 16), half), :]
    sent[...] = bundle[pl.ds(pl.multiple_of((1 - meta[1]) * half, 16), half), :]


def order_kernel(chunk, top, side, meta, own, got, *refs):
    down, up = refs[-2:]
    tile = down.shape[0]
    per = tile // chunk
    half = own.shape[0] // chunk

    def sorted_rows(ref, place):
        first = (pl.program_id(0) * per) ^ (place & (half - 1))
        blocks = []
        for i in range(per):
            at = pl.multiple_of((first ^ i) * chunk, chunk)
            blocks.append(ref[pl.ds(at, chunk), :].astype(f32))
        return blocks[0] if per == 1 else jnp.concatenate(blocks, axis=0)

    own_rows = sorted_rows(own, meta[2])
    got_rows = sorted_rows(got, meta[3])

    @pl.when(meta[1] == 0)
    def _():
        down[...] = own_rows
        up[...] = got_rows.T

    @pl.when(meta[1] != 0)
    def _():
        down[...] = got_rows
        up[...] = own_rows.T


def small_kernel(dims, meta, table, weights, own, got, wq, wo, keys, router, up_row, *outs):
    both, pad, rows = dims
    bundle = outs[-1]
    half, width = own.shape
    bundle[pl.ds(pl.multiple_of(meta[1] * half, 16), half), :] = own[...]
    bundle[pl.ds(pl.multiple_of((1 - meta[1]) * half, 16), half), :] = got[...]
    keys[...] = bundle[:both, :].astype(f32).T
    values = bundle[both:, :].astype(f32)
    router[...] = values[: router.shape[0], :]
    count = up_row.shape[0] // width
    for i in range(count):
        up_row[i * width : (i + 1) * width] = values[pad + i]
    for i, out in enumerate(outs[:-1]):
        out[...] = values[pad + count + i]
    size = wq.shape[0]
    for k in range(2 * size // rows):
        at = pl.multiple_of(table[k] * rows, 16)
        target = wq if k * rows < size else wo
        begin = k * rows % size
        target[begin : begin + rows, :] = weights[pl.ds(at, rows), :].astype(f32)


def shards(
    tokens, routes, lengths, gain_one, shift_one, router, key_value, w_query, w_out,
    gain_two, shift_two, w_up, up_bias, w_down, down_bias, cotangent,
):
    groups = lax.axis_size("expert")
    batch = lax.axis_size("batch")
    me = lax.axis_index("expert").astype(jnp.int32)
    mine = lax.axis_index("batch").astype(jnp.int32)
    micros, tok, width = tokens.shape
    top = routes.shape[2]
    local, _, head = w_query.shape
    experts = local * groups
    every = experts * head
    size = local * head
    hidden_units = w_up.shape[1]
    group_bits, batch_bits = log2(groups), log2(batch)
    chips = groups * batch // 2
    chunk = hidden_units // chips
    tile, block = min(256, tok), min(256, tok)
    tiles = tok // tile
    span = top * tile
    pad = -(-experts // 16) * 16
    both = 2 * head
    total = micros * tok
    core = me & 1

    x_bits = [("expert", bit) for bit in range(1, group_bits)]
    b_bits = [("batch", bit) for bit in range(batch_bits)]
    orders = (x_bits + b_bits, b_bits[:2] + x_bits + b_bits[2:])
    hops = list(zip(*orders))

    def place_of(order, expert, row):
        out = jnp.int32(0)
        for i, (axis, bit) in enumerate(order):
            index = expert if axis == "expert" else row
            out = out | (((index >> bit) & 1) << (len(order) - 1 - i))
        return out

    def by_core(first, second):
        return jnp.where(core == 0, first, second)

    high = group_bits - 1
    offsets = jnp.arange(groups, dtype=jnp.int32)
    away = offsets ^ me
    slots = (away >> 1) | ((away & 1) << high)
    devices = (((offsets << 1) & (groups - 1)) | (offsets >> high)) ^ me
    places = [place_of(order, me, mine) for order in orders]
    place_own, place_other = by_core(places[0], places[1]), by_core(places[1], places[0])
    meta = jnp.concatenate(
        [jnp.stack([me, core, place_own, place_other]), slots, devices, lengths.reshape(-1)]
    )
    rows_w = -(-2 * size // (16 * batch)) * 16
    subs = jnp.arange(2 * size // rows_w, dtype=jnp.int32)
    tables = [
        place_of(order, devices[:, None], subs[None, :]) ^ place_of(order, me, mine)
        for order in orders
    ]
    table = jnp.where(
        (offsets < groups // 2)[:, None],
        by_core(tables[0], tables[1]),
        by_core(tables[1], tables[0]),
    )
    final_table = place_of(b_bits, me, subs) ^ place_of(b_bits, me, mine)

    def gather_far(values):
        pieces = [values]
        for axis, bit in x_bits:
            pieces = pieces + [flip(p, axis, bit) for p in pieces]
        return pieces

    def gather_near(pieces):
        return pieces + [flip(p, "expert", 0) for p in pieces]

    def gather(values):
        return gather_near(gather_far(values))

    vmem = pl.BlockSpec(memory_space=pltpu.VMEM)
    smem = pl.BlockSpec(memory_space=pltpu.SMEM)

    def call(kernel, scalars, arrays, outs, scratch=(), limit=16, cost=1, far=(), sems=0):
        marks = [pltpu.SemaphoreType.DMA((sems,))] if sems else []
        far_spec = pl.BlockSpec(memory_space=pltpu.HBM)
        return pl.pallas_call(
            kernel,
            in_specs=[smem] * len(scalars) + [far_spec if i in far else vmem for i in range(len(arrays))],
            out_specs=[vmem] * len(outs),
            out_shape=[jax.ShapeDtypeStruct(*o) for o in outs],
            scratch_shapes=[pltpu.VMEM(*s) for s in scratch] + marks,
            compiler_params=pltpu.CompilerParams(vmem_limit_bytes=limit * MIB),
            cost_estimate=pl.CostEstimate(flops=int(cost * 1.1e9), bytes_accessed=0, transcendentals=0),
        )(
            *scalars,
            *[pltpu.with_memory_space_constraint(x, pltpu.HBM) if i in far else x for i, x in enumerate(arrays)],
        )

    wq = gather(w_query.transpose(0, 2, 1).reshape(size, width))
    router_t = router.T
    routes_t = routes.transpose(2, 0, 1)
    results = call(
        functools.partial(first_kernel, micros),
        [],
        [tokens, key_value, router_t, routes_t, gain_one, shift_one],
        [((tok, width), b16)] * micros + [((tok, both), b16)] * micros + [((8, tok), f32)] * micros,
        [
            ((micros, tok, width), b16), ((width, both), b16), ((experts, width), b16),
            ((top, micros, tok), jnp.int32), ((width,), b16), ((width,), b16),
        ],
        cost=2.4,
        far=range(6),
        sems=6,
    )
    normed, gates = list(results[:micros]), results[2 * micros :]
    kv_pieces = [gather_far(kv) for kv in results[micros : 2 * micros]]
    wo = gather(w_out.reshape(size, width))

    dims = (groups, tok, head, tile, block, top, local, lengths.shape[2])
    keys, keys_t, qt, ot, lse, mixt = [], [], [], [], [], []
    keys_all = groups * tok
    work = 2 * tok * top * keys_all * both
    for m in range(micros):
        if m > 0:
            kv_pieces[m] = after(kv_pieces[m], lse[m - 1])
        results = call(
            functools.partial(forward_kernel, dims[:4] + (min(512, tok),) + dims[5:], m),
            [meta],
            [normed[m], routes_t, gates[m]] + gather_near(kv_pieces[m]) + wq,
            [
                ((keys_all, both), b16), ((both, keys_all), b16), ((tiles, head, span), b16),
                ((tiles, head, span), f32), ((tiles, 1, span), f32), ((every, tok), b16),
            ],
            [((head, span), f32), ((groups, size, width), b16), ((top, micros, tok), jnp.int32)],
            cost=5,
            far=(1, *range(3, 3 + 2 * groups)),
            sems=2 * groups + 1,
        )
        for target, value in zip((keys, keys_t, qt, ot, lse, mixt), results):
            target.append(value)

    f_tile = 512
    ffn_own, ffn_sent, up_row, hidden, acc, grad_acc = call(
        functools.partial(ffn_kernel, (chunk, f_tile, min(512, tok), micros, groups)),
        [meta],
        [
            tokens, cotangent.reshape(total, width), gain_two, shift_two, down_bias, w_up,
            up_bias.reshape(1, -1), w_down,
        ]
        + mixt + wo,
        [
            ((hidden_units, width), b16), ((hidden_units, width), b16), ((1, hidden_units), f32),
            ((total, width), f32), ((total, width), f32), ((total, width), f32),
        ],
        [
            ((total, width), b16), ((total, f_tile), b16), ((total, f_tile), b16),
        ],
        limit=26,
        cost=11,
    )

    block_out, gh, ffn_rows = call(
        functools.partial(second_norm_kernel, min(512, tok)),
        [],
        [cotangent.reshape(total, width), gain_two, down_bias, hidden, acc, grad_acc],
        [((total, width), b16), ((total, width), f32), ((8, width), f32)],
        cost=1.5,
    )

    part, gq, chosen, kept, arrived, tokens_back = [], [], [], [], [], []
    for m in range(micros):
        p, keep, sent, g, c, token = call(
            functools.partial(backward_kernel, dims, m),
            [meta],
            [gh, routes_t, gates[m], keys[m], keys_t[m], qt[m], ot[m], lse[m], router_t] + wq + wo,
            [
                ((tok, width), f32), ((groups // 2, tok, both), b16),
                ((groups // 2, tok, both), b16), ((every, tok), b16), ((pad, tok), b16), ((8, 128), f32),
            ],
            [((keys_all, both), f32), ((head, span), f32)],
            cost=9,
        )
        part.append(p)
        gq.append(g)
        chosen.append(c)
        tokens_back.append(token)
        count = groups // 2
        got = flip(sent, "expert", 0)
        for way in x_bits[::-1]:
            count //= 2
            moving = add(keep[count:], got[count:])
            keep = add(keep[:count], got[:count])
            got = flip(moving, *way)
        kept.append(keep)
        arrived.append(got)
    def halve(keep, got, ways):
        count = keep.shape[0] // 2
        moving = hop(add(keep[count:], got[count:]), ways, groups, batch)
        return add(keep[:count], got[:count]), moving

    marks = []
    keep, got = ffn_own, flip(ffn_sent, "expert", 0)
    for i, ways in enumerate(hops):
        if 0 < i <= 2 and i <= micros:
            keep, gq[i - 1] = lax.optimization_barrier((keep, gq[i - 1]))
        keep, got = halve(keep, got, ways)
        marks.append(got)
    whole = add(keep, got)

    w_own, w_sent = call(
        functools.partial(weights_kernel, (groups, size, tok, micros), rows_w),
        [table],
        [marks[1], gh] + gq + normed + mixt,
        [((chips * rows_w, width), b16), ((chips * rows_w, width), b16)],
        cost=1.5,
        far=(0,),
    )
    rows_all = both + pad + 16
    half = -(-rows_all // 32) * 16
    input_grad, b_own, b_sent = call(
        functools.partial(last_kernel, micros),
        [meta],
        [marks[3], tokens, gh, gain_one, key_value, up_row, ffn_rows] + normed + part + kept + arrived + chosen,
        [((micros, tok, width), f32), ((half, width), b16), ((half, width), b16)],
        [((2 * half, width), b16)],
        cost=3.8,
        far=(0,),
    )

    o_tile = 256
    o_count = hidden_units // o_tile // 2
    top_bit = log2(chips) - 1

    def ordered(side, own, got, filled):
        def block(which):
            def index(j, meta):
                place = jnp.where(meta[1] == which, meta[2], meta[3])
                return j + ((place >> top_bit) ^ side) * o_count

            return index

        down_at, up_at = block(0), block(1)
        near = pl.BlockSpec(own.shape, lambda j, meta: (0, 0))
        return pl.pallas_call(
            functools.partial(order_kernel, chunk, top_bit, side),
            grid_spec=pltpu.PrefetchScalarGridSpec(
                num_scalar_prefetch=1,
                grid=(o_count,),
                in_specs=[near, near] + [pl.BlockSpec(memory_space=pl.ANY)] * len(filled),
                out_specs=[
                    pl.BlockSpec((o_tile, width), lambda j, meta: (down_at(j, meta), 0)),
                    pl.BlockSpec((width, o_tile), lambda j, meta: (0, up_at(j, meta))),
                ],
            ),
            out_shape=[
                jax.ShapeDtypeStruct((hidden_units, width), f32),
                jax.ShapeDtypeStruct((width, hidden_units), f32),
            ],
            input_output_aliases={3 + i: i for i in range(len(filled))},
            compiler_params=pltpu.CompilerParams(vmem_limit_bytes=16 * MIB),
            cost_estimate=pl.CostEstimate(flops=0, bytes_accessed=hidden_units * width * 6, transcendentals=0),
        )(meta, own, got, *filled)

    keep, got = w_own, flip(w_sent, "expert", 0)
    bundle = None
    for up, (ways, back) in enumerate(zip(hops, hops[::-1])):
        count = keep.shape[0] // 2
        moving = add(keep[count:], got[count:])
        keep = add(keep[:count], got[:count])
        if up == 1:
            bundle = add(b_own, flip(b_sent, "expert", 0))
        if 0 < up < len(hops) - 1:
            moving = jnp.concatenate([moving, bundle], axis=0)
        arrived_rows = hop(whole, back, groups, batch)
        moving = hop(moving, ways, groups, batch)
        if up < len(hops) - 1:
            whole = jnp.concatenate([whole, arrived_rows], axis=0)
        if up == len(hops) - 1:
            arrived_rows, moving = lax.optimization_barrier((arrived_rows, moving))
        got = moving[:count]
        if 0 < up < len(hops) - 1:
            bundle = add(bundle, moving[count:])
    for ways in (hops[-1], hops[0]):
        bundle = add(bundle, hop(bundle, ways, groups, batch))
    own_low, own_high = whole, arrived_rows
    got_low, got_high = flip(own_low, "expert", 0), flip(own_high, "expert", 0)
    weights = add(keep, got)
    ways_up = b_bits[::-1]
    for i, way in enumerate(ways_up):
        came = flip(weights, *way)
        if i == len(ways_up) - 3:
            filled = ordered(0, own_low, got_low, ())
            came, *filled = lax.optimization_barrier((came, *filled))
        if i == len(ways_up) - 1:
            filled = ordered(1, own_high, got_high, filled)
            came, *filled = lax.optimization_barrier((came, *filled))
        weights = jnp.concatenate([weights, came], axis=0)
    grad_down, grad_up = filled

    wq_grad, wo_grad, grad_key_value, grad_router, grad_up_bias, *rows = call(
        functools.partial(small_kernel, (both, pad, rows_w)),
        [meta, final_table],
        [weights, bundle, flip(bundle, "expert", 0)],
        [
            ((size, width), f32), ((size, width), f32), ((width, both), f32),
            ((experts, width), f32), ((hidden_units,), f32),
        ] + [((width,), f32)] * 5,
        [((2 * half, width), b16)],
    )
    grad_down_bias, grad_gain_two, grad_shift_two, grad_gain_one, grad_shift_one = rows


    return (
        block_out.reshape(micros, tok, width),
        input_grad,
        grad_gain_one,
        grad_shift_one,
        grad_router.T,
        grad_key_value,
        wq_grad.reshape(local, head, width).transpose(0, 2, 1),
        wo_grad.reshape(local, head, width),
        grad_gain_two,
        grad_shift_two,
        grad_up,
        grad_up_bias,
        grad_down,
        grad_down_bias,
    )


def solution(mesh):
    split = P(None, ("batch", "expert"), None)
    own = P("expert", None, None)
    in_specs = (
        split, split, P(None, "batch", None), P(), P(), P(), P(), own, own, P(), P(), P(), P(), P(),
        P(), split,
    )
    out_specs = (split, split, P(), P(), P(), P(), own, own, P(), P(), P(), P(), P(), P())
    return jax.shard_map(shards, mesh=mesh, in_specs=in_specs, out_specs=out_specs, check_vma=False)
```
